32 devices in a mesh: dp: 4 (over x, core), fsdp: 4 (over z), sp: 2 (over y).
Axes of the slice: x: 2, y: 2, z: 4, core: 2. Of those that a mesh axis runs over, the one named last changes fastest.
Arguments:
- tokens: bfloat16 [12288, 1024], P(('dp', 'fsdp', 'sp')), may hold values from -6 to 6
- cotangent: bfloat16 [12288, 1024], P(('dp', 'fsdp', 'sp')), may hold values from -6 to 6
- doc_lengths: int32 [16, 4], P(('dp', 'fsdp')), may hold values from 1 to 576, 768 in all within a row
- input_weight: bfloat16 [1024, 6144], P('fsdp'), may hold values from -0.1875 to 0.1875
- rate_weight: bfloat16 [1024, 16], P('fsdp'), may hold values from -0.1875 to 0.1875
- conv_weight: bfloat16 [4, 4096], P(None, 'fsdp'), may hold values from -3 to 3
- head_decay: bfloat16 [2, 8], P(None, 'fsdp'), may hold values from -8 to 1, as said below
- mixer_gain: bfloat16 [1024], P('fsdp'), may hold values from 0.099609375 to 1.8984375
- heads_gain: bfloat16 [256], P('fsdp'), may hold values from 0.099609375 to 1.8984375
- output_weight: bfloat16 [2048, 1024], P('fsdp'), may hold values from -0.25 to 0.25
- feed_gain: bfloat16 [1024], P('fsdp'), may hold values from 0.099609375 to 1.8984375
- up_weight: bfloat16 [1024, 5632], P('fsdp'), may hold values from -0.1875 to 0.1875
- down_weight: bfloat16 [2816, 1024], P('fsdp'), may hold values from -0.15625 to 0.15625
Outputs:
- block_out: bfloat16 [12288, 1024], P(('dp', 'fsdp', 'sp'))
- tokens_grad: bfloat16 [12288, 1024], P(('dp', 'fsdp', 'sp'))
- input_grad: float32 [1024, 6144], P('fsdp')
- rate_grad: float32 [1024, 16], P('fsdp')
- conv_grad: float32 [4, 4096], P(None, 'fsdp')
- decay_grad: float32 [2, 8], P(None, 'fsdp')
- mixer_grad: float32 [1024], P('fsdp')
- heads_grad: float32 [256], P('fsdp')
- output_grad: float32 [2048, 1024], P('fsdp')
- feed_grad: float32 [1024], P('fsdp')
- up_grad: float32 [1024, 5632], P('fsdp')
- down_grad: float32 [2816, 1024], P('fsdp')
The draws below stay inside these ranges and needn't reach their ends.
Inputs may be any that keep to these rules, and one draw needn't show every extreme that they name: `head_decay`: row 0 holds the logarithms of the heads' decay rates, row 1 the offsets of their decay inputs.
All inputs are finite; a program needn't handle non-finite values.
Results may differ from the reference program's by a relative error of at most 0.019.
Values may be sent and summed in bfloat16 or wider, within the bound.
No kernel may reach another device: no remote copies, remote signals or barrier semaphores. Data moves between devices by JAX's collectives and lax.ppermute only.
A program may use at most 256 MiB of HBM per device.

```python
import math
import jax
import jax.numpy as jnp
import numpy as np
from jax import lax

D = 1024
H = 8
DK = 128
DV = 256
FF = 2816
CONV = 4
BLOCK = 64
NDOC = 4
TOK_DEV = 384
SEQ = 768
SEQS = 16
TOKENS = 12288


def draw_head_decay(key, part):
    key = jax.random.fold_in(key, 11)
    rate_key, offset_key = jax.random.split(key)
    lower_end, upper_end = (math.log(0.001), math.log(0.06))
    log_rates = jax.random.uniform(rate_key, (H,), jnp.float32, lower_end, upper_end)
    offsets = jax.random.uniform(offset_key, (H,), jnp.float32, -1.0, 1.0)
    return jnp.stack([log_rates, offsets]).astype(jnp.bfloat16)


def block_levels(rng, shape, cuts, low, largest):
    factor_of = 1.0
    for dim, shards_of in cuts:
        steps = jax.random.uniform(jax.random.fold_in(jax.random.fold_in(rng, 6), dim), (shards_of,), jnp.float32, low / len(cuts), largest / len(cuts))
        factor_of = factor_of * jnp.repeat(jnp.exp(steps), shape[dim] // shards_of).reshape((-1,) + (1,) * (len(shape) - 1 - dim))
    return factor_of


def split_up(count, total, reach, lean):
    portions = [(1 << 20) // math.isqrt(standing ** lean) + 1 for standing in range(2, count + 1)]
    surplus, counts = total - reach - (count - 1), [1] * (count - 1)
    while surplus > 0:
        free = [i for i in range(count - 1) if counts[i] < reach]
        pool, budget = sum([portions[i] for i in free]), surplus
        for i in free:
            more = min(reach - counts[i], max(1, budget * portions[i] // pool), surplus)
            counts[i] = counts[i] + more
            surplus = surplus - more
    return np.array([reach] + counts)


def ragged(key, amount, total, most, lean):
    if amount == 2:
        one = jax.random.randint(key, (), max(1, total - most), min(most, total - 1) + 1)
        return jnp.stack([one, total - one])
    tallies = jnp.asarray(split_up(amount, total, most, lean), jnp.int32)
    pairs = (amount - 1) // 2
    giver, taker = tallies[1:1 + 2 * pairs:2], tallies[2:2 + 2 * pairs:2]
    room = jnp.minimum(giver - 1, most - taker)
    moved = jax.random.randint(jax.random.fold_in(key, 1), (pairs,), 0, 1 << 20) % (room + 1)
    tallies = tallies.at[1:1 + 2 * pairs:2].set(giver - moved).at[2:2 + 2 * pairs:2].set(taker + moved)
    return tallies[jax.random.permutation(jax.random.fold_in(key, 2), amount)]


def gaussian(stream_key, shape, width, bound, cuts=(), kind=jnp.bfloat16):
    array = width * jax.random.normal(stream_key, shape, jnp.float32)
    if cuts:
        array = array * block_levels(stream_key, shape, cuts, -0.22, 0.18)
    return jnp.clip(array, -bound, bound).astype(kind)


def setup_inputs(seed: int = 0) -> dict:
    streams_of = jax.random.split(jax.random.key(seed), 14)
    tokens = gaussian(streams_of[0], (TOKENS, D), 1.0, 6.0, ((0, 32),))
    cotangent = gaussian(streams_of[1], (TOKENS, D), 1.0, 6.0, ((0, 32),))
    doc_lengths = jax.vmap(lambda own: ragged(own, NDOC, SEQ, SEQ - TOK_DEV // 2, 2))(jax.random.split(streams_of[2], SEQS)).reshape((SEQS, NDOC)).astype(jnp.int32)
    input_weight = gaussian(streams_of[3], (D, H * (2 * DK + 2 * DV)), D ** -0.5, 0.1875, ((0, 4),))
    rate_weight = gaussian(streams_of[4], (D, 2 * H), D ** -0.5, 0.1875, ((0, 4),))
    conv_weight = gaussian(streams_of[5], (CONV, H * (2 * DK + DV)), CONV ** -0.5, 3.0, ((1, 4),))
    head_decay = draw_head_decay(jax.random.fold_in(streams_of[13], 71), 0)
    mixer_gain = jnp.clip(1.0 + 0.18 * jax.random.normal(streams_of[7], (D,), jnp.float32), 0.099609375, 1.8984375).astype(jnp.bfloat16)
    heads_gain = jnp.clip(1.0 + 0.18 * jax.random.normal(streams_of[8], (DV,), jnp.float32), 0.099609375, 1.8984375).astype(jnp.bfloat16)
    output_weight = gaussian(streams_of[9], (H * DV, D), (H * DV // 4) ** -0.5, 0.25, ((0, 4),))
    feed_gain = jnp.clip(1.0 + 0.18 * jax.random.normal(streams_of[10], (D,), jnp.float32), 0.099609375, 1.8984375).astype(jnp.bfloat16)
    up_weight = gaussian(streams_of[11], (D, 2 * FF), D ** -0.5, 0.1875, ((0, 4),))
    down_weight = gaussian(streams_of[12], (FF, D), (FF // 2) ** -0.5, 0.15625, ((0, 4),))
    return dict(tokens=tokens, cotangent=cotangent, doc_lengths=doc_lengths, input_weight=input_weight, rate_weight=rate_weight, conv_weight=conv_weight, head_decay=head_decay, mixer_gain=mixer_gain, heads_gain=heads_gain, output_weight=output_weight, feed_gain=feed_gain, up_weight=up_weight, down_weight=down_weight)


EPSILON = 1e-06

@jax.custom_vjp
def low(v):
    return lax.optimization_barrier(v.astype(jnp.bfloat16)).astype(jnp.float32)

@jax.custom_vjp
def low_back(v):
    return v

def low_keep(v):
    return (low(v), None)

def low_pass(kept, grad):
    return (grad,)

def back_keep(v):
    return (v, None)

def back_low(kept, grad):
    return (low(grad),)
low.defvjp(low_keep, low_pass)
low_back.defvjp(back_keep, back_low)

def matmul(operand, weights):
    return jnp.dot(operand.astype(jnp.float32), weights.astype(jnp.float32), precision=lax.Precision.HIGHEST, preferred_element_type=jnp.float32)

def rms_norm(values, scales):
    return values * lax.rsqrt(lax.optimization_barrier(jnp.mean(values * values, axis=-1, keepdims=True)) + EPSILON) * scales

def short_conv(values, kernel, doc_ids):
    length = values.shape[0]
    result = values * kernel[0]
    for offset in range(1, kernel.shape[0]):
        shifted = jnp.concatenate([jnp.zeros((offset,) + values.shape[1:], jnp.float32), values[:length - offset]], axis=0)
        earlier = jnp.concatenate([jnp.full((offset,), -1, jnp.int32), doc_ids[:length - offset]])
        inside = (earlier == doc_ids).astype(jnp.float32)
        result = result + shifted * kernel[offset] * inside[:, None, None]
    return result

def block_step(carried_state, inputs):
    query_rows, key_rows, v, strength, log_decay, doc_ids, before = inputs
    block_len = query_rows.shape[1]
    query_rows = query_rows * query_rows.shape[2] ** (-0.5)
    cumulative = jnp.cumsum(log_decay, axis=-1)
    row_idx = lax.broadcasted_iota(jnp.int32, (block_len, block_len), 0)
    col_idx = lax.broadcasted_iota(jnp.int32, (block_len, block_len), 1)
    same_doc = doc_ids[:, None] == doc_ids[None, :]
    strictly = jnp.logical_and(same_doc, row_idx > col_idx)
    through = jnp.logical_and(same_doc, row_idx >= col_idx)
    spread = cumulative[:, :, None] - cumulative[:, None, :]
    strict = jnp.exp(jnp.where(strictly[None], spread, -1e+30))
    within = jnp.exp(jnp.where(through[None], spread, -1e+30))
    incoming_state = jnp.exp(cumulative) * (doc_ids == before).astype(jnp.float32)
    final_sum = cumulative[:, -1:]
    decay_to_last = jnp.exp(final_sum - cumulative) * (doc_ids == doc_ids[-1]).astype(jnp.float32)
    keep_factors = jnp.exp(final_sum[:, 0]) * (doc_ids[-1] == before).astype(jnp.float32)
    key_gram = jnp.einsum('nid,njd->nij', key_rows, key_rows, precision=lax.Precision.HIGHEST)
    system = jnp.eye(block_len, dtype=jnp.float32) + strength[:, :, None] * key_gram * strict
    targets = jnp.concatenate([(strength * incoming_state)[:, :, None] * key_rows, strength[:, :, None] * v], axis=-1)
    triangular_result = jax.scipy.linalg.solve_triangular(system, targets, lower=True, unit_diagonal=True)
    key_portion = triangular_result[:, :, :key_rows.shape[2]]
    corrected_values = triangular_result[:, :, key_rows.shape[2]:] - jnp.einsum('vfu,vub->vfb', key_portion, carried_state, precision=lax.Precision.HIGHEST)
    attention_scores = jnp.einsum('nid,njd->nij', query_rows, key_rows, precision=lax.Precision.HIGHEST) * within
    block_output = jnp.einsum('vfu,vub->vfb', incoming_state[:, :, None] * query_rows, carried_state, precision=lax.Precision.HIGHEST)
    block_output = block_output + jnp.einsum('faq,fqp->fap', attention_scores, corrected_values, precision=lax.Precision.HIGHEST)
    next_state = keep_factors[:, None, None] * carried_state + jnp.einsum('trz,trb->tzb', decay_to_last[:, :, None] * key_rows, corrected_values, precision=lax.Precision.HIGHEST)
    return (next_state, block_output)

def delta_mixer(query_rows, key_rows, v, rate_inputs, kernel_q, kernel_k, kernel_v, decay_params, doc_ids, block_size):
    length, head_count = (query_rows.shape[0], query_rows.shape[1])
    query_rows = jax.nn.silu(short_conv(query_rows, kernel_q, doc_ids))
    key_rows = jax.nn.silu(short_conv(key_rows, kernel_k, doc_ids))
    v = jax.nn.silu(short_conv(v, kernel_v, doc_ids))
    query_rows = low(query_rows * lax.rsqrt(lax.optimization_barrier(jnp.sum(query_rows * query_rows, axis=-1, keepdims=True)) + EPSILON))
    key_rows = low(key_rows * lax.rsqrt(lax.optimization_barrier(jnp.sum(key_rows * key_rows, axis=-1, keepdims=True)) + EPSILON))
    v = low(v)
    strength = jax.nn.sigmoid(rate_inputs[:, :, 1])
    log_decay = -jnp.exp(decay_params[0]) * jax.nn.softplus(rate_inputs[:, :, 0] + decay_params[1])
    block_count = length // block_size

    def to_blocks(values):
        return jnp.swapaxes(values.reshape((block_count, block_size) + values.shape[1:]), 1, 2)
    doc_blocks = doc_ids.reshape(block_count, block_size)
    before = jnp.concatenate([jnp.full((1,), -1, jnp.int32), doc_blocks[:-1, -1]])
    initial = jnp.zeros((head_count, query_rows.shape[2], v.shape[2]), jnp.float32)
    inputs = (to_blocks(query_rows), to_blocks(key_rows), to_blocks(v), to_blocks(strength), to_blocks(log_decay), doc_blocks, before)
    _, outputs = lax.scan(jax.checkpoint(block_step), initial, inputs)
    return jnp.swapaxes(outputs, 1, 2).reshape(length, head_count, v.shape[2])

def layer_block(x, doc_ids, params):
    input_weight, rate_weight, conv_weight, head_decay, mixer_gain, heads_gain, output_weight, feed_gain, up_weight, down_weight = params
    length = x.shape[0]
    qkv_cols = H * (2 * DK + DV)
    normed = low(rms_norm(x, mixer_gain))
    projected = matmul(normed, input_weight)
    qkv = low_back(low(projected[:, :qkv_cols]))
    gate_raw = low_back(projected[:, qkv_cols:])
    rate_inputs = low_back(low(matmul(normed, rate_weight))).reshape(length, H, 2)
    queries = qkv[:, :H * DK].reshape(length, H, DK)
    keys = qkv[:, H * DK:2 * H * DK].reshape(length, H, DK)
    values = qkv[:, 2 * H * DK:].reshape(length, H, DV)
    kernel_q = conv_weight[:, :H * DK].reshape(CONV, H, DK)
    kernel_k = conv_weight[:, H * DK:2 * H * DK].reshape(CONV, H, DK)
    kernel_v = conv_weight[:, 2 * H * DK:].reshape(CONV, H, DV)
    mixed = delta_mixer(queries, keys, values, rate_inputs, kernel_q, kernel_k, kernel_v, head_decay, doc_ids, BLOCK)
    mixed = low_back(low(mixed))
    gated = low(rms_norm(mixed, heads_gain) * jax.nn.silu(gate_raw).reshape(mixed.shape)).reshape(length, H * DV)
    attended = low_back(matmul(gated, output_weight))
    hidden = x + attended
    normed_two = low(rms_norm(hidden, feed_gain))
    gate_up = low_back(matmul(normed_two, up_weight))
    activated = low(jax.nn.silu(gate_up[:, :FF]) * gate_up[:, FF:])
    return hidden + low_back(matmul(activated, down_weight))

def reference(tokens, cotangent, doc_lengths, input_weight, rate_weight, conv_weight, head_decay, mixer_gain, heads_gain, output_weight, feed_gain, up_weight, down_weight):
    params = (input_weight.astype(jnp.float32), rate_weight.astype(jnp.float32), conv_weight.astype(jnp.float32), head_decay.astype(jnp.float32), mixer_gain.astype(jnp.float32), heads_gain.astype(jnp.float32), output_weight.astype(jnp.float32), feed_gain.astype(jnp.float32), up_weight.astype(jnp.float32), down_weight.astype(jnp.float32))

    def one_sequence(totals, inputs):
        x_seq, cot_seq, lengths = inputs
        ends = jnp.cumsum(lengths.astype(jnp.int32))
        positions = jnp.arange(SEQ, dtype=jnp.int32)
        doc_ids = lax.optimization_barrier(jnp.sum((positions[:, None] >= ends[None, :]).astype(jnp.int32), axis=1))

        def run_block(x_in, *weights):
            return layer_block(x_in, doc_ids, weights)
        result, pullback = jax.vjp(run_block, x_seq, *params)
        grads = pullback(cot_seq)
        totals = tuple((total + grad for total, grad in zip(totals, grads[1:])))
        return (totals, (result.astype(jnp.bfloat16), grads[0].astype(jnp.bfloat16)))
    zeros = tuple((jnp.zeros_like(param) for param in params))
    xs = (tokens.astype(jnp.float32).reshape(SEQS, SEQ, D), cotangent.astype(jnp.float32).reshape(SEQS, SEQ, D), doc_lengths)
    totals, (results, input_grads) = lax.scan(one_sequence, zeros, xs)
    return (results.reshape(TOKENS, D), input_grads.reshape(TOKENS, D), totals[0], totals[1], totals[2], totals[3], totals[4], totals[5], totals[6], totals[7], totals[8], totals[9])
```

```python
import jax
import jax.numpy as jnp
from jax import lax
from jax.experimental import pallas as pl
from jax.experimental.pallas import tpu as pltpu
from jax.sharding import PartitionSpec as P

H = 8
DK = 128
DV = 256
CONV = 4
BLOCK = 64
EPSILON = 1e-06
HALO = 16
STACK = 4
ROWS = STACK * BLOCK
SCALE = DK ** (-0.5)
VMEM_BYTES = 56 * 1024 * 1024
F32 = jnp.float32
BF16 = jnp.bfloat16


def mm(a, b, dims=((1,), (0,))):
    return lax.dot_general(
        a.astype(BF16), b.astype(BF16), (dims, ((), ())), preferred_element_type=F32
    )


def halves(a):
    high = a.astype(BF16)
    return high, (a - high.astype(F32)).astype(BF16)


def mm_fine(a, b):
    (ah, al), (bh, bl) = a, b
    return mm(ah, bh) + (mm(ah, bl) + mm(al, bh))


def stack_heads(ref, block, group, base, width):
    rows = pl.ds(pl.multiple_of(block * BLOCK, BLOCK), BLOCK)
    return jnp.concatenate(
        [
            ref[rows, base + (group * STACK + h) * width : base + (group * STACK + h + 1) * width]
            for h in range(STACK)
        ],
        axis=0,
    )


def store_heads(ref, block, group, base, width, value):
    rows = pl.ds(pl.multiple_of(block * BLOCK, BLOCK), BLOCK)
    for h in range(STACK):
        start = base + (group * STACK + h) * width
        ref[rows, start : start + width] = value[h * BLOCK : (h + 1) * BLOCK].astype(ref.dtype)


def head(value, h):
    return value[h * BLOCK : (h + 1) * BLOCK]


def columns(col_ref, block, group):
    packed = col_ref[block, group]
    return [packed[:, i : i + 1] for i in range(6)]


def decay_matrix(cum, doc, row_ref, block, group):
    rows = row_ref[block, group]
    i = lax.broadcasted_iota(jnp.int32, (ROWS, ROWS), 0)
    j = lax.broadcasted_iota(jnp.int32, (ROWS, ROWS), 1)
    inside = ((i // BLOCK) == (j // BLOCK)) & (i >= j) & (doc == rows[1:2])
    decay = jnp.exp(jnp.where(inside, cum - rows[0:1], -1e30))
    return decay, jnp.where(i > j, decay, 0.0)


def unit_inverse(lower):
    i = lax.broadcasted_iota(jnp.int32, (ROWS, ROWS), 0)
    j = lax.broadcasted_iota(jnp.int32, (ROWS, ROWS), 1)
    apart = jnp.bitwise_xor(i, j)
    inverse = jnp.where(i == j, 1.0, 0.0) - jnp.where(apart == 1, lower, 0.0)
    size = 2
    while size < BLOCK:
        cross = jnp.where((apart >= size) & (apart < 2 * size), lower, 0.0)
        parts = halves(inverse)
        inverse = inverse - mm_fine(parts, halves(mm_fine(halves(cross), parts)))
        size *= 2
    return inverse


def conv_taps(x, masks, weights):
    taps = [x[HALO:]]
    for s in range(1, CONV):
        taps.append(pltpu.roll(x, s, 0)[HALO:] * masks[s - 1])
    z = taps[0] * weights[0:1]
    for s in range(1, CONV):
        z = z + taps[s] * weights[s : s + 1]
    return taps, z


def conv_masks(mask_ref, length):
    return [
        jnp.broadcast_to(mask_ref[:, s : s + 1], (length, 128)) for s in range(CONV - 1)
    ]


def prepare_kernel(x_ref, cw_ref, mask_ref, col_ref, row_ref, n_ref, inv_ref, state_ref):
    length = n_ref.shape[0]
    blocks = length // BLOCK
    qk_cols = 2 * H * DK

    def chunk(c, normalise):
        lanes = pl.ds(pl.multiple_of(c * 128, 128), 128)
        masks = conv_masks(mask_ref, length)
        _, z = conv_taps(x_ref[:, lanes].astype(F32), masks, cw_ref[:, lanes])
        y = z * jax.nn.sigmoid(z)
        if normalise:
            y = y * lax.rsqrt(jnp.sum(y * y, axis=1, keepdims=True) + EPSILON)
        n_ref[:, lanes] = y.astype(BF16)

    @pl.loop(0, qk_cols // 128)
    def _(c):
        chunk(c, True)

    @pl.loop(qk_cols // 128, x_ref.shape[1] // 128)
    def _(c):
        chunk(c, False)

    @pl.loop(0, blocks)
    def _(block):
        for group in range(H // STACK):
            cum, beta, _, _, _, doc = columns(col_ref, block, group)
            keys = stack_heads(n_ref, block, group, H * DK, DK)
            _, strict = decay_matrix(cum, doc, row_ref, block, group)
            gram = mm(keys, keys, ((1,), (1,)))
            inv_ref[block, group] = unit_inverse(beta * gram * strict)

    state_ref[...] = jnp.zeros_like(state_ref)
    state_steps(n_ref, inv_ref, col_ref, state_ref)


def state_steps(n_ref, inv_ref, col_ref, state_ref):
    @pl.loop(0, n_ref.shape[0] // BLOCK)
    def _(block):
        for group in range(H // STACK):
            _, beta, a, d, kappa, _ = columns(col_ref, block, group)
            keys = stack_heads(n_ref, block, group, H * DK, DK)
            values = stack_heads(n_ref, block, group, 2 * H * DK, DV).astype(F32)
            seen = jnp.concatenate(
                [mm(head(keys, h), state_ref[group * STACK + h]) for h in range(STACK)], axis=0
            )
            corrected = mm(inv_ref[block, group], beta * (values - a * seen))
            update = d * corrected
            for h in range(STACK):
                n = group * STACK + h
                state_ref[n] = kappa[h * BLOCK : h * BLOCK + 1] * state_ref[n] + mm(
                    head(keys, h), head(update, h), ((0,), (0,))
                )


def state_kernel(n_ref, inv_ref, col_ref, start_ref, state_ref):
    state_ref[...] = start_ref[...].astype(F32)
    state_steps(n_ref, inv_ref, col_ref, state_ref)


def scan_kernel(n_ref, inv_ref, col_ref, row_ref, start_ref, out_ref, cor_ref, states_ref, state):
    state[...] = start_ref[...].astype(F32)

    @pl.loop(0, n_ref.shape[0] // BLOCK)
    def _(block):
        for group in range(H // STACK):
            cum, beta, a, d, kappa, doc = columns(col_ref, block, group)
            queries = stack_heads(n_ref, block, group, 0, DK)
            keys = stack_heads(n_ref, block, group, H * DK, DK)
            values = stack_heads(n_ref, block, group, 2 * H * DK, DV).astype(F32)
            within, _ = decay_matrix(cum, doc, row_ref, block, group)
            scores = SCALE * mm(queries, keys, ((1,), (1,))) * within
            both = []
            for h in range(STACK):
                low = state[group * STACK + h].astype(BF16)
                states_ref[block, group * STACK + h] = low
                both.append(mm(jnp.concatenate([head(keys, h), head(queries, h)], axis=0), low))
            seen = jnp.concatenate([b[:BLOCK] for b in both], axis=0)
            asked = jnp.concatenate([b[BLOCK:] for b in both], axis=0)
            corrected = mm(inv_ref[block, group], beta * (values - a * seen))
            cor_ref[block, group] = corrected.astype(BF16)
            out = (SCALE * a) * asked + mm(scores, corrected)
            store_heads(out_ref, block, group, 0, DV, out)
            update = d * corrected
            for h in range(STACK):
                n = group * STACK + h
                state[n] = kappa[h * BLOCK : h * BLOCK + 1] * state[n] + mm(
                    head(keys, h), head(update, h), ((0,), (0,))
                )


def back_state_kernel(n_ref, inv_ref, col_ref, row_ref, dout_ref, start_ref, dstate_ref):
    blocks = n_ref.shape[0] // BLOCK
    dstate_ref[...] = start_ref[...].astype(F32)

    @pl.loop(0, blocks)
    def _(step):
        block = blocks - 1 - step
        for group in range(H // STACK):
            cum, beta, a, d, kappa, doc = columns(col_ref, block, group)
            queries = stack_heads(n_ref, block, group, 0, DK)
            keys = stack_heads(n_ref, block, group, H * DK, DK)
            within, _ = decay_matrix(cum, doc, row_ref, block, group)
            scores = SCALE * mm(queries, keys, ((1,), (1,))) * within
            dout = stack_heads(dout_ref, block, group, 0, DV)
            wide = (SCALE * a) * dout.astype(F32)
            pulled = jnp.concatenate(
                [mm(head(keys, h), dstate_ref[group * STACK + h]) for h in range(STACK)], axis=0
            )
            d_cor = mm(scores, dout, ((0,), (0,))) + d * pulled
            d_right = mm(inv_ref[block, group], d_cor, ((0,), (0,)))
            d_seen = (-a * beta) * d_right
            for h in range(STACK):
                n = group * STACK + h
                left = jnp.concatenate([head(keys, h), head(queries, h)], axis=0)
                right = jnp.concatenate([head(d_seen, h), head(wide, h)], axis=0)
                dstate_ref[n] = kappa[h * BLOCK : h * BLOCK + 1] * dstate_ref[n] + mm(
                    left, right, ((0,), (0,))
                )


def back_kernel(
    x_ref,
    cw_ref,
    mask_ref,
    n_ref,
    inv_ref,
    col_ref,
    row_ref,
    dout_ref,
    cor_ref,
    states_ref,
    start_ref,
    dx_ref,
    dcw_ref,
    gcol_ref,
    grow_ref,
    dstate,
    dn_ref,
):
    length = n_ref.shape[0]
    blocks = length // BLOCK
    dstate[...] = start_ref[...].astype(F32)

    @pl.loop(0, blocks)
    def _(step):
        block = blocks - 1 - step
        for group in range(H // STACK):
            cum, beta, a, d, kappa, doc = columns(col_ref, block, group)
            queries = stack_heads(n_ref, block, group, 0, DK)
            keys = stack_heads(n_ref, block, group, H * DK, DK)
            values = stack_heads(n_ref, block, group, 2 * H * DK, DV).astype(F32)
            within, strict = decay_matrix(cum, doc, row_ref, block, group)
            scores = SCALE * mm(queries, keys, ((1,), (1,))) * within
            weighted = mm(keys, keys, ((1,), (1,))) * strict
            dout = stack_heads(dout_ref, block, group, 0, DV)
            dout_wide = dout.astype(F32)
            corrected = cor_ref[block, group]
            cor_wide = corrected.astype(F32)
            wide = (SCALE * a) * dout_wide
            pulled, seen, asked, dk_state, d_kappa = [], [], [], [], []
            update = (d * cor_wide).astype(BF16)
            for h in range(STACK):
                n = group * STACK + h
                state = states_ref[block, n]
                after = dstate[n]
                after_low = after.astype(BF16)
                both = mm(jnp.concatenate([head(keys, h), head(queries, h)], axis=0), state)
                seen.append(both[:BLOCK])
                asked.append(both[BLOCK:])
                pulled.append(mm(head(keys, h), after_low))
                dk_state.append(mm(head(update, h), after_low, ((1,), (1,))))
                total = jnp.sum(
                    jnp.sum(state.astype(F32) * after, axis=0, keepdims=True),
                    axis=1,
                    keepdims=True,
                )
                d_kappa.append(jnp.broadcast_to(total * (1.0 / BLOCK), (BLOCK, 1)))
            pulled, seen, asked, d_kappa = (
                jnp.concatenate(p, axis=0) for p in (pulled, seen, asked, d_kappa)
            )
            d_cor = mm(scores, dout, ((0,), (0,))) + d * pulled
            d_right = mm(inv_ref[block, group], d_cor, ((0,), (0,)))
            scaled = beta * d_right
            d_seen = -a * scaled
            dk_left, dq_left = [], []
            for h in range(STACK):
                n = group * STACK + h
                left = jnp.concatenate([head(keys, h), head(queries, h)], axis=0)
                right = jnp.concatenate([head(d_seen, h), head(wide, h)], axis=0).astype(BF16)
                both = mm(right, states_ref[block, n], ((1,), (1,)))
                dk_left.append(both[:BLOCK])
                dq_left.append(both[BLOCK:])
                dstate[n] = kappa[h * BLOCK : h * BLOCK + 1] * dstate[n] + mm(
                    left, right, ((0,), (0,))
                )
            d_scores = mm(dout, corrected, ((1,), (1,)))
            d_system = -mm(d_right, corrected, ((1,), (1,)))
            to_rows = (SCALE * d_scores * within).astype(BF16)
            by_gram = d_system * weighted
            to_keys = (beta * d_system * strict).astype(BF16)
            dq = jnp.concatenate(dq_left, axis=0) + mm(to_rows, keys)
            dk = (
                jnp.concatenate(dk_left, axis=0)
                + jnp.concatenate(dk_state, axis=0)
                + mm(to_rows, queries, ((0,), (0,)))
                + mm(to_keys, keys)
                + mm(to_keys, keys, ((0,), (0,)))
            )
            store_heads(dn_ref, block, group, 0, DK, dq)
            store_heads(dn_ref, block, group, H * DK, DK, dk)
            store_heads(dn_ref, block, group, 2 * H * DK, DV, scaled)
            spread = d_scores * scores + beta * by_gram
            d_cum = jnp.sum(spread, axis=1, keepdims=True)
            d_beta = jnp.sum(by_gram, axis=1, keepdims=True) + jnp.sum(
                d_right * (values - a * seen), axis=1, keepdims=True
            )
            d_a = jnp.sum(SCALE * dout_wide * asked - scaled * seen, axis=1, keepdims=True)
            d_d = jnp.sum(cor_wide * pulled, axis=1, keepdims=True)
            lane = lax.broadcasted_iota(jnp.int32, (ROWS, 8), 1)
            packed = jnp.zeros((ROWS, 8), F32)
            for i, part in enumerate((d_cum, d_beta, d_a, d_d, d_kappa)):
                packed = jnp.where(lane == i, part, packed)
            gcol_ref[block, group] = packed
            grow_ref[block, group] = jnp.broadcast_to(
                -jnp.sum(spread, axis=0, keepdims=True), (8, ROWS)
            )

    def chunk(c, normalise):
        lanes = pl.ds(pl.multiple_of(c * 128, 128), 128)
        masks = conv_masks(mask_ref, length)
        weights = cw_ref[:, lanes]
        taps, z = conv_taps(x_ref[:, lanes].astype(F32), masks, weights)
        gate = jax.nn.sigmoid(z)
        dn = dn_ref[:, lanes]
        if normalise:
            y = z * gate
            r = lax.rsqrt(jnp.sum(y * y, axis=1, keepdims=True) + EPSILON)
            dn = r * dn - y * (r * r * r * jnp.sum(y * dn, axis=1, keepdims=True))
        dz = dn * gate * (1.0 + z * (1.0 - gate))
        edge = jnp.zeros((HALO, 128), F32)
        dx = jnp.concatenate([edge, dz * weights[0:1]], axis=0)
        sums = [jnp.sum(dz * taps[0], axis=0, keepdims=True)]
        for s in range(1, CONV):
            sums.append(jnp.sum(dz * taps[s], axis=0, keepdims=True))
            moved = jnp.concatenate([edge, dz * masks[s - 1] * weights[s : s + 1]], axis=0)
            dx = dx + pltpu.roll(moved, length + HALO - s, 0)
        dx_ref[:, lanes] = dx.astype(BF16)
        dcw_ref[:, lanes] = jnp.concatenate(sums, axis=0)

    qk_cols = 2 * H * DK

    @pl.loop(0, qk_cols // 128)
    def _(c):
        chunk(c, True)

    @pl.loop(qk_cols // 128, x_ref.shape[1] // 128)
    def _(c):
        chunk(c, False)


def call(kernel, outs, scratch, *args, flops=0):
    return pl.pallas_call(
        kernel,
        out_shape=[jax.ShapeDtypeStruct(s, t) for s, t in outs],
        in_specs=[pl.BlockSpec(memory_space=pltpu.VMEM)] * len(args),
        out_specs=[pl.BlockSpec(memory_space=pltpu.VMEM)] * len(outs),
        scratch_shapes=scratch,
        compiler_params=pltpu.CompilerParams(vmem_limit_bytes=VMEM_BYTES),
        cost_estimate=pl.CostEstimate(
            flops=flops, bytes_accessed=sum(a.nbytes for a in args), transcendentals=0
        ),
    )(*args)


def mixer(x, weights, rates, decay, doc_all, member, sp_size):
    length = x.shape[0] - HALO
    blocks = length // BLOCK
    groups = H // STACK
    channels = x.shape[1]
    padded = jnp.concatenate([jnp.full((HALO,), -1, jnp.int32), doc_all])
    near = lax.dynamic_slice_in_dim(padded, member * length, length + HALO, 0)
    docs = near[HALO:]
    masks = jnp.stack(
        [(near[HALO - s : HALO - s + length] == docs).astype(F32) for s in range(1, CONV)]
        + [jnp.zeros((length,), F32)] * (8 - CONV + 1),
        axis=1,
    )
    doc_blocks = docs.reshape(blocks, 1, BLOCK)
    before = jnp.concatenate([near[HALO - 1 : HALO], doc_blocks[:-1, 0, -1]]).reshape(
        blocks, 1, 1
    )
    last = doc_blocks[:, :, -1:]
    from_before = (doc_blocks == before).astype(F32)
    to_last = (doc_blocks == last).astype(F32)
    kept = (last == before).astype(F32)

    def small(rates, decay):
        by_block = jnp.transpose(rates.reshape(blocks, BLOCK, H, 2), (3, 0, 2, 1))
        beta = jax.nn.sigmoid(by_block[1])
        offset = decay[1].reshape(1, H, 1)
        log_decay = -jnp.exp(decay[0]).reshape(1, H, 1) * jax.nn.softplus(by_block[0] + offset)
        i = lax.broadcasted_iota(jnp.int32, (BLOCK, BLOCK), 0)
        j = lax.broadcasted_iota(jnp.int32, (BLOCK, BLOCK), 1)
        upper = (i <= j).astype(F32)
        cum = jnp.einsum("bhi,ij->bhj", log_decay, upper, precision=lax.Precision.HIGHEST)
        final = cum[:, :, -1:]
        a = jnp.exp(cum) * from_before
        d = jnp.exp(final - cum) * to_last
        kappa = jnp.broadcast_to(jnp.exp(final) * kept, cum.shape)
        return jnp.stack([cum, beta, a, d, kappa], axis=0)

    five, pull_small = jax.vjp(small, rates, decay)
    doc_row = jnp.broadcast_to(doc_blocks.astype(F32), (blocks, H, BLOCK))
    packed = jnp.concatenate([five, doc_row[None], jnp.zeros((2,) + doc_row.shape, F32)], axis=0)
    packed = packed.reshape(8, blocks, groups, ROWS)
    col = jnp.transpose(packed, (1, 2, 3, 0))
    row = jnp.transpose(jnp.stack([packed[0], packed[5]] + [packed[6]] * 6), (1, 2, 0, 3))

    n_shape = ((length, channels), BF16)
    inv_shape = ((blocks, groups, ROWS, ROWS), F32)
    state_shape = ((H, DK, DV), F32)
    cor_shape = ((blocks, groups, ROWS, ROWS), BF16)
    n, inv, state = call(
        prepare_kernel, [n_shape, inv_shape, state_shape], [], x, weights, masks, col, row
    )
    ahead = [(i, i + 1) for i in range(sp_size - 1)]
    behind = [(i + 1, i) for i in range(sp_size - 1)]
    start = lax.ppermute(state.astype(BF16), "sp", ahead)
    for _ in range(sp_size - 2):
        (state,) = call(state_kernel, [state_shape], [], n, inv, col, start)
        start = lax.ppermute(state.astype(BF16), "sp", ahead)
    mixed, cor, states = call(
        scan_kernel,
        [((length, H * DV), BF16), cor_shape, ((blocks, H, DK, DV), BF16)],
        [pltpu.VMEM((H, DK, DV), F32)],
        n,
        inv,
        col,
        row,
        start,
    )

    def pull(dout):
        dstart = jnp.zeros((H, DK, DV), BF16)
        for _ in range(sp_size - 1):
            (dstate,) = call(
                back_state_kernel, [state_shape], [], n, inv, col, row, dout, dstart
            )
            dstart = lax.ppermute(dstate.astype(BF16), "sp", behind)
        dx, dcw, gcol, grow = call(
            back_kernel,
            [
                ((length + HALO, channels), BF16),
                ((CONV, channels), F32),
                ((blocks, groups, ROWS, 8), F32),
                ((blocks, groups, 8, ROWS), F32),
            ],
            [pltpu.VMEM((H, DK, DV), F32), pltpu.VMEM((length, channels), F32)],
            x,
            weights,
            masks,
            n,
            inv,
            col,
            row,
            dout,
            cor,
            states,
            dstart,
        )
        grads = jnp.transpose(gcol[..., :5], (3, 0, 1, 2))
        grads = grads.at[0].add(grow[:, :, 0])
        d_rates, d_decay = pull_small(grads.reshape(5, blocks, H, BLOCK))
        from_next = lax.ppermute(dx[:HALO], "sp", behind)
        return dx, from_next, dcw, d_rates, d_decay

    return mixed, pull


def rms_norm(values, scales):
    return values * lax.rsqrt(jnp.mean(values * values, axis=-1, keepdims=True) + EPSILON) * scales


def output_gate(mixed, gate_raw, scales):
    length = mixed.shape[0]
    normed = rms_norm(mixed.reshape(length, H, DV), scales)
    return (normed * jax.nn.silu(gate_raw).reshape(length, H, DV)).reshape(length, H * DV)


def residual_norm(values, attended, scales):
    hidden = values + attended
    return (hidden, rms_norm(hidden, scales))


def feed_act(gate_up):
    half_width = gate_up.shape[1] // 2
    return jax.nn.silu(gate_up[:, :half_width]) * gate_up[:, half_width:]


WEIGHT_AXES = ("fsdp", "dp", "sp")
COPY_AXES = ("dp", "sp")


def copies():
    count = lax.axis_size("dp") * lax.axis_size("sp")
    return count, lax.axis_index("dp") * lax.axis_size("sp") + lax.axis_index("sp")


def gather_rows(shard):
    count, own = copies()
    rows = shard.shape[0] // count
    piece = lax.dynamic_slice_in_dim(shard, own * rows, rows, 0)
    return lax.all_gather(piece, WEIGHT_AXES, axis=0, tiled=True)


def sum_rows(grad):
    piece = lax.psum_scatter(
        grad.astype(BF16), WEIGHT_AXES, scatter_dimension=0, tiled=True
    )
    return lax.all_gather(piece, COPY_AXES, axis=0, tiled=True).astype(F32)


def gather_small(parts):
    flat = jnp.concatenate([p.reshape(-1) for p in parts])
    size = flat.shape[0]
    flat = jnp.pad(flat, (0, -size % 1024)).reshape(-1, 128)
    every = lax.all_gather(flat, "fsdp", axis=0).reshape(lax.axis_size("fsdp"), -1)
    out, start = [], 0
    for p in parts:
        out.append(every[:, start : start + p.size].reshape((-1,) + p.shape))
        start += p.size
    return out


def sum_small(parts):
    flat = jnp.concatenate([p.reshape(-1) for p in parts])
    size = flat.shape[0]
    flat = jnp.pad(flat, (0, -size % 1024)).reshape(-1, 128)
    total = lax.psum(flat, ("dp", "fsdp", "sp")).reshape(-1)
    out, start = [], 0
    for p in parts:
        out.append(total[start : start + p.size].reshape(p.shape))
        start += p.size
    return out


def own_part(value, axis):
    size = value.shape[axis] // lax.axis_size("fsdp")
    return lax.dynamic_slice_in_dim(value, lax.axis_index("fsdp") * size, size, axis)


def body(
    tokens,
    cotangent,
    doc_lengths,
    input_weight,
    rate_weight,
    conv_weight,
    head_decay,
    mixer_gain,
    heads_gain,
    output_weight,
    feed_gain,
    up_weight,
    down_weight,
):
    length = tokens.shape[0]
    sp_size = lax.axis_size("sp")
    member = lax.axis_index("sp")
    qkv_cols = H * (2 * DK + DV)
    rate_all, conv_all, decay_all, mixer_all, heads_all, feed_all = gather_small(
        (rate_weight, conv_weight, head_decay, mixer_gain, heads_gain, feed_gain)
    )
    rate_full = rate_all.reshape(-1, 2 * H)
    conv_full = jnp.swapaxes(conv_all, 0, 1).reshape(CONV, -1).astype(F32)
    decay_full = jnp.swapaxes(decay_all, 0, 1).reshape(2, H).astype(F32)
    mixer_scale = mixer_all.reshape(-1).astype(F32)
    heads_scale = heads_all.reshape(-1).astype(F32)
    feed_scale = feed_all.reshape(-1).astype(F32)
    in_full = gather_rows(input_weight)
    out_full = gather_rows(output_weight)
    up_full = gather_rows(up_weight)
    down_full = gather_rows(down_weight)

    ends = jnp.cumsum(doc_lengths[0])
    positions = lax.broadcasted_iota(jnp.int32, (length * sp_size, 1), 0)
    doc_ids = jnp.sum((positions >= ends[None, :]).astype(jnp.int32), axis=1)

    ahead = [(i, i + 1) for i in range(sp_size - 1)]
    halo = lax.ppermute(tokens[-HALO:], "sp", ahead)
    x_float = tokens.astype(F32)
    normed, pull_norm = jax.vjp(rms_norm, x_float, mixer_scale)
    normed_low = normed.astype(BF16)
    halo_low = rms_norm(halo.astype(F32), mixer_scale).astype(BF16)
    normed_more = jnp.concatenate([halo_low, normed_low], axis=0)
    qkv = jnp.dot(normed_more, in_full[:, :qkv_cols], preferred_element_type=F32).astype(BF16)
    gate_raw = jnp.dot(normed_low, in_full[:, qkv_cols:], preferred_element_type=F32)
    rate_raw = jnp.dot(normed_low, rate_full, preferred_element_type=F32)
    rates = rate_raw.astype(BF16).astype(F32).reshape(length, H, 2)
    mixed, pull_mix = mixer(qkv, conv_full, rates, decay_full, doc_ids, member, sp_size)
    gated, pull_gate = jax.vjp(output_gate, mixed.astype(F32), gate_raw, heads_scale)
    gated_low = gated.astype(BF16)
    attended = jnp.dot(gated_low, out_full, preferred_element_type=F32)
    (hidden, normed_two), pull_resid = jax.vjp(residual_norm, x_float, attended, feed_scale)
    two_low = normed_two.astype(BF16)
    gate_up = jnp.dot(two_low, up_full, preferred_element_type=F32)
    activated, pull_act = jax.vjp(feed_act, gate_up)
    act_low = activated.astype(BF16)
    block_out = (hidden + jnp.dot(act_low, down_full, preferred_element_type=F32)).astype(BF16)
    down_grad = jnp.einsum("tf,td->fd", act_low, cotangent, preferred_element_type=F32)
    down_shard = sum_rows(down_grad)
    d_act = jnp.einsum("td,fd->tf", cotangent, down_full, preferred_element_type=F32)
    d_gu_low = pull_act(d_act)[0].astype(BF16)
    up_grad = jnp.einsum("td,tf->df", two_low, d_gu_low, preferred_element_type=F32)
    up_shard = sum_rows(up_grad)
    d_two = jnp.einsum("tf,df->td", d_gu_low, up_full, preferred_element_type=F32)
    d_resid, d_attended, feed_grad = pull_resid((cotangent.astype(F32), d_two))
    d_att_low = d_attended.astype(BF16)
    output_grad = jnp.einsum("te,td->ed", gated_low, d_att_low, preferred_element_type=F32)
    output_shard = sum_rows(output_grad)
    d_gated = jnp.einsum("td,ed->te", d_att_low, out_full, preferred_element_type=F32)
    d_mixed, d_gate, heads_grad = pull_gate(d_gated)
    d_gate_low = d_gate.astype(BF16)
    gate_shard = sum_rows(
        jnp.einsum("td,tf->df", normed_low, d_gate_low, preferred_element_type=F32)
    )
    d_more, from_next, conv_grad, d_rates, decay_grad = pull_mix(d_mixed.astype(BF16))
    edge = jnp.pad(from_next.astype(F32), ((length - HALO, 0), (0, 0)))
    d_qkv = (d_more[HALO:].astype(F32) + edge).astype(BF16)
    d_rate_low = d_rates.reshape(length, 2 * H).astype(BF16)
    qkv_shard = sum_rows(
        jnp.einsum("td,tf->df", normed_low, d_qkv, preferred_element_type=F32)
    )
    rate_grad = jnp.einsum("td,tf->df", normed_low, d_rate_low, preferred_element_type=F32)
    d_project = jnp.concatenate([d_qkv, d_gate_low], axis=1)
    d_normed = jnp.einsum("tf,df->td", d_project, in_full, preferred_element_type=F32)
    d_normed = d_normed + jnp.einsum(
        "tf,df->td", d_rate_low, rate_full, preferred_element_type=F32
    )
    d_front, mixer_grad = pull_norm(d_normed)
    tokens_grad = (d_resid + d_front).astype(BF16)
    rate_sum, conv_sum, decay_sum, mixer_sum, heads_sum, feed_sum = sum_small(
        (rate_grad, conv_grad, decay_grad, mixer_grad, heads_grad, feed_grad)
    )
    return (
        block_out,
        tokens_grad,
        jnp.concatenate([qkv_shard, gate_shard], axis=1),
        own_part(rate_sum, 0),
        own_part(conv_sum, 1),
        own_part(decay_sum, 1),
        own_part(mixer_sum, 0),
        own_part(heads_sum, 0),
        output_shard,
        own_part(feed_sum, 0),
        up_shard,
        down_shard,
    )


def solution(mesh):
    rows = P(("dp", "fsdp", "sp"), None)
    split = P("fsdp", None)
    return jax.shard_map(
        body,
        mesh=mesh,
        in_specs=(
            rows,
            rows,
            P(("dp", "fsdp"), None),
            split,
            split,
            P(None, "fsdp"),
            P(None, "fsdp"),
            P("fsdp"),
            P("fsdp"),
            split,
            P("fsdp"),
            split,
            split,
        ),
        out_specs=(
            rows,
            rows,
            split,
            split,
            P(None, "fsdp"),
            P(None, "fsdp"),
            P("fsdp"),
            P("fsdp"),
            split,
            P("fsdp"),
            split,
            split,
        ),
        check_vma=False,
    )
```

```python
import jax
import jax.numpy as jnp
from jax import lax
from jax.experimental import pallas as pl
from jax.experimental.pallas import tpu as pltpu
from jax.sharding import PartitionSpec as P

H = 8
DK = 128
DV = 256
CONV = 4
BLOCK = 64
EPSILON = 1e-06
HALO = 16
STACK = 4
ROWS = STACK * BLOCK
SCALE = DK ** (-0.5)
VMEM_BYTES = 56 * 1024 * 1024
F32 = jnp.float32
BF16 = jnp.bfloat16


def mm(a, b, dims=((1,), (0,))):
    return lax.dot_general(
        a.astype(BF16), b.astype(BF16), (dims, ((), ())), preferred_element_type=F32
    )


def halves(a):
    high = a.astype(BF16)
    return high, (a - high.astype(F32)).astype(BF16)


def mm_fine(a, b):
    (ah, al), (bh, bl) = a, b
    return mm(ah, bh) + (mm(ah, bl) + mm(al, bh))


def stack_heads(ref, block, group, base, width):
    rows = pl.ds(pl.multiple_of(block * BLOCK, BLOCK), BLOCK)
    return jnp.concatenate(
        [
            ref[rows, base + (group * STACK + h) * width : base + (group * STACK + h + 1) * width]
            for h in range(STACK)
        ],
        axis=0,
    )


def store_heads(ref, block, group, base, width, value):
    rows = pl.ds(pl.multiple_of(block * BLOCK, BLOCK), BLOCK)
    for h in range(STACK):
        start = base + (group * STACK + h) * width
        ref[rows, start : start + width] = value[h * BLOCK : (h + 1) * BLOCK].astype(ref.dtype)


def head(value, h):
    return value[h * BLOCK : (h + 1) * BLOCK]


def columns(col_ref, block, group):
    packed = col_ref[block, group]
    return [packed[:, i : i + 1] for i in range(6)]


def decay_matrix(cum, doc, row_ref, block, group):
    rows = row_ref[block, group]
    i = lax.broadcasted_iota(jnp.int32, (ROWS, ROWS), 0)
    j = lax.broadcasted_iota(jnp.int32, (ROWS, ROWS), 1)
    inside = ((i // BLOCK) == (j // BLOCK)) & (i >= j) & (doc == rows[1:2])
    decay = jnp.exp(jnp.where(inside, cum - rows[0:1], -1e30))
    return decay, jnp.where(i > j, decay, 0.0)


def unit_inverses(lowers):
    i = lax.broadcasted_iota(jnp.int32, (ROWS, ROWS), 0)
    j = lax.broadcasted_iota(jnp.int32, (ROWS, ROWS), 1)
    apart = jnp.bitwise_xor(i, j)
    inverses = [
        jnp.where(i == j, 1.0, 0.0) - jnp.where(apart == 1, lower, 0.0) for lower in lowers
    ]
    size = 2
    while size < BLOCK:
        cross = (apart >= size) & (apart < 2 * size)
        parts = [halves(inverse) for inverse in inverses]
        right = [
            halves(mm_fine(halves(jnp.where(cross, lower, 0.0)), part))
            for lower, part in zip(lowers, parts)
        ]
        inverses = [
            inverse - mm_fine(part, r) for inverse, part, r in zip(inverses, parts, right)
        ]
        size *= 2
    return inverses


def conv_taps(x, masks, weights):
    taps = [x[HALO:]]
    for s in range(1, CONV):
        taps.append(pltpu.roll(x, s, 0)[HALO:] * masks[s - 1])
    z = taps[0] * weights[0:1]
    for s in range(1, CONV):
        z = z + taps[s] * weights[s : s + 1]
    return taps, z


def conv_masks(mask_ref, length):
    return [
        jnp.broadcast_to(mask_ref[:, s : s + 1], (length, 128)) for s in range(CONV - 1)
    ]


def conv_kernel(x_ref, cw_ref, mask_ref, n_ref):
    length = n_ref.shape[0]
    qk_cols = 2 * H * DK

    def chunk(c, normalise):
        lanes = pl.ds(pl.multiple_of(c * 128, 128), 128)
        masks = conv_masks(mask_ref, length)
        _, z = conv_taps(x_ref[:, lanes].astype(F32), masks, cw_ref[:, lanes])
        y = z * jax.nn.sigmoid(z)
        if normalise:
            y = y * lax.rsqrt(jnp.sum(y * y, axis=1, keepdims=True) + EPSILON)
        n_ref[:, lanes] = y.astype(BF16)

    @pl.loop(0, qk_cols // 128)
    def _(c):
        chunk(c, True)

    @pl.loop(qk_cols // 128, x_ref.shape[1] // 128)
    def _(c):
        chunk(c, False)


def inverse_kernel(n_ref, col_ref, row_ref, inv_ref):
    @pl.loop(0, n_ref.shape[0] // BLOCK)
    def _(block):
        lowers = []
        for group in range(H // STACK):
            cum, beta, _, _, _, doc = columns(col_ref, block, group)
            keys = stack_heads(n_ref, block, group, H * DK, DK)
            _, strict = decay_matrix(cum, doc, row_ref, block, group)
            lowers.append(beta * mm(keys, keys, ((1,), (1,))) * strict)
        for group, inverse in enumerate(unit_inverses(lowers)):
            inv_ref[block, group] = inverse


def state_steps(n_ref, inv_ref, col_ref, state_ref):
    @pl.loop(0, n_ref.shape[0] // BLOCK)
    def _(block):
        for group in range(H // STACK):
            _, beta, a, d, kappa, _ = columns(col_ref, block, group)
            keys = stack_heads(n_ref, block, group, H * DK, DK)
            values = stack_heads(n_ref, block, group, 2 * H * DK, DV).astype(F32)
            seen = jnp.concatenate(
                [mm(head(keys, h), state_ref[group * STACK + h]) for h in range(STACK)], axis=0
            )
            corrected = mm(inv_ref[block, group], beta * (values - a * seen))
            update = d * corrected
            for h in range(STACK):
                n = group * STACK + h
                state_ref[n] = kappa[h * BLOCK : h * BLOCK + 1] * state_ref[n] + mm(
                    head(keys, h), head(update, h), ((0,), (0,))
                )


def state_kernel(n_ref, inv_ref, col_ref, start_ref, state_ref):
    state_ref[...] = start_ref[...].astype(F32)
    state_steps(n_ref, inv_ref, col_ref, state_ref)


def scan_kernel(n_ref, inv_ref, col_ref, row_ref, start_ref, out_ref, cor_ref, states_ref, state):
    state[...] = start_ref[...].astype(F32)

    @pl.loop(0, n_ref.shape[0] // BLOCK)
    def _(block):
        for group in range(H // STACK):
            cum, beta, a, d, kappa, doc = columns(col_ref, block, group)
            queries = stack_heads(n_ref, block, group, 0, DK)
            keys = stack_heads(n_ref, block, group, H * DK, DK)
            values = stack_heads(n_ref, block, group, 2 * H * DK, DV).astype(F32)
            within, _ = decay_matrix(cum, doc, row_ref, block, group)
            scores = SCALE * mm(queries, keys, ((1,), (1,))) * within
            both = []
            for h in range(STACK):
                low = state[group * STACK + h].astype(BF16)
                states_ref[block, group * STACK + h] = low
                both.append(mm(jnp.concatenate([head(keys, h), head(queries, h)], axis=0), low))
            seen = jnp.concatenate([b[:BLOCK] for b in both], axis=0)
            asked = jnp.concatenate([b[BLOCK:] for b in both], axis=0)
            corrected = mm(inv_ref[block, group], beta * (values - a * seen))
            cor_ref[block, group] = corrected.astype(BF16)
            out = (SCALE * a) * asked + mm(scores, corrected)
            store_heads(out_ref, block, group, 0, DV, out)
            update = d * corrected
            for h in range(STACK):
                n = group * STACK + h
                state[n] = kappa[h * BLOCK : h * BLOCK + 1] * state[n] + mm(
                    head(keys, h), head(update, h), ((0,), (0,))
                )


def back_state_kernel(n_ref, inv_ref, col_ref, row_ref, dout_ref, start_ref, dstate_ref):
    blocks = n_ref.shape[0] // BLOCK
    dstate_ref[...] = start_ref[...].astype(F32)

    @pl.loop(0, blocks)
    def _(step):
        block = blocks - 1 - step
        for group in range(H // STACK):
            cum, beta, a, d, kappa, doc = columns(col_ref, block, group)
            queries = stack_heads(n_ref, block, group, 0, DK)
            keys = stack_heads(n_ref, block, group, H * DK, DK)
            within, _ = decay_matrix(cum, doc, row_ref, block, group)
            scores = SCALE * mm(queries, keys, ((1,), (1,))) * within
            dout = stack_heads(dout_ref, block, group, 0, DV)
            wide = (SCALE * a) * dout.astype(F32)
            pulled = jnp.concatenate(
                [mm(head(keys, h), dstate_ref[group * STACK + h]) for h in range(STACK)], axis=0
            )
            d_cor = mm(scores, dout, ((0,), (0,))) + d * pulled
            d_right = mm(inv_ref[block, group], d_cor, ((0,), (0,)))
            d_seen = (-a * beta) * d_right
            for h in range(STACK):
                n = group * STACK + h
                left = jnp.concatenate([head(keys, h), head(queries, h)], axis=0)
                right = jnp.concatenate([head(d_seen, h), head(wide, h)], axis=0)
                dstate_ref[n] = kappa[h * BLOCK : h * BLOCK + 1] * dstate_ref[n] + mm(
                    left, right, ((0,), (0,))
                )


def back_kernel(
    n_ref,
    inv_ref,
    col_ref,
    row_ref,
    dout_ref,
    cor_ref,
    states_ref,
    start_ref,
    dn_ref,
    gcol_ref,
    grow_ref,
    dstate,
):
    length = n_ref.shape[0]
    blocks = length // BLOCK
    dstate[...] = start_ref[...].astype(F32)

    @pl.loop(0, blocks)
    def _(step):
        block = blocks - 1 - step
        for group in range(H // STACK):
            cum, beta, a, d, kappa, doc = columns(col_ref, block, group)
            queries = stack_heads(n_ref, block, group, 0, DK)
            keys = stack_heads(n_ref, block, group, H * DK, DK)
            values = stack_heads(n_ref, block, group, 2 * H * DK, DV).astype(F32)
            within, strict = decay_matrix(cum, doc, row_ref, block, group)
            scores = SCALE * mm(queries, keys, ((1,), (1,))) * within
            weighted = mm(keys, keys, ((1,), (1,))) * strict
            dout = stack_heads(dout_ref, block, group, 0, DV)
            dout_wide = dout.astype(F32)
            corrected = cor_ref[block, group]
            cor_wide = corrected.astype(F32)
            wide = (SCALE * a) * dout_wide
            pulled, seen, asked, dk_state, d_kappa = [], [], [], [], []
            update = (d * cor_wide).astype(BF16)
            for h in range(STACK):
                n = group * STACK + h
                state = states_ref[block, n]
                after = dstate[n]
                after_low = after.astype(BF16)
                both = mm(jnp.concatenate([head(keys, h), head(queries, h)], axis=0), state)
                seen.append(both[:BLOCK])
                asked.append(both[BLOCK:])
                pulled.append(mm(head(keys, h), after_low))
                dk_state.append(mm(head(update, h), after_low, ((1,), (1,))))
                total = jnp.sum(
                    jnp.sum(state.astype(F32) * after, axis=0, keepdims=True),
                    axis=1,
                    keepdims=True,
                )
                d_kappa.append(jnp.broadcast_to(total * (1.0 / BLOCK), (BLOCK, 1)))
            pulled, seen, asked, d_kappa = (
                jnp.concatenate(p, axis=0) for p in (pulled, seen, asked, d_kappa)
            )
            d_cor = mm(scores, dout, ((0,), (0,))) + d * pulled
            d_right = mm(inv_ref[block, group], d_cor, ((0,), (0,)))
            scaled = beta * d_right
            d_seen = -a * scaled
            dk_left, dq_left = [], []
            for h in range(STACK):
                n = group * STACK + h
                left = jnp.concatenate([head(keys, h), head(queries, h)], axis=0)
                right = jnp.concatenate([head(d_seen, h), head(wide, h)], axis=0).astype(BF16)
                both = mm(right, states_ref[block, n], ((1,), (1,)))
                dk_left.append(both[:BLOCK])
                dq_left.append(both[BLOCK:])
                dstate[n] = kappa[h * BLOCK : h * BLOCK + 1] * dstate[n] + mm(
                    left, right, ((0,), (0,))
                )
            d_scores = mm(dout, corrected, ((1,), (1,)))
            d_system = -mm(d_right, corrected, ((1,), (1,)))
            to_rows = (SCALE * d_scores * within).astype(BF16)
            by_gram = d_system * weighted
            to_keys = (beta * d_system * strict).astype(BF16)
            dq = jnp.concatenate(dq_left, axis=0) + mm(to_rows, keys)
            dk = (
                jnp.concatenate(dk_left, axis=0)
                + jnp.concatenate(dk_state, axis=0)
                + mm(to_rows, queries, ((0,), (0,)))
                + mm(to_keys, keys)
                + mm(to_keys, keys, ((0,), (0,)))
            )
            store_heads(dn_ref, block, group, 0, DK, dq)
            store_heads(dn_ref, block, group, H * DK, DK, dk)
            store_heads(dn_ref, block, group, 2 * H * DK, DV, scaled)
            spread = d_scores * scores + beta * by_gram
            d_cum = jnp.sum(spread, axis=1, keepdims=True)
            d_beta = jnp.sum(by_gram, axis=1, keepdims=True) + jnp.sum(
                d_right * (values - a * seen), axis=1, keepdims=True
            )
            d_a = jnp.sum(SCALE * dout_wide * asked - scaled * seen, axis=1, keepdims=True)
            d_d = jnp.sum(cor_wide * pulled, axis=1, keepdims=True)
            lane = lax.broadcasted_iota(jnp.int32, (ROWS, 8), 1)
            packed = jnp.zeros((ROWS, 8), F32)
            for i, part in enumerate((d_cum, d_beta, d_a, d_d, d_kappa)):
                packed = jnp.where(lane == i, part, packed)
            gcol_ref[block, group] = packed
            grow_ref[block, group] = jnp.broadcast_to(
                -jnp.sum(spread, axis=0, keepdims=True), (8, ROWS)
            )


def conv_back_kernel(x_ref, cw_ref, mask_ref, dn_ref, dx_ref, dcw_ref):
    length = dn_ref.shape[0]

    def chunk(c, normalise):
        lanes = pl.ds(pl.multiple_of(c * 128, 128), 128)
        masks = conv_masks(mask_ref, length)
        weights = cw_ref[:, lanes]
        taps, z = conv_taps(x_ref[:, lanes].astype(F32), masks, weights)
        gate = jax.nn.sigmoid(z)
        dn = dn_ref[:, lanes]
        if normalise:
            y = z * gate
            r = lax.rsqrt(jnp.sum(y * y, axis=1, keepdims=True) + EPSILON)
            dn = r * dn - y * (r * r * r * jnp.sum(y * dn, axis=1, keepdims=True))
        dz = dn * gate * (1.0 + z * (1.0 - gate))
        edge = jnp.zeros((HALO, 128), F32)
        dx = jnp.concatenate([edge, dz * weights[0:1]], axis=0)
        sums = [jnp.sum(dz * taps[0], axis=0, keepdims=True)]
        for s in range(1, CONV):
            sums.append(jnp.sum(dz * taps[s], axis=0, keepdims=True))
            moved = jnp.concatenate([edge, dz * masks[s - 1] * weights[s : s + 1]], axis=0)
            dx = dx + pltpu.roll(moved, length + HALO - s, 0)
        dx_ref[:, lanes] = dx.astype(BF16)
        dcw_ref[:, lanes] = jnp.concatenate(sums, axis=0)

    qk_cols = 2 * H * DK

    @pl.loop(0, qk_cols // 128)
    def _(c):
        chunk(c, True)

    @pl.loop(qk_cols // 128, x_ref.shape[1] // 128)
    def _(c):
        chunk(c, False)


def call(kernel, outs, scratch, *args, micros):
    return pl.pallas_call(
        kernel,
        out_shape=[jax.ShapeDtypeStruct(s, t) for s, t in outs],
        in_specs=[pl.BlockSpec(memory_space=pltpu.VMEM)] * len(args),
        out_specs=[pl.BlockSpec(memory_space=pltpu.VMEM)] * len(outs),
        scratch_shapes=scratch,
        compiler_params=pltpu.CompilerParams(vmem_limit_bytes=VMEM_BYTES),
        cost_estimate=pl.CostEstimate(
            flops=int(micros * 1e9), bytes_accessed=4 * 2**20, transcendentals=0
        ),
    )(*args)


def mixer(x, weights, rates, decay, doc_all, member, sp_size, points):
    length = x.shape[0] - HALO
    blocks = length // BLOCK
    groups = H // STACK
    channels = x.shape[1]
    padded = jnp.concatenate([jnp.full((HALO,), -1, jnp.int32), doc_all])
    near = lax.dynamic_slice_in_dim(padded, member * length, length + HALO, 0)
    docs = near[HALO:]
    masks = jnp.stack(
        [(near[HALO - s : HALO - s + length] == docs).astype(F32) for s in range(1, CONV)]
        + [jnp.zeros((length,), F32)] * (8 - CONV + 1),
        axis=1,
    )
    doc_blocks = docs.reshape(blocks, 1, BLOCK)
    before = jnp.concatenate([near[HALO - 1 : HALO], doc_blocks[:-1, 0, -1]]).reshape(
        blocks, 1, 1
    )
    last = doc_blocks[:, :, -1:]
    from_before = (doc_blocks == before).astype(F32)
    to_last = (doc_blocks == last).astype(F32)
    kept = (last == before).astype(F32)

    def small(rates, decay):
        by_block = jnp.transpose(rates.reshape(blocks, BLOCK, H, 2), (3, 0, 2, 1))
        beta = jax.nn.sigmoid(by_block[1])
        offset = decay[1].reshape(1, H, 1)
        log_decay = -jnp.exp(decay[0]).reshape(1, H, 1) * jax.nn.softplus(by_block[0] + offset)
        i = lax.broadcasted_iota(jnp.int32, (BLOCK, BLOCK), 0)
        j = lax.broadcasted_iota(jnp.int32, (BLOCK, BLOCK), 1)
        upper = (i <= j).astype(F32)
        cum = jnp.einsum("bhi,ij->bhj", log_decay, upper, precision=lax.Precision.HIGHEST)
        final = cum[:, :, -1:]
        a = jnp.exp(cum) * from_before
        d = jnp.exp(final - cum) * to_last
        kappa = jnp.broadcast_to(jnp.exp(final) * kept, cum.shape)
        return jnp.stack([cum, beta, a, d, kappa], axis=0)

    five, pull_small = jax.vjp(small, rates, decay)
    doc_row = jnp.broadcast_to(doc_blocks.astype(F32), (blocks, H, BLOCK))
    packed = jnp.concatenate([five, doc_row[None], jnp.zeros((2,) + doc_row.shape, F32)], axis=0)
    packed = packed.reshape(8, blocks, groups, ROWS)
    col = jnp.transpose(packed, (1, 2, 3, 0))
    row = jnp.transpose(jnp.stack([packed[0], packed[5]] + [packed[6]] * 6), (1, 2, 0, 3))

    n_shape = ((length, channels), BF16)
    inv_shape = ((blocks, groups, ROWS, ROWS), F32)
    state_shape = ((H, DK, DV), F32)
    cor_shape = ((blocks, groups, ROWS, ROWS), BF16)
    (n,) = call(conv_kernel, [n_shape], [], x, weights, masks, micros=5)
    n = points("inverse", n)
    (inv,) = call(inverse_kernel, [inv_shape], [], n, col, row, micros=10)
    inv = points("state", inv)
    start = jnp.zeros((H, DK, DV), BF16)
    ahead = [(i, i + 1) for i in range(sp_size - 1)]
    behind = [(i + 1, i) for i in range(sp_size - 1)]
    for _ in range(sp_size - 1):
        (state,) = call(state_kernel, [state_shape], [], n, inv, col, start, micros=4)
        start = lax.ppermute(state.astype(BF16), "sp", ahead)
    mixed, cor, states = call(
        scan_kernel,
        [((length, H * DV), BF16), cor_shape, ((blocks, H, DK, DV), BF16)],
        [pltpu.VMEM((H, DK, DV), F32)],
        n,
        inv,
        col,
        row,
        start,
        micros=4,
    )

    def pull(dout):
        dstart = jnp.zeros((H, DK, DV), BF16)
        for _ in range(sp_size - 1):
            (dstate,) = call(
                back_state_kernel, [state_shape], [], n, inv, col, row, dout, dstart, micros=4
            )
            dstart = lax.ppermute(dstate.astype(BF16), "sp", behind)
        dstart = points("back", dstart)
        dn, gcol, grow = call(
            back_kernel,
            [
                ((length, channels), F32),
                ((blocks, groups, ROWS, 8), F32),
                ((blocks, groups, 8, ROWS), F32),
            ],
            [pltpu.VMEM((H, DK, DV), F32)],
            n,
            inv,
            col,
            row,
            dout,
            cor,
            states,
            dstart,
            micros=10,
        )
        dn = points("conv_back", dn)
        dx, dcw = call(
            conv_back_kernel,
            [((length + HALO, channels), BF16), ((CONV, channels), F32)],
            [],
            x,
            weights,
            masks,
            dn,
            micros=4,
        )
        grads = jnp.transpose(gcol[..., :5], (3, 0, 1, 2))
        grads = grads.at[0].add(grow[:, :, 0])
        d_rates, d_decay = pull_small(grads.reshape(5, blocks, H, BLOCK))
        from_next = lax.ppermute(dx[:HALO], "sp", behind)
        return dx, from_next, dcw, d_rates, d_decay

    return mixed, pull


def rms_norm(values, scales):
    return values * lax.rsqrt(jnp.mean(values * values, axis=-1, keepdims=True) + EPSILON) * scales


def output_gate(mixed, gate_raw, scales):
    length = mixed.shape[0]
    normed = rms_norm(mixed.reshape(length, H, DV), scales)
    return (normed * jax.nn.silu(gate_raw).reshape(length, H, DV)).reshape(length, H * DV)


def residual_norm(values, attended, scales):
    hidden = values + attended
    return (hidden, rms_norm(hidden, scales))


def after(value, *earlier):
    return lax.optimization_barrier((value,) + earlier)[0]


def swap(value, axis):
    return lax.ppermute(value, axis, [(0, 1), (1, 0)])


def other(first):
    return "sp" if first == "x" else "x"


def pair(axis, mine, theirs, dim):
    first = lax.axis_index(axis) == 0
    return jnp.where(
        first,
        jnp.concatenate([mine, theirs], axis=dim),
        jnp.concatenate([theirs, mine], axis=dim),
    )


def relative_axes(first):
    return ("core", first, other(first))


def place(first, k):
    total = 0
    for shift, axis in zip((2, 1, 0), relative_axes(first)):
        bit = lax.axis_index(axis)
        total = total + (1 << shift) * (1 - bit if (k >> shift) & 1 else bit)
    return total


def reorder(value, first):
    width = value.shape[1] // 8
    return jnp.concatenate(
        [lax.dynamic_slice_in_dim(value, place(first, i) * width, width, 1) for i in range(8)],
        axis=1,
    )


def shifted(value, step):
    count = lax.axis_size("fsdp")
    return lax.ppermute(value, "fsdp", [(i, (i + step) % count) for i in range(count)])


def gather_blocks(piece):
    count, rows = lax.axis_size("fsdp"), piece.shape[0]
    parts = [piece] + [shifted(piece, s) for s in range(1, count)]
    line = jnp.concatenate([parts[(count - 1 - i) % count] for i in range(2 * count - 1)], axis=0)
    start = (count - 1 - lax.axis_index("fsdp")) * rows
    return lax.dynamic_slice_in_dim(line, start, count * rows, 0)


def sum_blocks(value):
    count = lax.axis_size("fsdp")
    rows = value.shape[0] // count
    index = lax.axis_index("fsdp")

    def block(s):
        return lax.dynamic_slice_in_dim(value, lax.rem(index + s, count) * rows, rows, 0)

    total = block(0)
    for s in range(1, count):
        total = total + shifted(block(s).astype(BF16), s).astype(F32)
    if lax.axis_size("hi") > 1:
        total = lax.psum(total, "hi")
    return total


class ColumnGather:
    def __init__(self, shard, first):
        width = shard.shape[1] // 8
        self.first = first
        self.piece = lax.dynamic_slice_in_dim(shard, place(first, 0) * width, width, 1)

    def blocks(self, *earlier):
        self.held = gather_blocks(after(self.piece, *earlier) if earlier else self.piece)
        return self.held

    def second(self, *earlier):
        held = after(self.held, *earlier) if earlier else self.held
        self.held = jnp.concatenate([held, swap(held, other(self.first))], axis=1)
        return self.held

    def third(self, *earlier):
        held = after(self.held, *earlier) if earlier else self.held
        self.held = jnp.concatenate([held, swap(held, self.first)], axis=1)
        return self.held

    def full(self):
        return self.held, swap(self.held, "core")


class HalfGather(ColumnGather):
    def __init__(self, shard):
        rows, width = shard.shape[0] // 2, shard.shape[1] // 4
        column = (2 * lax.axis_index("core") + lax.axis_index("x")) * width
        self.first = "x"
        self.piece = lax.dynamic_slice(
            shard, (lax.axis_index("sp") * rows, column), (rows, width)
        )

    def second(self, *earlier):
        held = after(self.held, *earlier) if earlier else self.held
        self.held = jnp.concatenate([held, swap(held, "sp")], axis=0)
        return self.held


def dot_columns(values, halves_of):
    parts = [jnp.dot(values, w, preferred_element_type=F32) for w in halves_of]
    return jnp.concatenate(parts, axis=1)


def dot_back(grads, halves_of):
    half = grads.shape[1] // 2
    return jnp.einsum(
        "tf,df->td", grads[:, :half], halves_of[0], preferred_element_type=F32
    ) + jnp.einsum("tf,df->td", grads[:, half:], halves_of[1], preferred_element_type=F32)


def grad_dot(left, right):
    return jnp.einsum("td,tf->df", left, right, preferred_element_type=F32)


class ColumnSum:
    def __init__(self, left, right, first):
        self.left, self.right, self.first = left, right, first
        self.width = right.shape[1] // 8
        self.from_core = swap(grad_dot(left, right[:, 4 * self.width :]).astype(BF16), "core")

    def second(self):
        width = self.width
        outgoing = grad_dot(self.left, self.right[:, 2 * width : 4 * width])
        self.outgoing = (outgoing + self.from_core[:, 2 * width :].astype(F32)).astype(BF16)
        self.from_first = swap(self.outgoing, self.first)
        return self.outgoing

    def third(self):
        width = self.width
        self.outgoing = (
            grad_dot(self.left, self.right[:, width : 2 * width])
            + self.from_core[:, width : 2 * width].astype(F32)
            + self.from_first[:, width:].astype(F32)
        ).astype(BF16)
        self.from_second = swap(self.outgoing, other(self.first))
        return self.outgoing

    def own(self):
        width = self.width
        return (
            grad_dot(self.left, self.right[:, :width])
            + self.from_core[:, :width].astype(F32)
            + self.from_first[:, :width].astype(F32)
            + self.from_second.astype(F32)
        )

    def finish(self):
        total = sum_blocks(self.own()).astype(BF16)
        for axis in (other(self.first), self.first, "core"):
            total = pair(axis, total, swap(total, axis), 1)
        return total.astype(F32)


def by_half(values):
    blocks = values.reshape(values.shape[0], lax.axis_size("fsdp"), 2, -1)
    low = blocks[:, :, 0].reshape(values.shape[0], -1)
    high = blocks[:, :, 1].reshape(values.shape[0], -1)
    first = lax.axis_index("sp") == 0
    return jnp.concatenate(
        [jnp.where(first, low, high), jnp.where(first, high, low)], axis=1
    )


def from_half(values):
    half = values.shape[1] // 2
    first = lax.axis_index("sp") == 0
    low = jnp.where(first, values[:, :half], values[:, half:])
    high = jnp.where(first, values[:, half:], values[:, :half])
    shape = (values.shape[0], lax.axis_size("fsdp"), 1, half // lax.axis_size("fsdp"))
    return jnp.concatenate([low.reshape(shape), high.reshape(shape)], axis=2).reshape(
        values.shape
    )


class HalfSum:
    def __init__(self, left, near_core, far_core):
        self.left, self.near = left, near_core
        self.width = near_core.shape[1] // 2
        self.rows = left.shape[1] // 2
        self.from_core = swap(grad_dot(left, far_core).astype(BF16), "core")

    def second(self):
        width = self.width
        outgoing = grad_dot(self.left, self.near[:, width:])
        self.outgoing = (outgoing + self.from_core[:, width:].astype(F32)).astype(BF16)
        self.from_x = swap(self.outgoing, "x")
        return self.outgoing

    def third(self):
        rows, width = self.rows, self.width
        self.outgoing = (
            grad_dot(self.left[:, rows:], self.near[:, :width])
            + self.from_core[rows:, :width].astype(F32)
            + self.from_x[rows:].astype(F32)
        ).astype(BF16)
        self.from_y = swap(self.outgoing, "sp")
        return self.outgoing

    def finish(self):
        rows, width = self.rows, self.width
        own = (
            grad_dot(self.left[:, :rows], self.near[:, :width])
            + self.from_core[:rows, :width].astype(F32)
            + self.from_x[:rows].astype(F32)
            + self.from_y.astype(F32)
        )
        total = sum_blocks(own).astype(BF16)
        for axis, dim in (("sp", 0), ("x", 1), ("core", 1)):
            total = pair(axis, total, swap(total, axis), dim)
        return total.astype(F32)


def gather_small(parts):
    flat = jnp.concatenate([p.reshape(-1) for p in parts])
    size = flat.shape[0]
    flat = jnp.pad(flat, (0, -size % 1024)).reshape(-1, 128)
    every = gather_blocks(flat).reshape(lax.axis_size("fsdp"), -1)
    out, start = [], 0
    for p in parts:
        out.append(every[:, start : start + p.size].reshape((-1,) + p.shape))
        start += p.size
    return out


def sum_small(parts):
    flat = jnp.concatenate([p.reshape(-1) for p in parts])
    size = flat.shape[0]
    flat = jnp.pad(flat, (0, -size % 1024)).reshape(-1, 128)
    for axis in ("core", "x", "sp"):
        flat = flat + swap(flat, axis)
    members = lax.axis_size("fsdp")
    for bit in range(members.bit_length() - 1):
        flat = flat + lax.ppermute(flat, "fsdp", [(i, i ^ (1 << bit)) for i in range(members)])
    if lax.axis_size("hi") > 1:
        flat = lax.psum(flat, "hi")
    total = flat.reshape(-1)
    out, start = [], 0
    for p in parts:
        out.append(total[start : start + p.size].reshape(p.shape))
        start += p.size
    return out


def own_part(value, axis):
    size = value.shape[axis] // lax.axis_size("fsdp")
    return lax.dynamic_slice_in_dim(value, lax.axis_index("fsdp") * size, size, axis)


def body(
    tokens,
    cotangent,
    doc_lengths,
    input_weight,
    rate_weight,
    conv_weight,
    head_decay,
    mixer_gain,
    heads_gain,
    output_weight,
    feed_gain,
    up_weight,
    down_weight,
):
    length = tokens.shape[0]
    sp_size = lax.axis_size("sp")
    member = lax.axis_index("sp")
    qkv_cols = H * (2 * DK + DV)
    rate_all, conv_all, decay_all, mixer_all, heads_all, feed_all = gather_small(
        (rate_weight, conv_weight, head_decay, mixer_gain, heads_gain, feed_gain)
    )
    rate_full = rate_all.reshape(-1, 2 * H)
    conv_full = jnp.swapaxes(conv_all, 0, 1).reshape(CONV, -1).astype(F32)
    decay_full = jnp.swapaxes(decay_all, 0, 1).reshape(2, H).astype(F32)
    mixer_scale = mixer_all.reshape(-1).astype(F32)
    heads_scale = heads_all.reshape(-1).astype(F32)
    feed_scale = feed_all.reshape(-1).astype(F32)
    qk_cols = 2 * H * DK
    qk_way = ColumnGather(input_weight[:, :qk_cols], "x")
    v_way = ColumnGather(input_weight[:, qk_cols:qkv_cols], "sp")
    gate_way = ColumnGather(input_weight[:, qkv_cols:], "sp")
    out_way = ColumnGather(output_weight, "sp")
    up_way = HalfGather(up_weight)
    down_way = ColumnGather(down_weight, "sp")
    qkv_blocks = (qk_way.blocks(), v_way.blocks())
    qkv_second = (qk_way.second(), v_way.second())
    gate_way.blocks(*qkv_blocks)
    out_way.blocks(*qkv_blocks)
    qkv_third = (qk_way.third(), v_way.third())
    up_way.blocks(*qkv_second)
    down_way.blocks(*qkv_second)
    early = (gate_way.second(*qkv_third), out_way.second(*qkv_third))
    qk_full, v_full = qk_way.full(), v_way.full()

    def points(name, value):
        if name == "inverse":
            return after(value, up_way.second(*early), down_way.second(*early))
        if name == "state":
            late = (gate_way.third(*early), out_way.third(*early))
            up_way.third(*late)
            down_way.third(*late)
            return after(value, *late)
        if name == "back":
            return after(value, sums["down"].third())
        if name == "conv_back":
            return after(value, *(sums[key].third() for key in ("up", "out", "gate")))

    sums = {}

    ends = jnp.cumsum(doc_lengths[0])
    positions = lax.broadcasted_iota(jnp.int32, (length * sp_size, 1), 0)
    doc_ids = jnp.sum((positions >= ends[None, :]).astype(jnp.int32), axis=1)

    ahead = [(i, i + 1) for i in range(sp_size - 1)]
    halo = lax.ppermute(tokens[-HALO:], "sp", ahead)
    x_float = tokens.astype(F32)
    normed, pull_norm = jax.vjp(rms_norm, x_float, mixer_scale)
    normed_low = normed.astype(BF16)
    halo_low = rms_norm(halo.astype(F32), mixer_scale).astype(BF16)
    normed_more = jnp.concatenate([halo_low, normed_low], axis=0)
    qkv = jnp.concatenate(
        [
            reorder(dot_columns(normed_more, qk_full).astype(BF16), "x"),
            reorder(dot_columns(normed_more, v_full).astype(BF16), "sp"),
        ],
        axis=1,
    )
    rate_raw = jnp.dot(normed_low, rate_full, preferred_element_type=F32)
    rates = rate_raw.astype(BF16).astype(F32).reshape(length, H, 2)
    mixed, pull_mix = mixer(after(qkv, *early), conv_full, rates, decay_full, doc_ids, member, sp_size, points)
    gate_full, out_full = gate_way.full(), out_way.full()
    up_full, down_full = up_way.full(), down_way.full()
    gate_raw = reorder(dot_columns(normed_low, gate_full), "sp")
    gated, pull_gate = jax.vjp(output_gate, mixed.astype(F32), gate_raw, heads_scale)
    gated_low = gated.astype(BF16)
    attended = reorder(dot_columns(gated_low, out_full), "sp")
    (hidden, normed_two), pull_resid = jax.vjp(residual_norm, x_float, attended, feed_scale)
    two_low = by_half(normed_two.astype(BF16))
    core_first = lax.axis_index("core") == 0
    own_side, far_side = (jnp.dot(two_low, w, preferred_element_type=F32) for w in up_full)

    def feed_act(own_side, far_side):
        gate = jnp.where(core_first, own_side, far_side)
        return jax.nn.silu(gate) * jnp.where(core_first, far_side, own_side)

    activated, pull_act = jax.vjp(feed_act, own_side, far_side)

    def turn(values):
        half = values.shape[1] // 2
        return pair("x", values[:, :half], values[:, half:], 1)

    act_low = turn(activated.astype(BF16))
    block_out = (hidden + reorder(dot_columns(act_low, down_full), "sp")).astype(BF16)
    cot_rel = reorder(cotangent, "sp")
    sums["down"] = ColumnSum(act_low, cot_rel, "sp")
    d_act = turn(dot_back(cot_rel, down_full))
    d_own, d_far = (d.astype(BF16) for d in pull_act(d_act))
    sums["up"] = HalfSum(two_low, d_own, d_far)
    d_both = after(jnp.concatenate([d_own, d_far], axis=1), sums["down"].second())
    d_two = from_half(dot_back(d_both, up_full))
    d_resid, d_attended, feed_grad = pull_resid((cotangent.astype(F32), d_two))
    d_att_rel = reorder(d_attended.astype(BF16), "sp")
    sums["out"] = ColumnSum(gated_low, d_att_rel, "sp")
    d_gated = dot_back(d_att_rel, out_full)
    d_mixed, d_gate, heads_grad = pull_gate(d_gated)
    d_gate_low = d_gate.astype(BF16)
    d_gate_rel = reorder(d_gate_low, "sp")
    sums["gate"] = ColumnSum(normed_low, d_gate_rel, "sp")
    d_mixed_low = after(
        d_mixed.astype(BF16), *(sums[key].second() for key in ("up", "out", "gate"))
    )
    d_more, from_next, conv_grad, d_rates, decay_grad = pull_mix(d_mixed_low)
    edge = jnp.pad(from_next.astype(F32), ((length - HALO, 0), (0, 0)))
    d_qkv = (d_more[HALO:].astype(F32) + edge).astype(BF16)
    d_rate_low = d_rates.reshape(length, 2 * H).astype(BF16)
    d_qk_rel = reorder(d_qkv[:, :qk_cols], "x")
    d_v_rel = reorder(d_qkv[:, qk_cols:], "sp")
    sums["qk"] = ColumnSum(normed_low, d_qk_rel, "x")
    sums["v"] = ColumnSum(normed_low, d_v_rel, "sp")
    for step in ("second", "third"):
        for key in ("qk", "v"):
            getattr(sums[key], step)()
    down_shard, up_shard, output_shard, gate_shard, qk_shard, v_shard = (
        sums[key].finish() for key in ("down", "up", "out", "gate", "qk", "v")
    )
    rate_grad = jnp.einsum("td,tf->df", normed_low, d_rate_low, preferred_element_type=F32)
    d_normed = dot_back(d_qk_rel, qk_full) + dot_back(d_v_rel, v_full)
    d_normed = d_normed + dot_back(d_gate_rel, gate_full)
    d_normed = d_normed + jnp.einsum(
        "tf,df->td", d_rate_low, rate_full, preferred_element_type=F32
    )
    d_front, mixer_grad = pull_norm(d_normed)
    tokens_grad = (d_resid + d_front).astype(BF16)
    rate_sum, conv_sum, decay_sum, mixer_sum, heads_sum, feed_sum = sum_small(
        (rate_grad, conv_grad, decay_grad, mixer_grad, heads_grad, feed_grad)
    )
    return (
        block_out,
        tokens_grad,
        jnp.concatenate([qk_shard, v_shard, gate_shard], axis=1),
        own_part(rate_sum, 0),
        own_part(conv_sum, 1),
        own_part(decay_sum, 1),
        own_part(mixer_sum, 0),
        own_part(heads_sum, 0),
        output_shard,
        own_part(feed_sum, 0),
        up_shard,
        down_shard,
    )


def solution(mesh):
    dp, fsdp, sp = (mesh.shape[axis] for axis in ("dp", "fsdp", "sp"))
    dp_axes = ("hi", "x", "core")
    cut = jax.sharding.Mesh(
        mesh.devices.reshape(dp // 4, 2, 2, fsdp, sp), dp_axes + ("fsdp", "sp")
    )
    rows = P(dp_axes + ("fsdp", "sp"), None)
    split = P("fsdp", None)
    return jax.shard_map(
        body,
        mesh=cut,
        in_specs=(
            rows,
            rows,
            P(dp_axes + ("fsdp",), None),
            split,
            split,
            P(None, "fsdp"),
            P(None, "fsdp"),
            P("fsdp"),
            P("fsdp"),
            split,
            P("fsdp"),
            split,
            split,
        ),
        out_specs=(
            rows,
            rows,
            split,
            split,
            P(None, "fsdp"),
            P(None, "fsdp"),
            P("fsdp"),
            P("fsdp"),
            split,
            P("fsdp"),
            split,
            split,
        ),
        check_vma=False,
    )
```

```python
import jax
import jax.numpy as jnp
from jax import lax
from jax.experimental import pallas as pl
from jax.experimental.pallas import tpu as pltpu
from jax.sharding import PartitionSpec as P

H = 8
DK = 128
DV = 256
CONV = 4
BLOCK = 64
EPSILON = 1e-06
HALO = 16
STACK = 4
ROWS = STACK * BLOCK
SCALE = DK ** (-0.5)
VMEM_BYTES = 56 * 1024 * 1024
F32 = jnp.float32
BF16 = jnp.bfloat16


def mm(a, b, dims=((1,), (0,))):
    return lax.dot_general(
        a.astype(BF16), b.astype(BF16), (dims, ((), ())), preferred_element_type=F32
    )


def halves(a):
    high = a.astype(BF16)
    return high, (a - high.astype(F32)).astype(BF16)


def mm_fine(a, b):
    (ah, al), (bh, bl) = a, b
    return mm(ah, bh) + (mm(ah, bl) + mm(al, bh))


def stack_heads(ref, block, group, base, width):
    rows = pl.ds(pl.multiple_of(block * BLOCK, BLOCK), BLOCK)
    return jnp.concatenate(
        [
            ref[rows, base + (group * STACK + h) * width : base + (group * STACK + h + 1) * width]
            for h in range(STACK)
        ],
        axis=0,
    )


def store_heads(ref, block, group, base, width, value):
    rows = pl.ds(pl.multiple_of(block * BLOCK, BLOCK), BLOCK)
    for h in range(STACK):
        start = base + (group * STACK + h) * width
        ref[rows, start : start + width] = value[h * BLOCK : (h + 1) * BLOCK].astype(ref.dtype)


def head(value, h):
    return value[h * BLOCK : (h + 1) * BLOCK]


def columns(col_ref, block, group):
    packed = col_ref[block, group]
    return [packed[:, i : i + 1] for i in range(6)]


def decay_matrix(cum, doc, row_ref, block, group):
    rows = row_ref[block, group]
    i = lax.broadcasted_iota(jnp.int32, (ROWS, ROWS), 0)
    j = lax.broadcasted_iota(jnp.int32, (ROWS, ROWS), 1)
    inside = ((i // BLOCK) == (j // BLOCK)) & (i >= j) & (doc == rows[1:2])
    decay = jnp.exp(jnp.where(inside, cum - rows[0:1], -1e30))
    return decay, jnp.where(i > j, decay, 0.0)


def unit_inverses(lowers):
    i = lax.broadcasted_iota(jnp.int32, (ROWS, ROWS), 0)
    j = lax.broadcasted_iota(jnp.int32, (ROWS, ROWS), 1)
    apart = jnp.bitwise_xor(i, j)
    inverses = [
        jnp.where(i == j, 1.0, 0.0) - jnp.where(apart == 1, lower, 0.0) for lower in lowers
    ]
    size = 2
    while size < BLOCK:
        cross = (apart >= size) & (apart < 2 * size)
        parts = [halves(inverse) for inverse in inverses]
        right = [
            halves(mm_fine(halves(jnp.where(cross, lower, 0.0)), part))
            for lower, part in zip(lowers, parts)
        ]
        inverses = [
            inverse - mm_fine(part, r) for inverse, part, r in zip(inverses, parts, right)
        ]
        size *= 2
    return inverses


def conv_taps(x, masks, weights):
    taps = [x[HALO:]]
    for s in range(1, CONV):
        taps.append(pltpu.roll(x, s, 0)[HALO:] * masks[s - 1])
    z = taps[0] * weights[0:1]
    for s in range(1, CONV):
        z = z + taps[s] * weights[s : s + 1]
    return taps, z


def conv_masks(mask_ref, length):
    return [
        jnp.broadcast_to(mask_ref[:, s : s + 1], (length, 128)) for s in range(CONV - 1)
    ]


def conv_kernel(x_ref, cw_ref, mask_ref, n_ref):
    length = n_ref.shape[0]
    qk_cols = 2 * H * DK

    def chunk(c, normalise):
        lanes = pl.ds(pl.multiple_of(c * 128, 128), 128)
        masks = conv_masks(mask_ref, length)
        _, z = conv_taps(x_ref[:, lanes].astype(F32), masks, cw_ref[:, lanes])
        y = z * jax.nn.sigmoid(z)
        if normalise:
            y = y * lax.rsqrt(jnp.sum(y * y, axis=1, keepdims=True) + EPSILON)
        n_ref[:, lanes] = y.astype(BF16)

    @pl.loop(0, qk_cols // 128)
    def _(c):
        chunk(c, True)

    @pl.loop(qk_cols // 128, x_ref.shape[1] // 128)
    def _(c):
        chunk(c, False)


def inverse_kernel(n_ref, col_ref, row_ref, inv_ref):
    @pl.loop(0, n_ref.shape[0] // BLOCK)
    def _(block):
        lowers = []
        for group in range(H // STACK):
            cum, beta, _, _, _, doc = columns(col_ref, block, group)
            keys = stack_heads(n_ref, block, group, H * DK, DK)
            _, strict = decay_matrix(cum, doc, row_ref, block, group)
            lowers.append(beta * mm(keys, keys, ((1,), (1,))) * strict)
        for group, inverse in enumerate(unit_inverses(lowers)):
            inv_ref[block, group] = inverse


def state_steps(n_ref, inv_ref, col_ref, state_ref):
    @pl.loop(0, n_ref.shape[0] // BLOCK)
    def _(block):
        for group in range(H // STACK):
            _, beta, a, d, kappa, _ = columns(col_ref, block, group)
            keys = stack_heads(n_ref, block, group, H * DK, DK)
            values = stack_heads(n_ref, block, group, 2 * H * DK, DV).astype(F32)
            seen = jnp.concatenate(
                [mm(head(keys, h), state_ref[group * STACK + h]) for h in range(STACK)], axis=0
            )
            corrected = mm(inv_ref[block, group], beta * (values - a * seen))
            update = d * corrected
            for h in range(STACK):
                n = group * STACK + h
                state_ref[n] = kappa[h * BLOCK : h * BLOCK + 1] * state_ref[n] + mm(
                    head(keys, h), head(update, h), ((0,), (0,))
                )


def state_kernel(n_ref, inv_ref, col_ref, start_ref, state_ref):
    state_ref[...] = start_ref[...].astype(F32)
    state_steps(n_ref, inv_ref, col_ref, state_ref)


def scan_kernel(n_ref, inv_ref, col_ref, row_ref, start_ref, out_ref, cor_ref, states_ref, state):
    state[...] = start_ref[...].astype(F32)

    @pl.loop(0, n_ref.shape[0] // BLOCK)
    def _(block):
        for group in range(H // STACK):
            cum, beta, a, d, kappa, doc = columns(col_ref, block, group)
            queries = stack_heads(n_ref, block, group, 0, DK)
            keys = stack_heads(n_ref, block, group, H * DK, DK)
            values = stack_heads(n_ref, block, group, 2 * H * DK, DV).astype(F32)
            within, _ = decay_matrix(cum, doc, row_ref, block, group)
            scores = SCALE * mm(queries, keys, ((1,), (1,))) * within
            both = []
            for h in range(STACK):
                low = state[group * STACK + h].astype(BF16)
                states_ref[block, group * STACK + h] = low
                both.append(mm(jnp.concatenate([head(keys, h), head(queries, h)], axis=0), low))
            seen = jnp.concatenate([b[:BLOCK] for b in both], axis=0)
            asked = jnp.concatenate([b[BLOCK:] for b in both], axis=0)
            corrected = mm(inv_ref[block, group], beta * (values - a * seen))
            cor_ref[block, group] = corrected.astype(BF16)
            out = (SCALE * a) * asked + mm(scores, corrected)
            store_heads(out_ref, block, group, 0, DV, out)
            update = d * corrected
            for h in range(STACK):
                n = group * STACK + h
                state[n] = kappa[h * BLOCK : h * BLOCK + 1] * state[n] + mm(
                    head(keys, h), head(update, h), ((0,), (0,))
                )


def back_state_kernel(n_ref, inv_ref, col_ref, row_ref, dout_ref, start_ref, dstate_ref):
    blocks = n_ref.shape[0] // BLOCK
    dstate_ref[...] = start_ref[...].astype(F32)

    @pl.loop(0, blocks)
    def _(step):
        block = blocks - 1 - step
        for group in range(H // STACK):
            cum, beta, a, d, kappa, doc = columns(col_ref, block, group)
            queries = stack_heads(n_ref, block, group, 0, DK)
            keys = stack_heads(n_ref, block, group, H * DK, DK)
            within, _ = decay_matrix(cum, doc, row_ref, block, group)
            scores = SCALE * mm(queries, keys, ((1,), (1,))) * within
            dout = stack_heads(dout_ref, block, group, 0, DV)
            wide = (SCALE * a) * dout.astype(F32)
            pulled = jnp.concatenate(
                [mm(head(keys, h), dstate_ref[group * STACK + h]) for h in range(STACK)], axis=0
            )
            d_cor = mm(scores, dout, ((0,), (0,))) + d * pulled
            d_right = mm(inv_ref[block, group], d_cor, ((0,), (0,)))
            d_seen = (-a * beta) * d_right
            for h in range(STACK):
                n = group * STACK + h
                left = jnp.concatenate([head(keys, h), head(queries, h)], axis=0)
                right = jnp.concatenate([head(d_seen, h), head(wide, h)], axis=0)
                dstate_ref[n] = kappa[h * BLOCK : h * BLOCK + 1] * dstate_ref[n] + mm(
                    left, right, ((0,), (0,))
                )


def back_kernel(
    n_ref,
    inv_ref,
    col_ref,
    row_ref,
    dout_ref,
    cor_ref,
    states_ref,
    start_ref,
    dn_ref,
    gcol_ref,
    grow_ref,
    dstate,
):
    length = n_ref.shape[0]
    blocks = length // BLOCK
    dstate[...] = start_ref[...].astype(F32)

    @pl.loop(0, blocks)
    def _(step):
        block = blocks - 1 - step
        for group in range(H // STACK):
            cum, beta, a, d, kappa, doc = columns(col_ref, block, group)
            queries = stack_heads(n_ref, block, group, 0, DK)
            keys = stack_heads(n_ref, block, group, H * DK, DK)
            values = stack_heads(n_ref, block, group, 2 * H * DK, DV).astype(F32)
            within, strict = decay_matrix(cum, doc, row_ref, block, group)
            scores = SCALE * mm(queries, keys, ((1,), (1,))) * within
            weighted = mm(keys, keys, ((1,), (1,))) * strict
            dout = stack_heads(dout_ref, block, group, 0, DV)
            dout_wide = dout.astype(F32)
            corrected = cor_ref[block, group]
            cor_wide = corrected.astype(F32)
            wide = (SCALE * a) * dout_wide
            pulled, seen, asked, dk_state, d_kappa = [], [], [], [], []
            update = (d * cor_wide).astype(BF16)
            for h in range(STACK):
                n = group * STACK + h
                state = states_ref[block, n]
                after = dstate[n]
                after_low = after.astype(BF16)
                both = mm(jnp.concatenate([head(keys, h), head(queries, h)], axis=0), state)
                seen.append(both[:BLOCK])
                asked.append(both[BLOCK:])
                pulled.append(mm(head(keys, h), after_low))
                dk_state.append(mm(head(update, h), after_low, ((1,), (1,))))
                total = jnp.sum(
                    jnp.sum(state.astype(F32) * after, axis=0, keepdims=True),
                    axis=1,
                    keepdims=True,
                )
                d_kappa.append(jnp.broadcast_to(total * (1.0 / BLOCK), (BLOCK, 1)))
            pulled, seen, asked, d_kappa = (
                jnp.concatenate(p, axis=0) for p in (pulled, seen, asked, d_kappa)
            )
            d_cor = mm(scores, dout, ((0,), (0,))) + d * pulled
            d_right = mm(inv_ref[block, group], d_cor, ((0,), (0,)))
            scaled = beta * d_right
            d_seen = -a * scaled
            dk_left, dq_left = [], []
            for h in range(STACK):
                n = group * STACK + h
                left = jnp.concatenate([head(keys, h), head(queries, h)], axis=0)
                right = jnp.concatenate([head(d_seen, h), head(wide, h)], axis=0).astype(BF16)
                both = mm(right, states_ref[block, n], ((1,), (1,)))
                dk_left.append(both[:BLOCK])
                dq_left.append(both[BLOCK:])
                dstate[n] = kappa[h * BLOCK : h * BLOCK + 1] * dstate[n] + mm(
                    left, right, ((0,), (0,))
                )
            d_scores = mm(dout, corrected, ((1,), (1,)))
            d_system = -mm(d_right, corrected, ((1,), (1,)))
            to_rows = (SCALE * d_scores * within).astype(BF16)
            by_gram = d_system * weighted
            to_keys = (beta * d_system * strict).astype(BF16)
            dq = jnp.concatenate(dq_left, axis=0) + mm(to_rows, keys)
            dk = (
                jnp.concatenate(dk_left, axis=0)
                + jnp.concatenate(dk_state, axis=0)
                + mm(to_rows, queries, ((0,), (0,)))
                + mm(to_keys, keys)
                + mm(to_keys, keys, ((0,), (0,)))
            )
            store_heads(dn_ref, block, group, 0, DK, dq)
            store_heads(dn_ref, block, group, H * DK, DK, dk)
            store_heads(dn_ref, block, group, 2 * H * DK, DV, scaled)
            spread = d_scores * scores + beta * by_gram
            d_cum = jnp.sum(spread, axis=1, keepdims=True)
            d_beta = jnp.sum(by_gram, axis=1, keepdims=True) + jnp.sum(
                d_right * (values - a * seen), axis=1, keepdims=True
            )
            d_a = jnp.sum(SCALE * dout_wide * asked - scaled * seen, axis=1, keepdims=True)
            d_d = jnp.sum(cor_wide * pulled, axis=1, keepdims=True)
            lane = lax.broadcasted_iota(jnp.int32, (ROWS, 8), 1)
            packed = jnp.zeros((ROWS, 8), F32)
            for i, part in enumerate((d_cum, d_beta, d_a, d_d, d_kappa)):
                packed = jnp.where(lane == i, part, packed)
            gcol_ref[block, group] = packed
            grow_ref[block, group] = jnp.broadcast_to(
                -jnp.sum(spread, axis=0, keepdims=True), (8, ROWS)
            )


def conv_back_kernel(x_ref, cw_ref, mask_ref, dn_ref, dx_ref, dcw_ref):
    length = dn_ref.shape[0]

    def chunk(c, normalise):
        lanes = pl.ds(pl.multiple_of(c * 128, 128), 128)
        masks = conv_masks(mask_ref, length)
        weights = cw_ref[:, lanes]
        taps, z = conv_taps(x_ref[:, lanes].astype(F32), masks, weights)
        gate = jax.nn.sigmoid(z)
        dn = dn_ref[:, lanes]
        if normalise:
            y = z * gate
            r = lax.rsqrt(jnp.sum(y * y, axis=1, keepdims=True) + EPSILON)
            dn = r * dn - y * (r * r * r * jnp.sum(y * dn, axis=1, keepdims=True))
        dz = dn * gate * (1.0 + z * (1.0 - gate))
        edge = jnp.zeros((HALO, 128), F32)
        dx = jnp.concatenate([edge, dz * weights[0:1]], axis=0)
        sums = [jnp.sum(dz * taps[0], axis=0, keepdims=True)]
        for s in range(1, CONV):
            sums.append(jnp.sum(dz * taps[s], axis=0, keepdims=True))
            moved = jnp.concatenate([edge, dz * masks[s - 1] * weights[s : s + 1]], axis=0)
            dx = dx + pltpu.roll(moved, length + HALO - s, 0)
        dx_ref[:, lanes] = dx.astype(BF16)
        dcw_ref[:, lanes] = jnp.concatenate(sums, axis=0)

    qk_cols = 2 * H * DK

    @pl.loop(0, qk_cols // 128)
    def _(c):
        chunk(c, True)

    @pl.loop(qk_cols // 128, x_ref.shape[1] // 128)
    def _(c):
        chunk(c, False)


def call(kernel, outs, scratch, *args, micros):
    return pl.pallas_call(
        kernel,
        out_shape=[jax.ShapeDtypeStruct(s, t) for s, t in outs],
        in_specs=[pl.BlockSpec(memory_space=pltpu.VMEM)] * len(args),
        out_specs=[pl.BlockSpec(memory_space=pltpu.VMEM)] * len(outs),
        scratch_shapes=scratch,
        compiler_params=pltpu.CompilerParams(vmem_limit_bytes=VMEM_BYTES),
        cost_estimate=pl.CostEstimate(
            flops=int(micros * 1e9), bytes_accessed=4 * 2**20, transcendentals=0
        ),
    )(*args)


def mixer(x, weights, rates, decay, doc_all, member, sp_size, points):
    length = x.shape[0] - HALO
    blocks = length // BLOCK
    groups = H // STACK
    channels = x.shape[1]
    padded = jnp.concatenate([jnp.full((HALO,), -1, jnp.int32), doc_all])
    near = lax.dynamic_slice_in_dim(padded, member * length, length + HALO, 0)
    docs = near[HALO:]
    masks = jnp.stack(
        [(near[HALO - s : HALO - s + length] == docs).astype(F32) for s in range(1, CONV)]
        + [jnp.zeros((length,), F32)] * (8 - CONV + 1),
        axis=1,
    )
    doc_blocks = docs.reshape(blocks, 1, BLOCK)
    before = jnp.concatenate([near[HALO - 1 : HALO], doc_blocks[:-1, 0, -1]]).reshape(
        blocks, 1, 1
    )
    last = doc_blocks[:, :, -1:]
    from_before = (doc_blocks == before).astype(F32)
    to_last = (doc_blocks == last).astype(F32)
    kept = (last == before).astype(F32)

    def small(rates, decay):
        by_block = jnp.transpose(rates.reshape(blocks, BLOCK, H, 2), (3, 0, 2, 1))
        beta = jax.nn.sigmoid(by_block[1])
        offset = decay[1].reshape(1, H, 1)
        log_decay = -jnp.exp(decay[0]).reshape(1, H, 1) * jax.nn.softplus(by_block[0] + offset)
        i = lax.broadcasted_iota(jnp.int32, (BLOCK, BLOCK), 0)
        j = lax.broadcasted_iota(jnp.int32, (BLOCK, BLOCK), 1)
        upper = (i <= j).astype(F32)
        cum = jnp.einsum("bhi,ij->bhj", log_decay, upper, precision=lax.Precision.HIGHEST)
        final = cum[:, :, -1:]
        a = jnp.exp(cum) * from_before
        d = jnp.exp(final - cum) * to_last
        kappa = jnp.broadcast_to(jnp.exp(final) * kept, cum.shape)
        return jnp.stack([cum, beta, a, d, kappa], axis=0)

    five, pull_small = jax.vjp(small, rates, decay)
    doc_row = jnp.broadcast_to(doc_blocks.astype(F32), (blocks, H, BLOCK))
    packed = jnp.concatenate([five, doc_row[None], jnp.zeros((2,) + doc_row.shape, F32)], axis=0)
    packed = packed.reshape(8, blocks, groups, ROWS)
    col = jnp.transpose(packed, (1, 2, 3, 0))
    row = jnp.transpose(jnp.stack([packed[0], packed[5]] + [packed[6]] * 6), (1, 2, 0, 3))

    n_shape = ((length, channels), BF16)
    inv_shape = ((blocks, groups, ROWS, ROWS), F32)
    state_shape = ((H, DK, DV), F32)
    cor_shape = ((blocks, groups, ROWS, ROWS), BF16)
    (n,) = call(conv_kernel, [n_shape], [], x, weights, masks, micros=5)
    n = points("inverse", n)
    (inv,) = call(inverse_kernel, [inv_shape], [], n, col, row, micros=10)
    start = jnp.zeros((H, DK, DV), BF16)
    ahead = [(i, i + 1) for i in range(sp_size - 1)]
    behind = [(i + 1, i) for i in range(sp_size - 1)]
    for _ in range(sp_size - 1):
        (state,) = call(state_kernel, [state_shape], [], n, inv, col, start, micros=4)
        start = lax.ppermute(state.astype(BF16), "sp", ahead)
    start = points("scan", start)
    mixed, cor, states = call(
        scan_kernel,
        [((length, H * DV), BF16), cor_shape, ((blocks, H, DK, DV), BF16)],
        [pltpu.VMEM((H, DK, DV), F32)],
        n,
        inv,
        col,
        row,
        start,
        micros=4,
    )

    def pull(dout):
        dstart = jnp.zeros((H, DK, DV), BF16)
        for _ in range(sp_size - 1):
            (dstate,) = call(
                back_state_kernel, [state_shape], [], n, inv, col, row, dout, dstart, micros=4
            )
            dstart = lax.ppermute(dstate.astype(BF16), "sp", behind)
        dstart = points("back", dstart)
        dn, gcol, grow = call(
            back_kernel,
            [
                ((length, channels), F32),
                ((blocks, groups, ROWS, 8), F32),
                ((blocks, groups, 8, ROWS), F32),
            ],
            [pltpu.VMEM((H, DK, DV), F32)],
            n,
            inv,
            col,
            row,
            dout,
            cor,
            states,
            dstart,
            micros=10,
        )
        dn = points("conv_back", dn)
        dx, dcw = call(
            conv_back_kernel,
            [((length + HALO, channels), BF16), ((CONV, channels), F32)],
            [],
            x,
            weights,
            masks,
            dn,
            micros=4,
        )
        grads = jnp.transpose(gcol[..., :5], (3, 0, 1, 2))
        grads = grads.at[0].add(grow[:, :, 0])
        d_rates, d_decay = pull_small(grads.reshape(5, blocks, H, BLOCK))
        from_next = lax.ppermute(dx[:HALO], "sp", behind)
        return dx, from_next, dcw, d_rates, d_decay

    return mixed, pull


def rms_norm(values, scales):
    return values * lax.rsqrt(jnp.mean(values * values, axis=-1, keepdims=True) + EPSILON) * scales


def output_gate(mixed, gate_raw, scales):
    length = mixed.shape[0]
    normed = rms_norm(mixed.reshape(length, H, DV), scales)
    return (normed * jax.nn.silu(gate_raw).reshape(length, H, DV)).reshape(length, H * DV)


def residual_norm(values, attended, scales):
    hidden = values + attended
    return (hidden, rms_norm(hidden, scales))


def after(value, *earlier):
    return lax.optimization_barrier((value,) + earlier)[0]


def swap(value, axis):
    return lax.ppermute(value, axis, [(0, 1), (1, 0)])


def other(first):
    return "sp" if first == "x" else "x"


def pair(axis, mine, theirs, dim):
    first = lax.axis_index(axis) == 0
    return jnp.where(
        first,
        jnp.concatenate([mine, theirs], axis=dim),
        jnp.concatenate([theirs, mine], axis=dim),
    )


def relative_axes(first):
    return ("core", first, other(first))


def place(first, k):
    total = 0
    for shift, axis in zip((2, 1, 0), relative_axes(first)):
        bit = lax.axis_index(axis)
        total = total + (1 << shift) * (1 - bit if (k >> shift) & 1 else bit)
    return total


def reorder(value, first):
    width = value.shape[1] // 8
    return jnp.concatenate(
        [lax.dynamic_slice_in_dim(value, place(first, i) * width, width, 1) for i in range(8)],
        axis=1,
    )


def shifted(value, step):
    count = lax.axis_size("fsdp")
    return lax.ppermute(value, "fsdp", [(i, (i + step) % count) for i in range(count)])


def gather_blocks(piece):
    count, rows = lax.axis_size("fsdp"), piece.shape[0]
    parts = [piece] + [shifted(piece, s) for s in range(1, count)]
    line = jnp.concatenate([parts[(count - 1 - i) % count] for i in range(2 * count - 1)], axis=0)
    start = (count - 1 - lax.axis_index("fsdp")) * rows
    return lax.dynamic_slice_in_dim(line, start, count * rows, 0)


def sum_blocks(value):
    total = lax.psum_scatter(value.astype(BF16), "fsdp", scatter_dimension=0, tiled=True)
    if lax.axis_size("hi") > 1:
        total = lax.psum(total, "hi")
    return total


WEIGHT_AXES = ("fsdp", "hi", "x", "core", "sp")


def gather_rows(shard):
    count, own = 1, 0
    for axis in WEIGHT_AXES[1:]:
        count = count * lax.axis_size(axis)
        own = own * lax.axis_size(axis) + lax.axis_index(axis)
    rows = shard.shape[0] // count
    piece = lax.dynamic_slice_in_dim(shard, own * rows, rows, 0)
    return lax.all_gather(piece, WEIGHT_AXES, axis=0, tiled=True)


class ColumnGather:
    def __init__(self, shard, first):
        width = shard.shape[1] // 8
        self.first = first
        self.piece = lax.dynamic_slice_in_dim(shard, place(first, 0) * width, width, 1)

    def blocks(self, *earlier):
        self.held = gather_blocks(after(self.piece, *earlier) if earlier else self.piece)
        return self.held

    def second(self, *earlier):
        held = after(self.held, *earlier) if earlier else self.held
        self.held = jnp.concatenate([held, swap(held, other(self.first))], axis=1)
        return self.held

    def third(self, *earlier):
        held = after(self.held, *earlier) if earlier else self.held
        self.held = jnp.concatenate([held, swap(held, self.first)], axis=1)
        return self.held

    def full(self):
        return self.held, swap(self.held, "core")


def dot_columns(values, halves_of):
    parts = [jnp.dot(values, w, preferred_element_type=F32) for w in halves_of]
    return jnp.concatenate(parts, axis=1)


def dot_back(grads, halves_of):
    half = grads.shape[1] // 2
    return jnp.einsum(
        "tf,df->td", grads[:, :half], halves_of[0], preferred_element_type=F32
    ) + jnp.einsum("tf,df->td", grads[:, half:], halves_of[1], preferred_element_type=F32)


def grad_dot(left, right):
    return jnp.einsum("td,tf->df", left, right, preferred_element_type=F32)


class ColumnSum:
    def __init__(self, left, right, first):
        self.left, self.right, self.first = left, right, first
        self.width = right.shape[1] // 8
        self.from_core = swap(grad_dot(left, right[:, 4 * self.width :]).astype(BF16), "core")

    def second(self):
        width = self.width
        outgoing = grad_dot(self.left, self.right[:, 2 * width : 4 * width])
        self.outgoing = (outgoing + self.from_core[:, 2 * width :].astype(F32)).astype(BF16)
        self.from_first = swap(self.outgoing, self.first)
        return self.outgoing

    def third(self):
        width = self.width
        self.outgoing = (
            grad_dot(self.left, self.right[:, width : 2 * width])
            + self.from_core[:, width : 2 * width].astype(F32)
            + self.from_first[:, width:].astype(F32)
        ).astype(BF16)
        self.from_second = swap(self.outgoing, other(self.first))
        return self.outgoing

    def own(self):
        width = self.width
        return (
            grad_dot(self.left, self.right[:, :width])
            + self.from_core[:, :width].astype(F32)
            + self.from_first[:, :width].astype(F32)
            + self.from_second.astype(F32)
        )

    def block(self):
        return sum_blocks(self.own())

    def spread(self, every):
        ways = {"core": 0, "x": 1, "sp": 2}
        order = tuple(ways[axis] for axis in relative_axes(self.first))
        pieces = widen(jnp.transpose(every, order + (3, 4)), self.width)
        pieces = pieces.reshape((8,) + pieces.shape[3:])
        return jnp.swapaxes(pieces, 0, 1).reshape(pieces.shape[1], -1).astype(F32)


def finish(sums):
    blocks = [narrow(s.block()) for s in sums]
    held = jnp.concatenate(blocks, axis=0)[None]
    for axis in ("sp", "x", "core"):
        held = pair(axis, held, swap(held, axis), 0)
    held = held.reshape((2, 2, 2) + held.shape[1:])
    out, start = [], 0
    for s, block in zip(sums, blocks):
        out.append(s.spread(held[:, :, :, start : start + block.shape[0]]))
        start += block.shape[0]
    return out


def by_half(values):
    blocks = values.reshape(values.shape[0], lax.axis_size("fsdp"), 2, -1)
    low = blocks[:, :, 0].reshape(values.shape[0], -1)
    high = blocks[:, :, 1].reshape(values.shape[0], -1)
    first = lax.axis_index("sp") == 0
    return jnp.concatenate(
        [jnp.where(first, low, high), jnp.where(first, high, low)], axis=1
    )


class HalfSum:
    def __init__(self, left, right):
        self.left, self.first = left, "x"
        self.width = width = right.shape[1] // 4
        core, x = lax.axis_index("core"), lax.axis_index("x")

        def half(c):
            return jnp.concatenate(
                [
                    lax.dynamic_slice_in_dim(right, (2 * c + d) * width, width, 1)
                    for d in (x, 1 - x)
                ],
                axis=1,
            )

        self.near, far_core = half(core), half(1 - core)
        self.rows = left.shape[1] // 2
        self.from_core = swap(grad_dot(left, far_core).astype(BF16), "core")

    def second(self):
        width = self.width
        outgoing = grad_dot(self.left, self.near[:, width:])
        self.outgoing = (outgoing + self.from_core[:, width:].astype(F32)).astype(BF16)
        self.from_x = swap(self.outgoing, "x")
        return self.outgoing

    def third(self):
        rows, width = self.rows, self.width
        self.outgoing = (
            grad_dot(self.left[:, rows:], self.near[:, :width])
            + self.from_core[rows:, :width].astype(F32)
            + self.from_x[rows:].astype(F32)
        ).astype(BF16)
        self.from_y = swap(self.outgoing, "sp")
        return self.outgoing

    def block(self):
        rows, width = self.rows, self.width
        own = (
            grad_dot(self.left[:, :rows], self.near[:, :width])
            + self.from_core[:rows, :width].astype(F32)
            + self.from_x[:rows].astype(F32)
            + self.from_y.astype(F32)
        )
        return sum_blocks(own)

    def spread(self, every):
        pieces = widen(every, self.width)
        return (
            jnp.transpose(pieces, (2, 3, 0, 1, 4))
            .reshape(2 * pieces.shape[3], 4 * self.width)
            .astype(F32)
        )


def narrow(value):
    return jnp.concatenate(
        [value[:, i : i + 128] for i in range(0, value.shape[1], 128)], axis=0
    )


def widen(value, width):
    blocks = width // 128
    split = value.reshape(value.shape[:-2] + (blocks, value.shape[-2] // blocks, 128))
    return jnp.swapaxes(split, -3, -2).reshape(value.shape[:-2] + (-1, width))


def pack_small(parts, width):
    flat = jnp.concatenate([p.reshape(-1) for p in parts])
    return jnp.pad(flat, (0, -flat.shape[0] % (16 * width))).reshape(-1, width)


def unpack_small(every, parts):
    out, start = [], 0
    for p in parts:
        out.append(every[:, start : start + p.size].reshape((-1,) + p.shape))
        start += p.size
    return out


def sum_small(parts):
    flat = jnp.concatenate([p.reshape(-1) for p in parts])
    size = flat.shape[0]
    flat = jnp.pad(flat, (0, -size % 1024)).reshape(-1, 128)
    for axis in ("core", "x", "sp"):
        flat = flat + swap(flat, axis)
    members = lax.axis_size("fsdp")
    for bit in range(members.bit_length() - 1):
        flat = flat + lax.ppermute(flat, "fsdp", [(i, i ^ (1 << bit)) for i in range(members)])
    if lax.axis_size("hi") > 1:
        flat = lax.psum(flat, "hi")
    total = flat.reshape(-1)
    out, start = [], 0
    for p in parts:
        out.append(total[start : start + p.size].reshape(p.shape))
        start += p.size
    return out


def own_part(value, axis):
    size = value.shape[axis] // lax.axis_size("fsdp")
    return lax.dynamic_slice_in_dim(value, lax.axis_index("fsdp") * size, size, axis)


def body(
    tokens,
    cotangent,
    doc_lengths,
    input_weight,
    rate_weight,
    conv_weight,
    head_decay,
    mixer_gain,
    heads_gain,
    output_weight,
    feed_gain,
    up_weight,
    down_weight,
):
    length = tokens.shape[0]
    sp_size = lax.axis_size("sp")
    member = lax.axis_index("sp")
    qkv_cols = H * (2 * DK + DV)
    qk_cols = 2 * H * DK
    members = lax.axis_size("fsdp")
    qk_way = ColumnGather(input_weight[:, :qk_cols], "x")
    v_way = ColumnGather(input_weight[:, qk_cols:qkv_cols], "sp")
    gate_way = ColumnGather(input_weight[:, qkv_cols:], "x")
    down_way = ColumnGather(down_weight, "sp")
    pair_rows, pair_cols = qk_way.piece.shape[0], 2 * qk_way.piece.shape[1]
    smalls = (rate_weight, conv_weight, head_decay, mixer_gain, heads_gain, feed_gain)
    first_load = jnp.concatenate(
        [
            jnp.concatenate([qk_way.piece, v_way.piece], axis=1),
            pack_small(smalls, pair_cols),
        ],
        axis=0,
    )
    first_all = gather_blocks(first_load).reshape(members, -1, pair_cols)
    both = first_all[:, :pair_rows].reshape(-1, pair_cols)
    qk_way.held, v_way.held = both[:, : pair_cols // 2], both[:, pair_cols // 2 :]
    rate_all, conv_all, decay_all, mixer_all, heads_all, feed_all = unpack_small(
        first_all[:, pair_rows:].reshape(members, -1), smalls
    )
    qkv_second = (qk_way.second(), v_way.second())
    gate_rows = narrow(gate_way.piece).shape[0]
    second_load = after(
        jnp.concatenate([narrow(gate_way.piece), narrow(down_way.piece)], axis=0), both
    )
    second_all = gather_blocks(second_load).reshape(members, -1, 128)
    gate_way.held = widen(second_all[:, :gate_rows], gate_way.piece.shape[1]).reshape(
        -1, gate_way.piece.shape[1]
    )
    down_way.held = widen(second_all[:, gate_rows:], down_way.piece.shape[1]).reshape(
        -1, down_way.piece.shape[1]
    )
    qkv_third = (qk_way.third(), v_way.third())
    early = (gate_way.second(*qkv_third), down_way.second(*qkv_third))
    qk_full, v_full = qk_way.full(), v_way.full()
    out_full = gather_rows(output_weight)
    up_full = gather_rows(up_weight)
    rate_full = rate_all.reshape(-1, 2 * H)
    conv_full = jnp.swapaxes(conv_all, 0, 1).reshape(CONV, -1).astype(F32)
    decay_full = jnp.swapaxes(decay_all, 0, 1).reshape(2, H).astype(F32)
    mixer_scale = mixer_all.reshape(-1).astype(F32)
    heads_scale = heads_all.reshape(-1).astype(F32)
    feed_scale = feed_all.reshape(-1).astype(F32)

    def points(name, value):
        if name == "inverse":
            for way in (gate_way, down_way):
                way.third(value)
            return after(value, *early)
        if name == "scan":
            return after(value, gate_way.held, down_way.held)
        if name == "back":
            return after(value, sums["down"].third())
        if name == "conv_back":
            return after(value, *(sums[key].third() for key in ("up", "out", "gate")))
        return value

    sums = {}

    ends = jnp.cumsum(doc_lengths[0])
    positions = lax.broadcasted_iota(jnp.int32, (length * sp_size, 1), 0)
    doc_ids = jnp.sum((positions >= ends[None, :]).astype(jnp.int32), axis=1)

    ahead = [(i, i + 1) for i in range(sp_size - 1)]
    halo = lax.ppermute(tokens[-HALO:], "sp", ahead)
    x_float = tokens.astype(F32)
    normed, pull_norm = jax.vjp(rms_norm, x_float, mixer_scale)
    normed_low = normed.astype(BF16)
    halo_low = rms_norm(halo.astype(F32), mixer_scale).astype(BF16)
    normed_more = jnp.concatenate([halo_low, normed_low], axis=0)
    qkv = jnp.concatenate(
        [
            reorder(dot_columns(normed_more, qk_full).astype(BF16), "x"),
            reorder(dot_columns(normed_more, v_full).astype(BF16), "sp"),
        ],
        axis=1,
    )
    rate_raw = jnp.dot(normed_low, rate_full, preferred_element_type=F32)
    rates = rate_raw.astype(BF16).astype(F32).reshape(length, H, 2)
    mixed, pull_mix = mixer(qkv, conv_full, rates, decay_full, doc_ids, member, sp_size, points)
    gate_full, down_full = gate_way.full(), down_way.full()
    gate_raw = reorder(dot_columns(normed_low, gate_full), "x")
    gated, pull_gate = jax.vjp(output_gate, mixed.astype(F32), gate_raw, heads_scale)
    gated_low = gated.astype(BF16)
    attended = jnp.dot(gated_low, out_full, preferred_element_type=F32)
    (hidden, normed_two), pull_resid = jax.vjp(residual_norm, x_float, attended, feed_scale)
    two_low = normed_two.astype(BF16)
    gate_up = jnp.dot(two_low, up_full, preferred_element_type=F32)

    def feed_act(gate_up):
        half = gate_up.shape[1] // 2
        return jax.nn.silu(gate_up[:, :half]) * gate_up[:, half:]

    activated, pull_act = jax.vjp(feed_act, gate_up)
    act_low = activated.astype(BF16)
    block_out = (hidden + reorder(dot_columns(act_low, down_full), "sp")).astype(BF16)
    cot_rel = reorder(cotangent, "sp")
    sums["down"] = ColumnSum(act_low, cot_rel, "sp")
    d_act = dot_back(cot_rel, down_full)
    d_gu_low = pull_act(d_act)[0].astype(BF16)
    sums["up"] = HalfSum(by_half(two_low), d_gu_low)
    d_gu_low = after(d_gu_low, sums["down"].second())
    d_two = jnp.einsum("tf,df->td", d_gu_low, up_full, preferred_element_type=F32)
    d_resid, d_attended, feed_grad = pull_resid((cotangent.astype(F32), d_two))
    d_att_low = d_attended.astype(BF16)
    d_att_rel = reorder(d_att_low, "sp")
    sums["out"] = ColumnSum(gated_low, d_att_rel, "sp")
    d_gated = jnp.einsum("td,ed->te", d_att_low, out_full, preferred_element_type=F32)
    d_mixed, d_gate, heads_grad = pull_gate(d_gated)
    d_gate_low = d_gate.astype(BF16)
    d_gate_rel = reorder(d_gate_low, "x")
    sums["gate"] = ColumnSum(normed_low, d_gate_rel, "x")
    d_mixed_low = after(
        d_mixed.astype(BF16), *(sums[key].second() for key in ("up", "out", "gate"))
    )
    d_more, from_next, conv_grad, d_rates, decay_grad = pull_mix(d_mixed_low)
    edge = jnp.pad(from_next.astype(F32), ((length - HALO, 0), (0, 0)))
    d_qkv = (d_more[HALO:].astype(F32) + edge).astype(BF16)
    d_rate_low = d_rates.reshape(length, 2 * H).astype(BF16)
    d_qk_rel = reorder(d_qkv[:, :qk_cols], "x")
    d_v_rel = reorder(d_qkv[:, qk_cols:], "sp")
    sums["qk"] = ColumnSum(normed_low, d_qk_rel, "x")
    sums["v"] = ColumnSum(normed_low, d_v_rel, "sp")
    for step in ("second", "third"):
        for key in ("qk", "v"):
            getattr(sums[key], step)()
    down_shard, output_shard, gate_shard = finish([sums[k] for k in ("down", "out", "gate")])
    (up_shard,) = finish([sums["up"]])
    qk_shard, v_shard = finish([sums["qk"], sums["v"]])
    rate_grad = jnp.einsum("td,tf->df", normed_low, d_rate_low, preferred_element_type=F32)
    d_normed = dot_back(d_qk_rel, qk_full) + dot_back(d_v_rel, v_full)
    d_normed = d_normed + dot_back(d_gate_rel, gate_full)
    d_normed = d_normed + jnp.einsum(
        "tf,df->td", d_rate_low, rate_full, preferred_element_type=F32
    )
    d_front, mixer_grad = pull_norm(d_normed)
    tokens_grad = (d_resid + d_front).astype(BF16)
    rate_sum, conv_sum, decay_sum, mixer_sum, heads_sum, feed_sum = sum_small(
        (rate_grad, conv_grad, decay_grad, mixer_grad, heads_grad, feed_grad)
    )
    return (
        block_out,
        tokens_grad,
        jnp.concatenate([qk_shard, v_shard, gate_shard], axis=1),
        own_part(rate_sum, 0),
        own_part(conv_sum, 1),
        own_part(decay_sum, 1),
        own_part(mixer_sum, 0),
        own_part(heads_sum, 0),
        output_shard,
        own_part(feed_sum, 0),
        up_shard,
        down_shard,
    )


def solution(mesh):
    dp, fsdp, sp = (mesh.shape[axis] for axis in ("dp", "fsdp", "sp"))
    dp_axes = ("hi", "x", "core")
    cut = jax.sharding.Mesh(
        mesh.devices.reshape(dp // 4, 2, 2, fsdp, sp), dp_axes + ("fsdp", "sp")
    )
    rows = P(dp_axes + ("fsdp", "sp"), None)
    split = P("fsdp", None)
    return jax.shard_map(
        body,
        mesh=cut,
        in_specs=(
            rows,
            rows,
            P(dp_axes + ("fsdp",), None),
            split,
            split,
            P(None, "fsdp"),
            P(None, "fsdp"),
            P("fsdp"),
            P("fsdp"),
            split,
            P("fsdp"),
            split,
            split,
        ),
        out_specs=(
            rows,
            rows,
            split,
            split,
            P(None, "fsdp"),
            P(None, "fsdp"),
            P("fsdp"),
            P("fsdp"),
            split,
            P("fsdp"),
            split,
            split,
        ),
        check_vma=False,
    )
```

```python
import functools
import jax
import jax.numpy as jnp
from jax import lax
from jax.experimental import pallas as pl
from jax.experimental.pallas import tpu as pltpu
from jax.sharding import PartitionSpec as P

H = 8
DK = 128
DV = 256
CONV = 4
BLOCK = 64
EPSILON = 1e-06
HALO = 16
STACK = 4
ROWS = STACK * BLOCK
SCALE = DK ** (-0.5)
VMEM_BYTES = 56 * 1024 * 1024
F32 = jnp.float32
BF16 = jnp.bfloat16


def mm(a, b, dims=((1,), (0,))):
    return lax.dot_general(
        a.astype(BF16), b.astype(BF16), (dims, ((), ())), preferred_element_type=F32
    )


def halves(a):
    high = a.astype(BF16)
    return high, (a - high.astype(F32)).astype(BF16)


def mm_fine(a, b):
    (ah, al), (bh, bl) = a, b
    return mm(ah, bh) + (mm(ah, bl) + mm(al, bh))


def stack_heads(ref, block, group, base, width):
    rows = pl.ds(pl.multiple_of(block * BLOCK, BLOCK), BLOCK)
    return jnp.concatenate(
        [
            ref[rows, base + (group * STACK + h) * width : base + (group * STACK + h + 1) * width]
            for h in range(STACK)
        ],
        axis=0,
    )


def store_heads(ref, block, group, base, width, value):
    rows = pl.ds(pl.multiple_of(block * BLOCK, BLOCK), BLOCK)
    for h in range(STACK):
        start = base + (group * STACK + h) * width
        ref[rows, start : start + width] = value[h * BLOCK : (h + 1) * BLOCK].astype(ref.dtype)


def head(value, h):
    return value[h * BLOCK : (h + 1) * BLOCK]


def columns(col_ref, block, group):
    packed = col_ref[block, group]
    return [packed[:, i : i + 1] for i in range(6)]


def decay_matrix(cum, doc, row_ref, block, group):
    rows = row_ref[block, group]
    i = lax.broadcasted_iota(jnp.int32, (ROWS, ROWS), 0)
    j = lax.broadcasted_iota(jnp.int32, (ROWS, ROWS), 1)
    inside = ((i // BLOCK) == (j // BLOCK)) & (i >= j) & (doc == rows[1:2])
    decay = jnp.exp(jnp.where(inside, cum - rows[0:1], -1e30))
    return decay, jnp.where(i > j, decay, 0.0)


def unit_inverses(lowers):
    i = lax.broadcasted_iota(jnp.int32, (ROWS, ROWS), 0)
    j = lax.broadcasted_iota(jnp.int32, (ROWS, ROWS), 1)
    apart = jnp.bitwise_xor(i, j)
    inverses = [
        jnp.where(i == j, 1.0, 0.0) - jnp.where(apart == 1, lower, 0.0) for lower in lowers
    ]
    size = 2
    while size < BLOCK:
        cross = (apart >= size) & (apart < 2 * size)
        parts = [halves(inverse) for inverse in inverses]
        right = [
            halves(mm_fine(halves(jnp.where(cross, lower, 0.0)), part))
            for lower, part in zip(lowers, parts)
        ]
        inverses = [
            inverse - mm_fine(part, r) for inverse, part, r in zip(inverses, parts, right)
        ]
        size *= 2
    return inverses


def conv_taps(x, masks, weights):
    taps = [x[HALO:]]
    for s in range(1, CONV):
        taps.append(pltpu.roll(x, s, 0)[HALO:] * masks[s - 1])
    z = taps[0] * weights[0:1]
    for s in range(1, CONV):
        z = z + taps[s] * weights[s : s + 1]
    return taps, z


def conv_masks(mask_ref, length):
    return [
        jnp.broadcast_to(mask_ref[:, s : s + 1], (length, 128)) for s in range(CONV - 1)
    ]


def conv_kernel(x_ref, cw_ref, mask_ref, n_ref):
    length = n_ref.shape[0]
    qk_cols = 2 * H * DK

    def chunk(c, normalise):
        lanes = pl.ds(pl.multiple_of(c * 128, 128), 128)
        masks = conv_masks(mask_ref, length)
        _, z = conv_taps(x_ref[:, lanes].astype(F32), masks, cw_ref[:, lanes])
        y = z * jax.nn.sigmoid(z)
        if normalise:
            y = y * lax.rsqrt(jnp.sum(y * y, axis=1, keepdims=True) + EPSILON)
        n_ref[:, lanes] = y.astype(BF16)

    @pl.loop(0, qk_cols // 128)
    def _(c):
        chunk(c, True)

    @pl.loop(qk_cols // 128, x_ref.shape[1] // 128)
    def _(c):
        chunk(c, False)


def inverse_kernel(n_ref, col_ref, row_ref, inv_ref):
    @pl.loop(0, n_ref.shape[0] // BLOCK)
    def _(block):
        lowers = []
        for group in range(H // STACK):
            cum, beta, _, _, _, doc = columns(col_ref, block, group)
            keys = stack_heads(n_ref, block, group, H * DK, DK)
            _, strict = decay_matrix(cum, doc, row_ref, block, group)
            lowers.append(beta * mm(keys, keys, ((1,), (1,))) * strict)
        for group, inverse in enumerate(unit_inverses(lowers)):
            inv_ref[block, group] = inverse


def state_steps(n_ref, inv_ref, col_ref, state_ref):
    @pl.loop(0, n_ref.shape[0] // BLOCK)
    def _(block):
        for group in range(H // STACK):
            _, beta, a, d, kappa, _ = columns(col_ref, block, group)
            keys = stack_heads(n_ref, block, group, H * DK, DK)
            values = stack_heads(n_ref, block, group, 2 * H * DK, DV).astype(F32)
            seen = jnp.concatenate(
                [mm(head(keys, h), state_ref[group * STACK + h]) for h in range(STACK)], axis=0
            )
            corrected = mm(inv_ref[block, group], beta * (values - a * seen))
            update = d * corrected
            for h in range(STACK):
                n = group * STACK + h
                state_ref[n] = kappa[h * BLOCK : h * BLOCK + 1] * state_ref[n] + mm(
                    head(keys, h), head(update, h), ((0,), (0,))
                )


def state_kernel(n_ref, inv_ref, col_ref, start_ref, state_ref):
    state_ref[...] = start_ref[...].astype(F32)
    state_steps(n_ref, inv_ref, col_ref, state_ref)


def scan_kernel(n_ref, inv_ref, col_ref, row_ref, start_ref, out_ref, cor_ref, states_ref, state):
    state[...] = start_ref[...].astype(F32)

    @pl.loop(0, n_ref.shape[0] // BLOCK)
    def _(block):
        for group in range(H // STACK):
            cum, beta, a, d, kappa, doc = columns(col_ref, block, group)
            queries = stack_heads(n_ref, block, group, 0, DK)
            keys = stack_heads(n_ref, block, group, H * DK, DK)
            values = stack_heads(n_ref, block, group, 2 * H * DK, DV).astype(F32)
            within, _ = decay_matrix(cum, doc, row_ref, block, group)
            scores = SCALE * mm(queries, keys, ((1,), (1,))) * within
            both = []
            for h in range(STACK):
                low = state[group * STACK + h].astype(BF16)
                states_ref[block, group * STACK + h] = low
                both.append(mm(jnp.concatenate([head(keys, h), head(queries, h)], axis=0), low))
            seen = jnp.concatenate([b[:BLOCK] for b in both], axis=0)
            asked = jnp.concatenate([b[BLOCK:] for b in both], axis=0)
            corrected = mm(inv_ref[block, group], beta * (values - a * seen))
            cor_ref[block, group] = corrected.astype(BF16)
            out = (SCALE * a) * asked + mm(scores, corrected)
            store_heads(out_ref, block, group, 0, DV, out)
            update = d * corrected
            for h in range(STACK):
                n = group * STACK + h
                state[n] = kappa[h * BLOCK : h * BLOCK + 1] * state[n] + mm(
                    head(keys, h), head(update, h), ((0,), (0,))
                )


def back_state_kernel(n_ref, inv_ref, col_ref, row_ref, dout_ref, start_ref, dstate_ref):
    blocks = n_ref.shape[0] // BLOCK
    dstate_ref[...] = start_ref[...].astype(F32)

    @pl.loop(0, blocks)
    def _(step):
        block = blocks - 1 - step
        for group in range(H // STACK):
            cum, beta, a, d, kappa, doc = columns(col_ref, block, group)
            queries = stack_heads(n_ref, block, group, 0, DK)
            keys = stack_heads(n_ref, block, group, H * DK, DK)
            within, _ = decay_matrix(cum, doc, row_ref, block, group)
            scores = SCALE * mm(queries, keys, ((1,), (1,))) * within
            dout = stack_heads(dout_ref, block, group, 0, DV)
            wide = (SCALE * a) * dout.astype(F32)
            pulled = jnp.concatenate(
                [mm(head(keys, h), dstate_ref[group * STACK + h]) for h in range(STACK)], axis=0
            )
            d_cor = mm(scores, dout, ((0,), (0,))) + d * pulled
            d_right = mm(inv_ref[block, group], d_cor, ((0,), (0,)))
            d_seen = (-a * beta) * d_right
            for h in range(STACK):
                n = group * STACK + h
                left = jnp.concatenate([head(keys, h), head(queries, h)], axis=0)
                right = jnp.concatenate([head(d_seen, h), head(wide, h)], axis=0)
                dstate_ref[n] = kappa[h * BLOCK : h * BLOCK + 1] * dstate_ref[n] + mm(
                    left, right, ((0,), (0,))
                )


def back_kernel(
    n_ref,
    inv_ref,
    col_ref,
    row_ref,
    dout_ref,
    cor_ref,
    states_ref,
    start_ref,
    dn_ref,
    gcol_ref,
    grow_ref,
    dstate,
):
    length = n_ref.shape[0]
    blocks = length // BLOCK
    dstate[...] = start_ref[...].astype(F32)

    @pl.loop(0, blocks)
    def _(step):
        block = blocks - 1 - step
        for group in range(H // STACK):
            cum, beta, a, d, kappa, doc = columns(col_ref, block, group)
            queries = stack_heads(n_ref, block, group, 0, DK)
            keys = stack_heads(n_ref, block, group, H * DK, DK)
            values = stack_heads(n_ref, block, group, 2 * H * DK, DV).astype(F32)
            within, strict = decay_matrix(cum, doc, row_ref, block, group)
            scores = SCALE * mm(queries, keys, ((1,), (1,))) * within
            weighted = mm(keys, keys, ((1,), (1,))) * strict
            dout = stack_heads(dout_ref, block, group, 0, DV)
            dout_wide = dout.astype(F32)
            corrected = cor_ref[block, group]
            cor_wide = corrected.astype(F32)
            wide = (SCALE * a) * dout_wide
            pulled, seen, asked, dk_state, d_kappa = [], [], [], [], []
            update = (d * cor_wide).astype(BF16)
            for h in range(STACK):
                n = group * STACK + h
                state = states_ref[block, n]
                after = dstate[n]
                after_low = after.astype(BF16)
                both = mm(jnp.concatenate([head(keys, h), head(queries, h)], axis=0), state)
                seen.append(both[:BLOCK])
                asked.append(both[BLOCK:])
                pulled.append(mm(head(keys, h), after_low))
                dk_state.append(mm(head(update, h), after_low, ((1,), (1,))))
                total = jnp.sum(
                    jnp.sum(state.astype(F32) * after, axis=0, keepdims=True),
                    axis=1,
                    keepdims=True,
                )
                d_kappa.append(jnp.broadcast_to(total * (1.0 / BLOCK), (BLOCK, 1)))
            pulled, seen, asked, d_kappa = (
                jnp.concatenate(p, axis=0) for p in (pulled, seen, asked, d_kappa)
            )
            d_cor = mm(scores, dout, ((0,), (0,))) + d * pulled
            d_right = mm(inv_ref[block, group], d_cor, ((0,), (0,)))
            scaled = beta * d_right
            d_seen = -a * scaled
            dk_left, dq_left = [], []
            for h in range(STACK):
                n = group * STACK + h
                left = jnp.concatenate([head(keys, h), head(queries, h)], axis=0)
                right = jnp.concatenate([head(d_seen, h), head(wide, h)], axis=0).astype(BF16)
                both = mm(right, states_ref[block, n], ((1,), (1,)))
                dk_left.append(both[:BLOCK])
                dq_left.append(both[BLOCK:])
                dstate[n] = kappa[h * BLOCK : h * BLOCK + 1] * dstate[n] + mm(
                    left, right, ((0,), (0,))
                )
            d_scores = mm(dout, corrected, ((1,), (1,)))
            d_system = -mm(d_right, corrected, ((1,), (1,)))
            to_rows = (SCALE * d_scores * within).astype(BF16)
            by_gram = d_system * weighted
            to_keys = (beta * d_system * strict).astype(BF16)
            dq = jnp.concatenate(dq_left, axis=0) + mm(to_rows, keys)
            dk = (
                jnp.concatenate(dk_left, axis=0)
                + jnp.concatenate(dk_state, axis=0)
                + mm(to_rows, queries, ((0,), (0,)))
                + mm(to_keys, keys)
                + mm(to_keys, keys, ((0,), (0,)))
            )
            store_heads(dn_ref, block, group, 0, DK, dq)
            store_heads(dn_ref, block, group, H * DK, DK, dk)
            store_heads(dn_ref, block, group, 2 * H * DK, DV, scaled)
            spread = d_scores * scores + beta * by_gram
            d_cum = jnp.sum(spread, axis=1, keepdims=True)
            d_beta = jnp.sum(by_gram, axis=1, keepdims=True) + jnp.sum(
                d_right * (values - a * seen), axis=1, keepdims=True
            )
            d_a = jnp.sum(SCALE * dout_wide * asked - scaled * seen, axis=1, keepdims=True)
            d_d = jnp.sum(cor_wide * pulled, axis=1, keepdims=True)
            lane = lax.broadcasted_iota(jnp.int32, (ROWS, 8), 1)
            packed = jnp.zeros((ROWS, 8), F32)
            for i, part in enumerate((d_cum, d_beta, d_a, d_d, d_kappa)):
                packed = jnp.where(lane == i, part, packed)
            gcol_ref[block, group] = packed
            grow_ref[block, group] = jnp.broadcast_to(
                -jnp.sum(spread, axis=0, keepdims=True), (8, ROWS)
            )


def conv_back_kernel(x_ref, cw_ref, mask_ref, dn_ref, dx_ref, dcw_ref):
    length = dn_ref.shape[0]

    def chunk(c, normalise):
        lanes = pl.ds(pl.multiple_of(c * 128, 128), 128)
        masks = conv_masks(mask_ref, length)
        weights = cw_ref[:, lanes]
        taps, z = conv_taps(x_ref[:, lanes].astype(F32), masks, weights)
        gate = jax.nn.sigmoid(z)
        dn = dn_ref[:, lanes]
        if normalise:
            y = z * gate
            r = lax.rsqrt(jnp.sum(y * y, axis=1, keepdims=True) + EPSILON)
            dn = r * dn - y * (r * r * r * jnp.sum(y * dn, axis=1, keepdims=True))
        dz = dn * gate * (1.0 + z * (1.0 - gate))
        edge = jnp.zeros((HALO, 128), F32)
        dx = jnp.concatenate([edge, dz * weights[0:1]], axis=0)
        sums = [jnp.sum(dz * taps[0], axis=0, keepdims=True)]
        for s in range(1, CONV):
            sums.append(jnp.sum(dz * taps[s], axis=0, keepdims=True))
            moved = jnp.concatenate([edge, dz * masks[s - 1] * weights[s : s + 1]], axis=0)
            dx = dx + pltpu.roll(moved, length + HALO - s, 0)
        dx_ref[:, lanes] = dx.astype(BF16)
        dcw_ref[:, lanes] = jnp.concatenate(sums, axis=0)

    qk_cols = 2 * H * DK

    @pl.loop(0, qk_cols // 128)
    def _(c):
        chunk(c, True)

    @pl.loop(qk_cols // 128, x_ref.shape[1] // 128)
    def _(c):
        chunk(c, False)


def call(kernel, outs, scratch, *args):
    return pl.pallas_call(
        kernel,
        out_shape=[jax.ShapeDtypeStruct(s, t) for s, t in outs],
        in_specs=[pl.BlockSpec(memory_space=pltpu.VMEM)] * len(args),
        out_specs=[pl.BlockSpec(memory_space=pltpu.VMEM)] * len(outs),
        scratch_shapes=scratch,
        compiler_params=pltpu.CompilerParams(vmem_limit_bytes=VMEM_BYTES),
        cost_estimate=pl.CostEstimate(flops=1, bytes_accessed=1, transcendentals=0),
    )(*args)


def mixer(x, weights, rates, decay, doc_all, member, sp_size, points):
    length = x.shape[0] - HALO
    blocks = length // BLOCK
    groups = H // STACK
    channels = x.shape[1]
    padded = jnp.concatenate([jnp.full((HALO,), -1, jnp.int32), doc_all])
    near = lax.dynamic_slice_in_dim(padded, member * length, length + HALO, 0)
    docs = near[HALO:]
    masks = jnp.stack(
        [(near[HALO - s : HALO - s + length] == docs).astype(F32) for s in range(1, CONV)]
        + [jnp.zeros((length,), F32)] * (8 - CONV + 1),
        axis=1,
    )
    doc_blocks = docs.reshape(blocks, 1, BLOCK)
    before = jnp.concatenate([near[HALO - 1 : HALO], doc_blocks[:-1, 0, -1]]).reshape(
        blocks, 1, 1
    )
    last = doc_blocks[:, :, -1:]
    from_before = (doc_blocks == before).astype(F32)
    to_last = (doc_blocks == last).astype(F32)
    kept = (last == before).astype(F32)

    def small(rates, decay):
        by_block = jnp.transpose(rates.reshape(blocks, BLOCK, H, 2), (3, 0, 2, 1))
        beta = jax.nn.sigmoid(by_block[1])
        offset = decay[1].reshape(1, H, 1)
        log_decay = -jnp.exp(decay[0]).reshape(1, H, 1) * jax.nn.softplus(by_block[0] + offset)
        i = lax.broadcasted_iota(jnp.int32, (BLOCK, BLOCK), 0)
        j = lax.broadcasted_iota(jnp.int32, (BLOCK, BLOCK), 1)
        upper = (i <= j).astype(F32)
        cum = jnp.einsum("bhi,ij->bhj", log_decay, upper, precision=lax.Precision.HIGHEST)
        final = cum[:, :, -1:]
        a = jnp.exp(cum) * from_before
        d = jnp.exp(final - cum) * to_last
        kappa = jnp.broadcast_to(jnp.exp(final) * kept, cum.shape)
        return jnp.stack([cum, beta, a, d, kappa], axis=0)

    five, pull_small = jax.vjp(small, rates, decay)
    doc_row = jnp.broadcast_to(doc_blocks.astype(F32), (blocks, H, BLOCK))
    packed = jnp.concatenate([five, doc_row[None], jnp.zeros((2,) + doc_row.shape, F32)], axis=0)
    packed = packed.reshape(8, blocks, groups, ROWS)
    col = jnp.transpose(packed, (1, 2, 3, 0))
    row = jnp.transpose(jnp.stack([packed[0], packed[5]] + [packed[6]] * 6), (1, 2, 0, 3))

    n_shape = ((length, channels), BF16)
    inv_shape = ((blocks, groups, ROWS, ROWS), F32)
    state_shape = ((H, DK, DV), F32)
    cor_shape = ((blocks, groups, ROWS, ROWS), BF16)
    x = points("conv", x)
    (n,) = call(conv_kernel, [n_shape], [], x, weights, masks)
    n = points("inverse", n)
    (inv,) = call(inverse_kernel, [inv_shape], [], n, col, row)
    inv = points("state", inv)
    start = jnp.zeros((H, DK, DV), BF16)
    ahead = [(i, i + 1) for i in range(sp_size - 1)]
    behind = [(i + 1, i) for i in range(sp_size - 1)]
    for _ in range(sp_size - 1):
        (state,) = call(state_kernel, [state_shape], [], n, inv, col, start)
        start = lax.ppermute(state.astype(BF16), "sp", ahead)
    mixed, cor, states = call(
        scan_kernel,
        [((length, H * DV), BF16), cor_shape, ((blocks, H, DK, DV), BF16)],
        [pltpu.VMEM((H, DK, DV), F32)],
        n,
        inv,
        col,
        row,
        start,
    )

    def pull(dout):
        dstart = jnp.zeros((H, DK, DV), BF16)
        for _ in range(sp_size - 1):
            (dstate,) = call(
                back_state_kernel, [state_shape], [], n, inv, col, row, dout, dstart
            )
            dstart = lax.ppermute(dstate.astype(BF16), "sp", behind)
        dstart = points("back", dstart)
        dn, gcol, grow = call(
            back_kernel,
            [
                ((length, channels), F32),
                ((blocks, groups, ROWS, 8), F32),
                ((blocks, groups, 8, ROWS), F32),
            ],
            [pltpu.VMEM((H, DK, DV), F32)],
            n,
            inv,
            col,
            row,
            dout,
            cor,
            states,
            dstart,
        )
        dn = points("conv_back", dn)
        dx, dcw = call(
            conv_back_kernel,
            [((length + HALO, channels), BF16), ((CONV, channels), F32)],
            [],
            x,
            weights,
            masks,
            dn,
        )
        grads = jnp.transpose(gcol[..., :5], (3, 0, 1, 2))
        grads = grads.at[0].add(grow[:, :, 0])
        d_rates, d_decay = pull_small(grads.reshape(5, blocks, H, BLOCK))
        from_next = lax.ppermute(dx[:HALO], "sp", behind)
        return dx, from_next, dcw, d_rates, d_decay

    return mixed, pull


def rms_norm(values, scales):
    return values * lax.rsqrt(jnp.mean(values * values, axis=-1, keepdims=True) + EPSILON) * scales


def output_gate(mixed, gate_raw, scales):
    length = mixed.shape[0]
    normed = rms_norm(mixed.reshape(length, H, DV), scales)
    return (normed * jax.nn.silu(gate_raw).reshape(length, H, DV)).reshape(length, H * DV)


def residual_norm(values, attended, scales):
    hidden = values + attended
    return (hidden, rms_norm(hidden, scales))


def after(value, *earlier):
    return lax.optimization_barrier((value,) + earlier)[0]


def swap(value, axis):
    return lax.ppermute(value, axis, [(0, 1), (1, 0)])


def other(first):
    return "sp" if first == "x" else "x"


def pair(axis, mine, theirs, dim):
    first = lax.axis_index(axis) == 0
    return jnp.where(
        first,
        jnp.concatenate([mine, theirs], axis=dim),
        jnp.concatenate([theirs, mine], axis=dim),
    )


def relative_axes(first):
    return ("core", first, other(first))


def place(first, k):
    total = 0
    for shift, axis in zip((2, 1, 0), relative_axes(first)):
        bit = lax.axis_index(axis)
        total = total + (1 << shift) * (1 - bit if (k >> shift) & 1 else bit)
    return total


def reorder(value, first):
    width = value.shape[1] // 8
    return jnp.concatenate(
        [lax.dynamic_slice_in_dim(value, place(first, i) * width, width, 1) for i in range(8)],
        axis=1,
    )


def shifted(value, step):
    count = lax.axis_size("fsdp")
    return lax.ppermute(value, "fsdp", [(i, (i + step) % count) for i in range(count)])


def gather_blocks(piece):
    count, rows = lax.axis_size("fsdp"), piece.shape[0]
    parts = [piece] + [shifted(piece, s) for s in range(1, count)]
    line = jnp.concatenate([parts[(count - 1 - i) % count] for i in range(2 * count - 1)], axis=0)
    start = (count - 1 - lax.axis_index("fsdp")) * rows
    return lax.dynamic_slice_in_dim(line, start, count * rows, 0)


def sum_blocks(value):
    total = lax.psum_scatter(value.astype(BF16), "fsdp", scatter_dimension=0, tiled=True)
    if lax.axis_size("hi") > 1:
        total = lax.psum(total, "hi")
    return total


WEIGHT_AXES = ("fsdp", "hi", "x", "core", "sp")


def gather_rows(shard):
    count, own = 1, 0
    for axis in WEIGHT_AXES[1:]:
        count = count * lax.axis_size(axis)
        own = own * lax.axis_size(axis) + lax.axis_index(axis)
    rows = shard.shape[0] // count
    piece = lax.dynamic_slice_in_dim(shard, own * rows, rows, 0)
    return lax.all_gather(piece, WEIGHT_AXES, axis=0, tiled=True)


class ColumnGather:
    def __init__(self, shard, first):
        width = shard.shape[1] // 8
        self.first = first
        self.piece = lax.dynamic_slice_in_dim(shard, place(first, 0) * width, width, 1)

    def blocks(self, *earlier):
        self.held = gather_blocks(after(self.piece, *earlier) if earlier else self.piece)
        return self.held

    def second(self, *earlier):
        held = after(self.held, *earlier) if earlier else self.held
        self.held = jnp.concatenate([held, swap(held, other(self.first))], axis=1)
        return self.held

    def third(self, *earlier):
        held = after(self.held, *earlier) if earlier else self.held
        self.held = jnp.concatenate([held, swap(held, self.first)], axis=1)
        return self.held

    def full(self):
        return self.held, swap(self.held, "core")


def dot_columns(values, halves_of):
    parts = [jnp.dot(values, w, preferred_element_type=F32) for w in halves_of]
    return jnp.concatenate(parts, axis=1)


def dot_back(grads, halves_of):
    half = grads.shape[1] // 2
    return jnp.einsum(
        "tf,df->td", grads[:, :half], halves_of[0], preferred_element_type=F32
    ) + jnp.einsum("tf,df->td", grads[:, half:], halves_of[1], preferred_element_type=F32)


def grad_dot(left, right):
    return jnp.einsum("td,tf->df", left, right, preferred_element_type=F32)


class ColumnSum:
    def __init__(self, left, right, first):
        self.left, self.right, self.first = left, right, first
        self.width = right.shape[1] // 8
        self.from_core = swap(grad_dot(left, right[:, 4 * self.width :]).astype(BF16), "core")

    def second(self):
        width = self.width
        outgoing = grad_dot(self.left, self.right[:, 2 * width : 4 * width])
        self.outgoing = (outgoing + self.from_core[:, 2 * width :].astype(F32)).astype(BF16)
        self.from_first = swap(self.outgoing, self.first)
        return self.outgoing

    def third(self):
        width = self.width
        self.outgoing = (
            grad_dot(self.left, self.right[:, width : 2 * width])
            + self.from_core[:, width : 2 * width].astype(F32)
            + self.from_first[:, width:].astype(F32)
        ).astype(BF16)
        self.from_second = swap(self.outgoing, other(self.first))
        return self.outgoing

    def own(self):
        width = self.width
        return (
            grad_dot(self.left, self.right[:, :width])
            + self.from_core[:, :width].astype(F32)
            + self.from_first[:, :width].astype(F32)
            + self.from_second.astype(F32)
        )


def spread(blocks):
    held = jnp.concatenate(blocks, axis=0)[None]
    for axis in ("sp", "x"):
        held = jnp.concatenate([held, swap(held, axis)], axis=0)
    return held, swap(held, "core")


def unpack_kernel(segments, count, places_ref, *refs):
    sources, outs = refs[:count], refs[count:]
    for source, row, out, column, rows, blocks, way in segments:
        for k in range(8):
            piece = sources[2 * source + k // 4]
            at = pl.multiple_of(column + places_ref[2 * way, k] * (128 * blocks), 128)
            down = pl.multiple_of(places_ref[2 * way + 1, k] * rows, 16)
            for j in range(blocks):
                outs[out][pl.ds(down, rows), pl.ds(at + 128 * j, 128)] = piece[
                    k % 4, row + j * rows : row + (j + 1) * rows
                ].astype(F32)


def unpack(places, segments, sources, shapes):
    count = len(sources)
    return pl.pallas_call(
        functools.partial(unpack_kernel, segments, count),
        out_shape=[jax.ShapeDtypeStruct(s, F32) for s in shapes],
        in_specs=[pl.BlockSpec(memory_space=pltpu.SMEM)]
        + [pl.BlockSpec(memory_space=pltpu.VMEM)] * count,
        out_specs=[pl.BlockSpec(memory_space=pltpu.VMEM)] * len(shapes),
        compiler_params=pltpu.CompilerParams(vmem_limit_bytes=VMEM_BYTES),
    )(places, *sources)


def spread_places():
    core, x, y = lax.axis_index("core"), lax.axis_index("x"), lax.axis_index("sp")
    table = [[] for _ in range(6)]
    for k in range(8):
        c, d, e = (
            1 - bit if (k >> shift) & 1 else bit for shift, bit in ((2, core), (1, x), (0, y))
        )
        for line, value in enumerate((4 * c + 2 * d + e, 0, 4 * c + 2 * e + d, 0, 2 * c + d, e)):
            table[line].append(jnp.asarray(value, jnp.int32))
    return jnp.stack([jnp.stack(line) for line in table])


def by_half(values):
    blocks = values.reshape(values.shape[0], lax.axis_size("fsdp"), 2, -1)
    low = blocks[:, :, 0].reshape(values.shape[0], -1)
    high = blocks[:, :, 1].reshape(values.shape[0], -1)
    first = lax.axis_index("sp") == 0
    return jnp.concatenate(
        [jnp.where(first, low, high), jnp.where(first, high, low)], axis=1
    )


class HalfSum:
    def __init__(self, left, right):
        self.left, self.first = left, "x"
        self.width = width = right.shape[1] // 4
        core, x = lax.axis_index("core"), lax.axis_index("x")

        def half(c):
            return jnp.concatenate(
                [
                    lax.dynamic_slice_in_dim(right, (2 * c + d) * width, width, 1)
                    for d in (x, 1 - x)
                ],
                axis=1,
            )

        self.near, far_core = half(core), half(1 - core)
        self.rows = left.shape[1] // 2
        self.from_core = swap(grad_dot(left, far_core).astype(BF16), "core")

    def second(self):
        width = self.width
        outgoing = grad_dot(self.left, self.near[:, width:])
        self.outgoing = (outgoing + self.from_core[:, width:].astype(F32)).astype(BF16)
        self.from_x = swap(self.outgoing, "x")
        return self.outgoing

    def third(self):
        rows, width = self.rows, self.width
        self.outgoing = (
            grad_dot(self.left[:, rows:], self.near[:, :width])
            + self.from_core[rows:, :width].astype(F32)
            + self.from_x[rows:].astype(F32)
        ).astype(BF16)
        self.from_y = swap(self.outgoing, "sp")
        return self.outgoing

    def own(self):
        rows, width = self.rows, self.width
        return (
            grad_dot(self.left[:, :rows], self.near[:, :width])
            + self.from_core[:rows, :width].astype(F32)
            + self.from_x[:rows].astype(F32)
            + self.from_y.astype(F32)
        )


def narrow(value):
    return jnp.concatenate(
        [value[:, i : i + 128] for i in range(0, value.shape[1], 128)], axis=0
    )


def pack_small(parts, width):
    flat = jnp.concatenate([p.reshape(-1) for p in parts])
    return jnp.pad(flat, (0, -flat.shape[0] % (16 * width))).reshape(-1, width)


def unpack_small(every, parts):
    out, start = [], 0
    for p in parts:
        out.append(every[:, start : start + p.size].reshape((-1,) + p.shape))
        start += p.size
    return out


def sum_small(parts, *earlier):
    flat = jnp.concatenate([p.reshape(-1) for p in parts])
    size = flat.shape[0]
    flat = after(jnp.pad(flat, (0, -size % 1024)).reshape(-1, 128), *earlier)
    for axis in ("core", "x", "sp"):
        flat = flat + swap(flat, axis)
    members = lax.axis_size("fsdp")
    for bit in range(members.bit_length() - 1):
        flat = flat + lax.ppermute(flat, "fsdp", [(i, i ^ (1 << bit)) for i in range(members)])
    if lax.axis_size("hi") > 1:
        flat = lax.psum(flat, "hi")
    total = flat.reshape(-1)
    out, start = [], 0
    for p in parts:
        out.append(total[start : start + p.size].reshape(p.shape))
        start += p.size
    return out


def own_part(value, axis):
    size = value.shape[axis] // lax.axis_size("fsdp")
    return lax.dynamic_slice_in_dim(value, lax.axis_index("fsdp") * size, size, axis)


def body(
    tokens,
    cotangent,
    doc_lengths,
    input_weight,
    rate_weight,
    conv_weight,
    head_decay,
    mixer_gain,
    heads_gain,
    output_weight,
    feed_gain,
    up_weight,
    down_weight,
):
    length = tokens.shape[0]
    sp_size = lax.axis_size("sp")
    member = lax.axis_index("sp")
    qkv_cols = H * (2 * DK + DV)
    qk_cols = 2 * H * DK
    members = lax.axis_size("fsdp")
    qk_way = ColumnGather(input_weight[:, :qk_cols], "x")
    v_way = ColumnGather(input_weight[:, qk_cols:qkv_cols], "sp")
    gate_way = ColumnGather(input_weight[:, qkv_cols:], "x")
    down_way = ColumnGather(down_weight, "sp")
    pair_rows, pair_cols = qk_way.piece.shape[0], 2 * qk_way.piece.shape[1]
    smalls = (rate_weight, conv_weight, head_decay, mixer_gain, heads_gain, feed_gain)
    first_load = jnp.concatenate(
        [
            jnp.concatenate([qk_way.piece, v_way.piece], axis=1),
            pack_small(smalls, pair_cols),
        ],
        axis=0,
    )
    first_all = gather_blocks(first_load).reshape(members, -1, pair_cols)
    both = first_all[:, :pair_rows].reshape(-1, pair_cols)
    qk_way.held, v_way.held = both[:, : pair_cols // 2], both[:, pair_cols // 2 :]
    rate_all, conv_all, decay_all, mixer_all, heads_all, feed_all = unpack_small(
        first_all[:, pair_rows:].reshape(members, -1), smalls
    )
    qkv_second = (qk_way.second(), v_way.second())
    gate_way.blocks(*qkv_second)
    qkv_third = (qk_way.third(), v_way.third())
    gate_way.second(*qkv_third)
    qk_full, v_full = qk_way.full(), v_way.full()
    out_full = gather_rows(output_weight)
    up_full = gather_rows(up_weight)
    rate_full = rate_all.reshape(-1, 2 * H)
    conv_full = jnp.swapaxes(conv_all, 0, 1).reshape(CONV, -1).astype(F32)
    decay_full = jnp.swapaxes(decay_all, 0, 1).reshape(2, H).astype(F32)
    mixer_scale = mixer_all.reshape(-1).astype(F32)
    heads_scale = heads_all.reshape(-1).astype(F32)
    feed_scale = feed_all.reshape(-1).astype(F32)

    def points(name, value):
        if name == "conv":
            down_way.blocks(value)
            return value
        if name == "inverse":
            value = after(value, gate_way.held, down_way.held)
            gate_way.third(value)
            down_way.second(value)
            return value
        if name == "state":
            value = after(value, gate_way.held, down_way.held)
            down_way.third(value)
            return value
        if name == "back":
            return after(value, sums["down"].third())
        if name == "conv_back":
            return after(value, *(sums[key].third() for key in ("out", "gate")))
        return value

    sums = {}

    ends = jnp.cumsum(doc_lengths[0])
    positions = lax.broadcasted_iota(jnp.int32, (length * sp_size, 1), 0)
    doc_ids = jnp.sum((positions >= ends[None, :]).astype(jnp.int32), axis=1)

    ahead = [(i, i + 1) for i in range(sp_size - 1)]
    halo = lax.ppermute(tokens[-HALO:], "sp", ahead)
    x_float = tokens.astype(F32)
    normed, pull_norm = jax.vjp(rms_norm, x_float, mixer_scale)
    normed_low = normed.astype(BF16)
    halo_low = rms_norm(halo.astype(F32), mixer_scale).astype(BF16)
    normed_more = jnp.concatenate([halo_low, normed_low], axis=0)
    qkv = jnp.concatenate(
        [
            reorder(dot_columns(normed_more, qk_full).astype(BF16), "x"),
            reorder(dot_columns(normed_more, v_full).astype(BF16), "sp"),
        ],
        axis=1,
    )
    rate_raw = jnp.dot(normed_low, rate_full, preferred_element_type=F32)
    rates = rate_raw.astype(BF16).astype(F32).reshape(length, H, 2)
    mixed, pull_mix = mixer(qkv, conv_full, rates, decay_full, doc_ids, member, sp_size, points)
    gate_full, down_full = gate_way.full(), down_way.full()
    gate_raw = reorder(dot_columns(normed_low, gate_full), "x")
    gated, pull_gate = jax.vjp(output_gate, mixed.astype(F32), gate_raw, heads_scale)
    gated_low = gated.astype(BF16)
    attended = jnp.dot(gated_low, out_full, preferred_element_type=F32)
    (hidden, normed_two), pull_resid = jax.vjp(residual_norm, x_float, attended, feed_scale)
    two_low = normed_two.astype(BF16)
    gate_up = jnp.dot(two_low, up_full, preferred_element_type=F32)

    def feed_act(gate_up):
        half = gate_up.shape[1] // 2
        return jax.nn.silu(gate_up[:, :half]) * gate_up[:, half:]

    activated, pull_act = jax.vjp(feed_act, gate_up)
    act_low = activated.astype(BF16)
    block_out = (hidden + reorder(dot_columns(act_low, down_full), "sp")).astype(BF16)
    cot_rel = reorder(cotangent, "sp")
    sums["down"] = ColumnSum(act_low, cot_rel, "sp")
    d_act = dot_back(cot_rel, down_full)
    d_gu_low = pull_act(d_act)[0].astype(BF16)
    sums["up"] = HalfSum(by_half(two_low), d_gu_low)
    d_gu_low = after(d_gu_low, sums["down"].second())
    d_two = jnp.einsum("tf,df->td", d_gu_low, up_full, preferred_element_type=F32)
    d_resid, d_attended, feed_grad = pull_resid((cotangent.astype(F32), d_two))
    d_att_low = d_attended.astype(BF16)
    d_att_rel = reorder(d_att_low, "sp")
    sums["out"] = ColumnSum(gated_low, d_att_rel, "sp")
    d_gated = jnp.einsum("td,ed->te", d_att_low, out_full, preferred_element_type=F32)
    d_mixed, d_gate, heads_grad = pull_gate(d_gated)
    d_gate_low = d_gate.astype(BF16)
    d_gate_rel = reorder(d_gate_low, "x")
    sums["gate"] = ColumnSum(normed_low, d_gate_rel, "x")
    d_mixed_low = after(
        d_mixed.astype(BF16), *(sums[key].second() for key in ("up", "out", "gate"))
    )
    d_more, from_next, conv_grad, d_rates, decay_grad = pull_mix(d_mixed_low)
    edge = jnp.pad(from_next.astype(F32), ((length - HALO, 0), (0, 0)))
    d_qkv = (d_more[HALO:].astype(F32) + edge).astype(BF16)
    d_rate_low = d_rates.reshape(length, 2 * H).astype(BF16)
    d_qk_rel = reorder(d_qkv[:, :qk_cols], "x")
    d_v_rel = reorder(d_qkv[:, qk_cols:], "sp")
    sums["qk"] = ColumnSum(normed_low, d_qk_rel, "x")
    sums["v"] = ColumnSum(normed_low, d_v_rel, "sp")
    for step in ("second", "third"):
        for key in ("qk", "v"):
            getattr(sums[key], step)()
    sums["up"].third()
    places = spread_places()
    blocks = [sum_blocks(sums[k].own()) for k in ("down", "out", "gate")]
    down_rows, out_rows = blocks[0].shape[0], blocks[1].shape[0]
    early_sums = spread([narrow(block) for block in blocks])
    down_shard, output_shard = unpack(
        places,
        [(0, 0, 0, 0, down_rows, 1, 1), (0, down_rows, 1, 0, out_rows, 1, 1)],
        early_sums,
        [down_weight.shape, output_weight.shape],
    )
    up_block = sum_blocks(sums["up"].own())
    (up_shard,) = unpack(
        places,
        [(0, 0, 0, 0, up_block.shape[0], up_block.shape[1] // 128, 2)],
        spread([narrow(up_block)]),
        [up_weight.shape],
    )
    late_block = sum_blocks(jnp.concatenate([sums["qk"].own(), sums["v"].own()], axis=1))
    rows, wide = late_block.shape[0], late_block.shape[1] // 256
    gate_wide = blocks[2].shape[1] // 128
    (input_shard,) = unpack(
        places,
        [
            (0, 0, 0, 0, rows, wide, 0),
            (0, wide * rows, 0, qk_cols, rows, wide, 1),
            (1, down_rows + out_rows, 0, qkv_cols, rows, gate_wide, 0),
        ],
        spread([narrow(late_block)]) + early_sums,
        [input_weight.shape],
    )
    rate_grad = jnp.einsum("td,tf->df", normed_low, d_rate_low, preferred_element_type=F32)
    d_normed = dot_back(d_qk_rel, qk_full) + dot_back(d_v_rel, v_full)
    d_normed = d_normed + dot_back(d_gate_rel, gate_full)
    d_normed = d_normed + jnp.einsum(
        "tf,df->td", d_rate_low, rate_full, preferred_element_type=F32
    )
    d_front, mixer_grad = pull_norm(d_normed)
    tokens_grad = (d_resid + d_front).astype(BF16)
    rate_sum, conv_sum, decay_sum, mixer_sum, heads_sum, feed_sum = sum_small(
        (rate_grad, conv_grad, decay_grad, mixer_grad, heads_grad, feed_grad),
        sums["qk"].outgoing,
        sums["v"].outgoing,
    )
    return (
        block_out,
        tokens_grad,
        input_shard,
        own_part(rate_sum, 0),
        own_part(conv_sum, 1),
        own_part(decay_sum, 1),
        own_part(mixer_sum, 0),
        own_part(heads_sum, 0),
        output_shard,
        own_part(feed_sum, 0),
        up_shard,
        down_shard,
    )


def solution(mesh):
    dp, fsdp, sp = (mesh.shape[axis] for axis in ("dp", "fsdp", "sp"))
    dp_axes = ("hi", "x", "core")
    cut = jax.sharding.Mesh(
        mesh.devices.reshape(dp // 4, 2, 2, fsdp, sp), dp_axes + ("fsdp", "sp")
    )
    rows = P(dp_axes + ("fsdp", "sp"), None)
    split = P("fsdp", None)
    return jax.shard_map(
        body,
        mesh=cut,
        in_specs=(
            rows,
            rows,
            P(dp_axes + ("fsdp",), None),
            split,
            split,
            P(None, "fsdp"),
            P(None, "fsdp"),
            P("fsdp"),
            P("fsdp"),
            split,
            P("fsdp"),
            split,
            split,
        ),
        out_specs=(
            rows,
            rows,
            split,
            split,
            P(None, "fsdp"),
            P(None, "fsdp"),
            P("fsdp"),
            P("fsdp"),
            split,
            P("fsdp"),
            split,
            split,
        ),
        check_vma=False,
    )
```

```python
import functools
import jax
import jax.numpy as jnp
from jax import lax
from jax.experimental import pallas as pl
from jax.experimental.pallas import tpu as pltpu
from jax.sharding import PartitionSpec as P

H = 8
DK = 128
DV = 256
CONV = 4
BLOCK = 64
EPSILON = 1e-06
HALO = 16
STACK = 4
ROWS = STACK * BLOCK
SCALE = DK ** (-0.5)
VMEM_BYTES = 56 * 1024 * 1024
F32 = jnp.float32
BF16 = jnp.bfloat16


def mm(a, b, dims=((1,), (0,))):
    return lax.dot_general(
        a.astype(BF16), b.astype(BF16), (dims, ((), ())), preferred_element_type=F32
    )


def halves(a):
    high = a.astype(BF16)
    return high, (a - high.astype(F32)).astype(BF16)


def mm_fine(a, b):
    (ah, al), (bh, bl) = a, b
    return mm(ah, bh) + (mm(ah, bl) + mm(al, bh))


def stack_heads(ref, block, group, base, width):
    rows = pl.ds(pl.multiple_of(block * BLOCK, BLOCK), BLOCK)
    return jnp.concatenate(
        [
            ref[rows, base + (group * STACK + h) * width : base + (group * STACK + h + 1) * width]
            for h in range(STACK)
        ],
        axis=0,
    )


def store_heads(ref, block, group, base, width, value):
    rows = pl.ds(pl.multiple_of(block * BLOCK, BLOCK), BLOCK)
    for h in range(STACK):
        start = base + (group * STACK + h) * width
        ref[rows, start : start + width] = value[h * BLOCK : (h + 1) * BLOCK].astype(ref.dtype)


def head(value, h):
    return value[h * BLOCK : (h + 1) * BLOCK]


def columns(feat_ref, block, group):
    packed = feat_ref[pl.ds(pl.multiple_of(block * BLOCK, BLOCK), BLOCK), :]
    return [
        jnp.concatenate(
            [
                packed[:, f * H + group * STACK + h : f * H + group * STACK + h + 1]
                for h in range(STACK)
            ],
            axis=0,
        )
        for f in range(6)
    ]


def decay_matrix(cum, doc):
    i = lax.broadcasted_iota(jnp.int32, (ROWS, ROWS), 0)
    j = lax.broadcasted_iota(jnp.int32, (ROWS, ROWS), 1)
    cum_row, doc_row = (
        jnp.sum(jnp.where(i == j, c, 0.0), axis=0, keepdims=True) for c in (cum, doc)
    )
    inside = ((i // BLOCK) == (j // BLOCK)) & (i >= j) & (doc == doc_row)
    decay = jnp.exp(jnp.where(inside, cum - cum_row, -1e30))
    return decay, jnp.where(i > j, decay, 0.0)


def unit_inverses(lowers):
    i = lax.broadcasted_iota(jnp.int32, (ROWS, ROWS), 0)
    j = lax.broadcasted_iota(jnp.int32, (ROWS, ROWS), 1)
    apart = jnp.bitwise_xor(i, j)
    inverses = [
        jnp.where(i == j, 1.0, 0.0) - jnp.where(apart == 1, lower, 0.0) for lower in lowers
    ]
    size = 2
    while size < BLOCK:
        cross = (apart >= size) & (apart < 2 * size)
        parts = [halves(inverse) for inverse in inverses]
        right = [
            halves(mm_fine(halves(jnp.where(cross, lower, 0.0)), part))
            for lower, part in zip(lowers, parts)
        ]
        inverses = [
            inverse - mm_fine(part, r) for inverse, part, r in zip(inverses, parts, right)
        ]
        size *= 2
    return inverses


def conv_taps(x, masks, weights):
    taps = [x[HALO:]]
    for s in range(1, CONV):
        taps.append(pltpu.roll(x, s, 0)[HALO:] * masks[s - 1])
    z = taps[0] * weights[0:1]
    for s in range(1, CONV):
        z = z + taps[s] * weights[s : s + 1]
    return taps, z


def conv_masks(mask_ref, length):
    return [
        jnp.broadcast_to(mask_ref[:, s : s + 1], (length, 128)) for s in range(CONV - 1)
    ]


def conv_kernel(x_ref, cw_ref, mask_ref, n_ref):
    length = n_ref.shape[0]
    qk_cols = 2 * H * DK

    def chunk(c, normalise):
        lanes = pl.ds(pl.multiple_of(c * 128, 128), 128)
        masks = conv_masks(mask_ref, length)
        _, z = conv_taps(x_ref[:, lanes].astype(F32), masks, cw_ref[:, lanes])
        y = z * jax.nn.sigmoid(z)
        if normalise:
            y = y * lax.rsqrt(jnp.sum(y * y, axis=1, keepdims=True) + EPSILON)
        n_ref[:, lanes] = y.astype(BF16)

    @pl.loop(0, qk_cols // 128)
    def _(c):
        chunk(c, True)

    @pl.loop(qk_cols // 128, x_ref.shape[1] // 128)
    def _(c):
        chunk(c, False)


def inverse_kernel(n_ref, col_ref, inv_ref):
    @pl.loop(0, n_ref.shape[0] // BLOCK)
    def _(block):
        lowers = []
        for group in range(H // STACK):
            cum, beta, _, _, _, doc = columns(col_ref, block, group)
            keys = stack_heads(n_ref, block, group, H * DK, DK)
            _, strict = decay_matrix(cum, doc)
            lowers.append(beta * mm(keys, keys, ((1,), (1,))) * strict)
        for group, inverse in enumerate(unit_inverses(lowers)):
            inv_ref[block, group] = inverse


def state_steps(n_ref, inv_ref, col_ref, state_ref):
    @pl.loop(0, n_ref.shape[0] // BLOCK)
    def _(block):
        for group in range(H // STACK):
            _, beta, a, d, kappa, _ = columns(col_ref, block, group)
            keys = stack_heads(n_ref, block, group, H * DK, DK)
            values = stack_heads(n_ref, block, group, 2 * H * DK, DV).astype(F32)
            seen = jnp.concatenate(
                [mm(head(keys, h), state_ref[group * STACK + h]) for h in range(STACK)], axis=0
            )
            corrected = mm(inv_ref[block, group], beta * (values - a * seen))
            update = d * corrected
            for h in range(STACK):
                n = group * STACK + h
                state_ref[n] = kappa[h * BLOCK : h * BLOCK + 1] * state_ref[n] + mm(
                    head(keys, h), head(update, h), ((0,), (0,))
                )


def state_kernel(n_ref, inv_ref, col_ref, start_ref, state_ref):
    state_ref[...] = start_ref[...].astype(F32)
    state_steps(n_ref, inv_ref, col_ref, state_ref)


def scan_kernel(n_ref, inv_ref, col_ref, start_ref, out_ref, cor_ref, states_ref, state):
    state[...] = start_ref[...].astype(F32)

    @pl.loop(0, n_ref.shape[0] // BLOCK)
    def _(block):
        for group in range(H // STACK):
            cum, beta, a, d, kappa, doc = columns(col_ref, block, group)
            queries = stack_heads(n_ref, block, group, 0, DK)
            keys = stack_heads(n_ref, block, group, H * DK, DK)
            values = stack_heads(n_ref, block, group, 2 * H * DK, DV).astype(F32)
            within, _ = decay_matrix(cum, doc)
            scores = SCALE * mm(queries, keys, ((1,), (1,))) * within
            both = []
            for h in range(STACK):
                low = state[group * STACK + h].astype(BF16)
                states_ref[block, group * STACK + h] = low
                both.append(mm(jnp.concatenate([head(keys, h), head(queries, h)], axis=0), low))
            seen = jnp.concatenate([b[:BLOCK] for b in both], axis=0)
            asked = jnp.concatenate([b[BLOCK:] for b in both], axis=0)
            corrected = mm(inv_ref[block, group], beta * (values - a * seen))
            cor_ref[block, group] = corrected.astype(BF16)
            out = (SCALE * a) * asked + mm(scores, corrected)
            store_heads(out_ref, block, group, 0, DV, out)
            update = d * corrected
            for h in range(STACK):
                n = group * STACK + h
                state[n] = kappa[h * BLOCK : h * BLOCK + 1] * state[n] + mm(
                    head(keys, h), head(update, h), ((0,), (0,))
                )


def back_state_kernel(n_ref, inv_ref, col_ref, dout_ref, start_ref, dstate_ref):
    blocks = n_ref.shape[0] // BLOCK
    dstate_ref[...] = start_ref[...].astype(F32)

    @pl.loop(0, blocks)
    def _(step):
        block = blocks - 1 - step
        for group in range(H // STACK):
            cum, beta, a, d, kappa, doc = columns(col_ref, block, group)
            queries = stack_heads(n_ref, block, group, 0, DK)
            keys = stack_heads(n_ref, block, group, H * DK, DK)
            within, _ = decay_matrix(cum, doc)
            scores = SCALE * mm(queries, keys, ((1,), (1,))) * within
            dout = stack_heads(dout_ref, block, group, 0, DV)
            wide = (SCALE * a) * dout.astype(F32)
            pulled = jnp.concatenate(
                [mm(head(keys, h), dstate_ref[group * STACK + h]) for h in range(STACK)], axis=0
            )
            d_cor = mm(scores, dout, ((0,), (0,))) + d * pulled
            d_right = mm(inv_ref[block, group], d_cor, ((0,), (0,)))
            d_seen = (-a * beta) * d_right
            for h in range(STACK):
                n = group * STACK + h
                left = jnp.concatenate([head(keys, h), head(queries, h)], axis=0)
                right = jnp.concatenate([head(d_seen, h), head(wide, h)], axis=0)
                dstate_ref[n] = kappa[h * BLOCK : h * BLOCK + 1] * dstate_ref[n] + mm(
                    left, right, ((0,), (0,))
                )


def back_kernel(
    n_ref,
    inv_ref,
    col_ref,

    dout_ref,
    cor_ref,
    states_ref,
    start_ref,
    dn_ref,
    gfeat_ref,
    dstate,
):
    length = n_ref.shape[0]
    blocks = length // BLOCK
    dstate[...] = start_ref[...].astype(F32)

    @pl.loop(0, blocks)
    def _(step):
        block = blocks - 1 - step
        packed = jnp.zeros((BLOCK, 128), F32)
        for group in range(H // STACK):
            cum, beta, a, d, kappa, doc = columns(col_ref, block, group)
            queries = stack_heads(n_ref, block, group, 0, DK)
            keys = stack_heads(n_ref, block, group, H * DK, DK)
            values = stack_heads(n_ref, block, group, 2 * H * DK, DV).astype(F32)
            within, strict = decay_matrix(cum, doc)
            scores = SCALE * mm(queries, keys, ((1,), (1,))) * within
            weighted = mm(keys, keys, ((1,), (1,))) * strict
            dout = stack_heads(dout_ref, block, group, 0, DV)
            dout_wide = dout.astype(F32)
            corrected = cor_ref[block, group]
            cor_wide = corrected.astype(F32)
            wide = (SCALE * a) * dout_wide
            pulled, seen, asked, dk_state, d_kappa = [], [], [], [], []
            update = (d * cor_wide).astype(BF16)
            for h in range(STACK):
                n = group * STACK + h
                state = states_ref[block, n]
                after = dstate[n]
                after_low = after.astype(BF16)
                both = mm(jnp.concatenate([head(keys, h), head(queries, h)], axis=0), state)
                seen.append(both[:BLOCK])
                asked.append(both[BLOCK:])
                pulled.append(mm(head(keys, h), after_low))
                dk_state.append(mm(head(update, h), after_low, ((1,), (1,))))
                total = jnp.sum(
                    jnp.sum(state.astype(F32) * after, axis=0, keepdims=True),
                    axis=1,
                    keepdims=True,
                )
                d_kappa.append(jnp.broadcast_to(total * (1.0 / BLOCK), (BLOCK, 1)))
            pulled, seen, asked, d_kappa = (
                jnp.concatenate(p, axis=0) for p in (pulled, seen, asked, d_kappa)
            )
            d_cor = mm(scores, dout, ((0,), (0,))) + d * pulled
            d_right = mm(inv_ref[block, group], d_cor, ((0,), (0,)))
            scaled = beta * d_right
            d_seen = -a * scaled
            dk_left, dq_left = [], []
            for h in range(STACK):
                n = group * STACK + h
                left = jnp.concatenate([head(keys, h), head(queries, h)], axis=0)
                right = jnp.concatenate([head(d_seen, h), head(wide, h)], axis=0).astype(BF16)
                both = mm(right, states_ref[block, n], ((1,), (1,)))
                dk_left.append(both[:BLOCK])
                dq_left.append(both[BLOCK:])
                dstate[n] = kappa[h * BLOCK : h * BLOCK + 1] * dstate[n] + mm(
                    left, right, ((0,), (0,))
                )
            d_scores = mm(dout, corrected, ((1,), (1,)))
            d_system = -mm(d_right, corrected, ((1,), (1,)))
            to_rows = (SCALE * d_scores * within).astype(BF16)
            by_gram = d_system * weighted
            to_keys = (beta * d_system * strict).astype(BF16)
            dq = jnp.concatenate(dq_left, axis=0) + mm(to_rows, keys)
            dk = (
                jnp.concatenate(dk_left, axis=0)
                + jnp.concatenate(dk_state, axis=0)
                + mm(to_rows, queries, ((0,), (0,)))
                + mm(to_keys, keys)
                + mm(to_keys, keys, ((0,), (0,)))
            )
            store_heads(dn_ref, block, group, 0, DK, dq)
            store_heads(dn_ref, block, group, H * DK, DK, dk)
            store_heads(dn_ref, block, group, 2 * H * DK, DV, scaled)
            spread = d_scores * scores + beta * by_gram
            d_cum = jnp.sum(spread, axis=1, keepdims=True)
            d_beta = jnp.sum(by_gram, axis=1, keepdims=True) + jnp.sum(
                d_right * (values - a * seen), axis=1, keepdims=True
            )
            d_a = jnp.sum(SCALE * dout_wide * asked - scaled * seen, axis=1, keepdims=True)
            d_d = jnp.sum(cor_wide * pulled, axis=1, keepdims=True)
            i = lax.broadcasted_iota(jnp.int32, (ROWS, ROWS), 0)
            j = lax.broadcasted_iota(jnp.int32, (ROWS, ROWS), 1)
            by_column = jnp.sum(spread, axis=0, keepdims=True)
            d_cum = d_cum - jnp.sum(jnp.where(i == j, by_column, 0.0), axis=1, keepdims=True)
            lane = lax.broadcasted_iota(jnp.int32, (BLOCK, 128), 1)
            for f, part in enumerate((d_cum, d_beta, d_a, d_d, d_kappa)):
                for h in range(STACK):
                    packed = jnp.where(lane == f * H + group * STACK + h, head(part, h), packed)
        gfeat_ref[pl.ds(pl.multiple_of(block * BLOCK, BLOCK), BLOCK), :] = packed


def conv_back_kernel(x_ref, cw_ref, mask_ref, dn_ref, dx_ref, dcw_ref):
    length = dn_ref.shape[0]

    def chunk(c, normalise):
        lanes = pl.ds(pl.multiple_of(c * 128, 128), 128)
        masks = conv_masks(mask_ref, length)
        weights = cw_ref[:, lanes]
        taps, z = conv_taps(x_ref[:, lanes].astype(F32), masks, weights)
        gate = jax.nn.sigmoid(z)
        dn = dn_ref[:, lanes]
        if normalise:
            y = z * gate
            r = lax.rsqrt(jnp.sum(y * y, axis=1, keepdims=True) + EPSILON)
            dn = r * dn - y * (r * r * r * jnp.sum(y * dn, axis=1, keepdims=True))
        dz = dn * gate * (1.0 + z * (1.0 - gate))
        edge = jnp.zeros((HALO, 128), F32)
        dx = jnp.concatenate([edge, dz * weights[0:1]], axis=0)
        sums = [jnp.sum(dz * taps[0], axis=0, keepdims=True)]
        for s in range(1, CONV):
            sums.append(jnp.sum(dz * taps[s], axis=0, keepdims=True))
            moved = jnp.concatenate([edge, dz * masks[s - 1] * weights[s : s + 1]], axis=0)
            dx = dx + pltpu.roll(moved, length + HALO - s, 0)
        dx_ref[:, lanes] = dx.astype(BF16)
        dcw_ref[:, lanes] = jnp.concatenate(sums, axis=0)

    qk_cols = 2 * H * DK

    @pl.loop(0, qk_cols // 128)
    def _(c):
        chunk(c, True)

    @pl.loop(qk_cols // 128, x_ref.shape[1] // 128)
    def _(c):
        chunk(c, False)


def call(kernel, outs, scratch, *args):
    return pl.pallas_call(
        kernel,
        out_shape=[jax.ShapeDtypeStruct(s, t) for s, t in outs],
        in_specs=[pl.BlockSpec(memory_space=pltpu.VMEM)] * len(args),
        out_specs=[pl.BlockSpec(memory_space=pltpu.VMEM)] * len(outs),
        scratch_shapes=scratch,
        compiler_params=pltpu.CompilerParams(vmem_limit_bytes=VMEM_BYTES),
        cost_estimate=pl.CostEstimate(flops=1, bytes_accessed=1, transcendentals=0),
    )(*args)


def mixer(x, weights, rates, decay, doc_all, member, sp_size, points):
    length = x.shape[0] - HALO
    blocks = length // BLOCK
    groups = H // STACK
    channels = x.shape[1]
    padded = jnp.concatenate([jnp.full((HALO,), -1, jnp.int32), doc_all])
    near = lax.dynamic_slice_in_dim(padded, member * length, length + HALO, 0)
    docs = near[HALO:]
    masks = jnp.stack(
        [(near[HALO - s : HALO - s + length] == docs).astype(F32) for s in range(1, CONV)]
        + [jnp.zeros((length,), F32)] * (8 - CONV + 1),
        axis=1,
    )
    doc_blocks = docs.reshape(blocks, BLOCK, 1)
    before = near[HALO - 1 : -1].reshape(blocks, BLOCK, 1)[:, :1]
    last = doc_blocks[:, -1:]
    from_before = (doc_blocks == before).astype(F32)
    to_last = (doc_blocks == last).astype(F32)
    kept = (last == before).astype(F32)

    def small(rates, decay):
        beta = jax.nn.sigmoid(rates[:, H:]).reshape(blocks, BLOCK, H)
        log_decay = -jnp.exp(decay[:1]) * jax.nn.softplus(rates[:, :H] + decay[1:])
        i = lax.broadcasted_iota(jnp.int32, (BLOCK, BLOCK), 0)
        j = lax.broadcasted_iota(jnp.int32, (BLOCK, BLOCK), 1)
        cum = jnp.einsum(
            "bih,ij->bjh",
            log_decay.reshape(blocks, BLOCK, H),
            (i <= j).astype(F32),
            precision=lax.Precision.HIGHEST,
        )
        final = cum[:, -1:]
        a = jnp.exp(cum) * from_before
        d = jnp.exp(final - cum) * to_last
        kappa = jnp.broadcast_to(jnp.exp(final) * kept, cum.shape)
        return jnp.concatenate([cum, beta, a, d, kappa], axis=2).reshape(length, 5 * H)

    five, pull_small = jax.vjp(small, rates, decay)
    doc_lanes = jnp.broadcast_to(docs.astype(F32)[:, None], (length, H))
    col = jnp.concatenate([five, doc_lanes, jnp.zeros((length, 128 - 6 * H), F32)], axis=1)

    n_shape = ((length, channels), BF16)
    inv_shape = ((blocks, groups, ROWS, ROWS), F32)
    state_shape = ((H, DK, DV), F32)
    cor_shape = ((blocks, groups, ROWS, ROWS), BF16)
    x = points("conv", x)
    (n,) = call(conv_kernel, [n_shape], [], x, weights, masks)
    n = points("conv_done", n)
    n = points("inverse", n)
    (inv,) = call(inverse_kernel, [inv_shape], [], n, col)
    inv = points("state", inv)
    start = jnp.zeros((H, DK, DV), BF16)
    ahead = [(i, i + 1) for i in range(sp_size - 1)]
    behind = [(i + 1, i) for i in range(sp_size - 1)]
    for _ in range(sp_size - 1):
        (state,) = call(state_kernel, [state_shape], [], n, inv, col, start)
        start = lax.ppermute(state.astype(BF16), "sp", ahead)
    mixed, cor, states = call(
        scan_kernel,
        [((length, H * DV), BF16), cor_shape, ((blocks, H, DK, DV), BF16)],
        [pltpu.VMEM((H, DK, DV), F32)],
        n,
        inv,
        col,
        start,
    )

    def pull(dout):
        dstart = jnp.zeros((H, DK, DV), BF16)
        for _ in range(sp_size - 1):
            (dstate,) = call(
                back_state_kernel, [state_shape], [], n, inv, col, dout, dstart
            )
            dstart = lax.ppermute(points("sent", dstate.astype(BF16)), "sp", behind)
        dstart = points("back", dstart)
        dn, gfeat = call(
            back_kernel,
            [
                ((length, channels), F32),
                ((length, 128), F32),
            ],
            [pltpu.VMEM((H, DK, DV), F32)],
            n,
            inv,
            col,
                dout,
            cor,
            states,
            dstart,
        )
        dn = points("conv_back", dn)
        dx, dcw = call(
            conv_back_kernel,
            [((length + HALO, channels), BF16), ((CONV, channels), F32)],
            [],
            x,
            weights,
            masks,
            dn,
        )
        d_rates, d_decay = pull_small(gfeat[:, : 5 * H])
        from_next = lax.ppermute(dx[:HALO], "sp", behind)
        return dx, from_next, dcw, d_rates, d_decay

    return mixed, pull


def rms_norm(values, scales):
    return values * lax.rsqrt(jnp.mean(values * values, axis=-1, keepdims=True) + EPSILON) * scales


def output_gate(mixed, gate_raw, scales):
    length = mixed.shape[0]
    normed = rms_norm(mixed.reshape(length, H, DV), scales)
    return (normed * jax.nn.silu(gate_raw).reshape(length, H, DV)).reshape(length, H * DV)


def residual_norm(values, attended, scales):
    hidden = values + attended
    return (hidden, rms_norm(hidden, scales))


def after(value, *earlier):
    return lax.optimization_barrier((value,) + earlier)[0] if earlier else value


def swap(value, axis):
    return lax.ppermute(value, axis, [(0, 1), (1, 0)])


def other(first):
    return "sp" if first == "x" else "x"


def pair(axis, mine, theirs, dim):
    first = lax.axis_index(axis) == 0
    return jnp.where(
        first,
        jnp.concatenate([mine, theirs], axis=dim),
        jnp.concatenate([theirs, mine], axis=dim),
    )


def relative_axes(first):
    return ("core", first, other(first))


def place(first, k):
    total = 0
    for shift, axis in zip((2, 1, 0), relative_axes(first)):
        bit = lax.axis_index(axis)
        total = total + (1 << shift) * (1 - bit if (k >> shift) & 1 else bit)
    return total


def reorder(value, first):
    width = value.shape[1] // 8
    return jnp.concatenate(
        [lax.dynamic_slice_in_dim(value, place(first, i) * width, width, 1) for i in range(8)],
        axis=1,
    )


def shifted(value, step):
    count = lax.axis_size("fsdp")
    return lax.ppermute(value, "fsdp", [(i, (i + step) % count) for i in range(count)])


def gather_blocks(piece, *late):
    count, rows = lax.axis_size("fsdp"), piece.shape[0]
    parts = [piece] + [after(shifted(piece, s), *late) for s in range(1, count)]
    line = jnp.concatenate([parts[(count - 1 - i) % count] for i in range(2 * count - 1)], axis=0)
    start = (count - 1 - lax.axis_index("fsdp")) * rows
    return lax.dynamic_slice_in_dim(line, start, count * rows, 0)


def sum_blocks(value):
    total = lax.psum_scatter(value.astype(BF16), "fsdp", scatter_dimension=0, tiled=True)
    if lax.axis_size("hi") > 1:
        total = lax.psum(total, "hi")
    return total


WEIGHT_AXES = ("fsdp", "hi", "x", "core", "sp")


def gather_rows(shard):
    count, own = 1, 0
    for axis in WEIGHT_AXES[1:]:
        count = count * lax.axis_size(axis)
        own = own * lax.axis_size(axis) + lax.axis_index(axis)
    rows = shard.shape[0] // count
    piece = lax.dynamic_slice_in_dim(shard, own * rows, rows, 0)
    return lax.all_gather(piece, WEIGHT_AXES, axis=0, tiled=True)


class ColumnGather:
    def __init__(self, shard, first):
        width = shard.shape[1] // 8
        self.first = first
        self.piece = lax.dynamic_slice_in_dim(shard, place(first, 0) * width, width, 1)

    def blocks(self, earlier, late):
        self.held = gather_blocks(after(self.piece, *earlier), late)
        return self.held

    def second(self, *earlier):
        held = after(self.held, *earlier) if earlier else self.held
        self.held = jnp.concatenate([held, swap(held, other(self.first))], axis=1)
        return self.held

    def third(self, *earlier):
        held = after(self.held, *earlier) if earlier else self.held
        self.held = jnp.concatenate([held, swap(held, self.first)], axis=1)
        return self.held

    def full(self):
        return self.held, swap(self.held, "core")


def dot_columns(values, halves_of):
    parts = [jnp.dot(values, w, preferred_element_type=F32) for w in halves_of]
    return jnp.concatenate(parts, axis=1)


def dot_back(grads, halves_of):
    half = grads.shape[1] // 2
    return jnp.einsum(
        "tf,df->td", grads[:, :half], halves_of[0], preferred_element_type=F32
    ) + jnp.einsum("tf,df->td", grads[:, half:], halves_of[1], preferred_element_type=F32)


def grad_dot(left, right):
    return jnp.einsum("td,tf->df", left, right, preferred_element_type=F32)


class ColumnSum:
    def __init__(self, left, right, first):
        self.left, self.right, self.first = left, right, first
        self.width = right.shape[1] // 8
        self.from_core = swap(grad_dot(left, right[:, 4 * self.width :]).astype(BF16), "core")

    def second(self):
        width = self.width
        outgoing = grad_dot(self.left, self.right[:, 2 * width : 4 * width])
        self.outgoing = (outgoing + self.from_core[:, 2 * width :].astype(F32)).astype(BF16)
        self.from_first = swap(self.outgoing, self.first)
        return self.outgoing

    def third(self, *late):
        width = self.width
        self.from_first = after(self.from_first, *late)
        self.outgoing = (
            grad_dot(self.left, self.right[:, width : 2 * width])
            + self.from_core[:, width : 2 * width].astype(F32)
            + self.from_first[:, width:].astype(F32)
        ).astype(BF16)
        self.from_second = swap(self.outgoing, other(self.first))
        return self.outgoing

    def own(self):
        width = self.width
        return (
            grad_dot(self.left, self.right[:, :width])
            + self.from_core[:, :width].astype(F32)
            + self.from_first[:, :width].astype(F32)
            + self.from_second.astype(F32)
        )


def spread(blocks):
    held = jnp.concatenate(blocks, axis=0)[None]
    for axis in ("sp", "x"):
        held = jnp.concatenate([held, swap(held, axis)], axis=0)
    return held, swap(held, "core")


def spread_aside(blocks):
    every = lax.all_gather(jnp.concatenate(blocks, axis=0), ("x", "core", "sp"), axis=0)
    return every[:4], every[4:]


def unpack_kernel(segments, count, places_ref, *refs):
    sources, outs = refs[:count], refs[count:]
    for source, row, out, column, rows, blocks, way in segments:
        for k in range(8):
            piece = sources[2 * source + k // 4]
            at = pl.multiple_of(column + places_ref[2 * way, k] * (128 * blocks), 128)
            down = pl.multiple_of(places_ref[2 * way + 1, k] * rows, 16)
            for j in range(blocks):
                outs[out][pl.ds(down, rows), pl.ds(at + 128 * j, 128)] = piece[
                    k % 4, row + j * rows : row + (j + 1) * rows
                ].astype(F32)


def unpack(places, segments, sources, shapes):
    count = len(sources)
    return pl.pallas_call(
        functools.partial(unpack_kernel, segments, count),
        out_shape=[jax.ShapeDtypeStruct(s, F32) for s in shapes],
        in_specs=[pl.BlockSpec(memory_space=pltpu.SMEM)]
        + [pl.BlockSpec(memory_space=pltpu.VMEM)] * count,
        out_specs=[pl.BlockSpec(memory_space=pltpu.VMEM)] * len(shapes),
        compiler_params=pltpu.CompilerParams(vmem_limit_bytes=VMEM_BYTES),
    )(places, *sources)


def spread_places():
    core, x, y = lax.axis_index("core"), lax.axis_index("x"), lax.axis_index("sp")
    table = [[] for _ in range(12)]
    for k in range(8):
        c, d, e = (
            1 - bit if (k >> shift) & 1 else bit for shift, bit in ((2, core), (1, x), (0, y))
        )
        for line, value in enumerate((4 * c + 2 * d + e, 0, 4 * c + 2 * e + d, 0, 2 * c + d, e)):
            table[line].append(jnp.asarray(value, jnp.int32))
        d, c, e = (k >> 2) & 1, (k >> 1) & 1, k & 1
        for line, value in enumerate((4 * c + 2 * d + e, 0, 4 * c + 2 * e + d, 0, 2 * c + d, e)):
            table[6 + line].append(jnp.asarray(value, jnp.int32))
    return jnp.stack([jnp.stack(line) for line in table])


def by_half(values):
    blocks = values.reshape(values.shape[0], lax.axis_size("fsdp"), 2, -1)
    low = blocks[:, :, 0].reshape(values.shape[0], -1)
    high = blocks[:, :, 1].reshape(values.shape[0], -1)
    first = lax.axis_index("sp") == 0
    return jnp.concatenate(
        [jnp.where(first, low, high), jnp.where(first, high, low)], axis=1
    )


class HalfSum:
    def __init__(self, left, right):
        self.left, self.first = left, "x"
        self.width = width = right.shape[1] // 4
        core, x = lax.axis_index("core"), lax.axis_index("x")

        def half(c):
            return jnp.concatenate(
                [
                    lax.dynamic_slice_in_dim(right, (2 * c + d) * width, width, 1)
                    for d in (x, 1 - x)
                ],
                axis=1,
            )

        self.near, far_core = half(core), half(1 - core)
        self.rows = left.shape[1] // 2
        self.from_core = swap(grad_dot(left, far_core).astype(BF16), "core")

    def second(self):
        width = self.width
        outgoing = grad_dot(self.left, self.near[:, width:])
        self.outgoing = (outgoing + self.from_core[:, width:].astype(F32)).astype(BF16)
        self.from_x = swap(self.outgoing, "x")
        return self.outgoing

    def third(self):
        rows, width = self.rows, self.width
        self.outgoing = (
            grad_dot(self.left[:, rows:], self.near[:, :width])
            + self.from_core[rows:, :width].astype(F32)
            + self.from_x[rows:].astype(F32)
        ).astype(BF16)
        self.from_y = swap(self.outgoing, "sp")
        return self.outgoing

    def own(self):
        rows, width = self.rows, self.width
        return (
            grad_dot(self.left[:, :rows], self.near[:, :width])
            + self.from_core[:rows, :width].astype(F32)
            + self.from_x[:rows].astype(F32)
            + self.from_y.astype(F32)
        )


def narrow(value):
    return jnp.concatenate(
        [value[:, i : i + 128] for i in range(0, value.shape[1], 128)], axis=0
    )


def pack_small(parts, width):
    flat = jnp.concatenate([p.reshape(-1) for p in parts])
    return jnp.pad(flat, (0, -flat.shape[0] % (16 * width))).reshape(-1, width)


def unpack_small(every, parts):
    out, start = [], 0
    for p in parts:
        out.append(every[:, start : start + p.size].reshape((-1,) + p.shape))
        start += p.size
    return out


def sum_small(parts, *earlier):
    flat = jnp.concatenate([p.reshape(-1) for p in parts])
    size = flat.shape[0]
    flat = after(jnp.pad(flat, (0, -size % 1024)).reshape(-1, 128), *earlier)
    for axis in ("core", "x", "sp"):
        flat = flat + swap(flat, axis)
    members = lax.axis_size("fsdp")
    for bit in range(members.bit_length() - 1):
        flat = flat + lax.ppermute(flat, "fsdp", [(i, i ^ (1 << bit)) for i in range(members)])
    if lax.axis_size("hi") > 1:
        flat = lax.psum(flat, "hi")
    total = flat.reshape(-1)
    out, start = [], 0
    for p in parts:
        out.append(total[start : start + p.size].reshape(p.shape))
        start += p.size
    return out


def own_part(value, axis):
    size = value.shape[axis] // lax.axis_size("fsdp")
    return lax.dynamic_slice_in_dim(value, lax.axis_index("fsdp") * size, size, axis)


def body(
    tokens,
    cotangent,
    doc_lengths,
    input_weight,
    rate_weight,
    conv_weight,
    head_decay,
    mixer_gain,
    heads_gain,
    output_weight,
    feed_gain,
    up_weight,
    down_weight,
):
    length = tokens.shape[0]
    sp_size = lax.axis_size("sp")
    member = lax.axis_index("sp")
    qkv_cols = H * (2 * DK + DV)
    qk_cols = 2 * H * DK
    members = lax.axis_size("fsdp")
    qk_way = ColumnGather(input_weight[:, :qk_cols], "x")
    v_way = ColumnGather(input_weight[:, qk_cols:qkv_cols], "sp")
    gate_way = ColumnGather(input_weight[:, qkv_cols:], "x")
    down_way = ColumnGather(down_weight, "x")
    pair_rows, pair_cols = qk_way.piece.shape[0], 2 * qk_way.piece.shape[1]
    smalls = (rate_weight, conv_weight, head_decay, mixer_gain, heads_gain, feed_gain)
    first_load = jnp.concatenate(
        [
            jnp.concatenate([qk_way.piece, v_way.piece], axis=1),
            pack_small(smalls, pair_cols),
        ],
        axis=0,
    )
    first_all = gather_blocks(first_load).reshape(members, -1, pair_cols)
    both = first_all[:, :pair_rows].reshape(-1, pair_cols)
    qk_way.held, v_way.held = both[:, : pair_cols // 2], both[:, pair_cols // 2 :]
    rate_all, conv_all, decay_all, mixer_all, heads_all, feed_all = unpack_small(
        first_all[:, pair_rows:].reshape(members, -1), smalls
    )
    qkv_second = (qk_way.second(), v_way.second())
    qkv_third = (qk_way.third(), v_way.third())
    qk_full, v_full = qk_way.full(), v_way.full()
    out_full = gather_rows(output_weight)
    up_full = gather_rows(up_weight)
    rate_full = jnp.swapaxes(rate_all.reshape(-1, H, 2), 1, 2).reshape(-1, 2 * H)
    conv_full = jnp.swapaxes(conv_all, 0, 1).reshape(CONV, -1).astype(F32)
    decay_full = jnp.swapaxes(decay_all, 0, 1).reshape(2, H).astype(F32)
    mixer_scale = mixer_all.reshape(-1).astype(F32)
    heads_scale = heads_all.reshape(-1).astype(F32)
    feed_scale = feed_all.reshape(-1).astype(F32)

    def points(name, value):
        if name == "conv":
            gate_way.blocks(qkv_third, value)
            gate_way.second()
            x_ready.append(value)
            return value
        if name == "conv_done":
            down_way.blocks((x_ready[0],), value)
            return value
        if name == "inverse":
            value = after(value, gate_way.held, down_way.held)
            gate_way.third(value)
            down_way.second(value)
            return value
        if name == "state":
            value = after(value, gate_way.held, down_way.held)
            down_way.third(value)
            return value
        if name == "sent":
            for key in ("out", "gate"):
                sums[key].third(value)
            return value
        if name == "back":
            return after(value, sums["down"].third())
        if name == "conv_back":
            for key in ("out", "gate"):
                sums[key].from_second = after(sums[key].from_second, value)
            owns.extend(sums[key].own().astype(BF16) for key in ("down", "out", "gate"))
            return after(value, *owns)
        return value

    sums, x_ready, owns = {}, [], []

    ends = jnp.cumsum(doc_lengths[0])
    positions = lax.broadcasted_iota(jnp.int32, (length * sp_size, 1), 0)
    doc_ids = jnp.sum((positions >= ends[None, :]).astype(jnp.int32), axis=1)

    ahead = [(i, i + 1) for i in range(sp_size - 1)]
    halo = lax.ppermute(tokens[-HALO:], "sp", ahead)
    x_float = tokens.astype(F32)
    normed, pull_norm = jax.vjp(rms_norm, x_float, mixer_scale)
    normed_low = normed.astype(BF16)
    halo_low = rms_norm(halo.astype(F32), mixer_scale).astype(BF16)
    normed_more = jnp.concatenate([halo_low, normed_low], axis=0)
    qkv = jnp.concatenate(
        [
            reorder(dot_columns(normed_more, qk_full).astype(BF16), "x"),
            reorder(dot_columns(normed_more, v_full).astype(BF16), "sp"),
        ],
        axis=1,
    )
    rate_raw = jnp.dot(normed_low, rate_full, preferred_element_type=F32)
    rates = rate_raw.astype(BF16).astype(F32)
    mixed, pull_mix = mixer(qkv, conv_full, rates, decay_full, doc_ids, member, sp_size, points)
    gate_full, down_full = gate_way.full(), down_way.full()
    gate_raw = reorder(dot_columns(normed_low, gate_full), "x")
    gated, pull_gate = jax.vjp(output_gate, mixed.astype(F32), gate_raw, heads_scale)
    gated_low = gated.astype(BF16)
    attended = jnp.dot(gated_low, out_full, preferred_element_type=F32)
    (hidden, normed_two), pull_resid = jax.vjp(residual_norm, x_float, attended, feed_scale)
    two_low = normed_two.astype(BF16)
    gate_up = jnp.dot(two_low, up_full, preferred_element_type=F32)

    def feed_act(gate_up):
        half = gate_up.shape[1] // 2
        return jax.nn.silu(gate_up[:, :half]) * gate_up[:, half:]

    activated, pull_act = jax.vjp(feed_act, gate_up)
    act_low = activated.astype(BF16)
    block_out = (hidden + reorder(dot_columns(act_low, down_full), "x")).astype(BF16)
    cot_rel = reorder(cotangent, "x")
    sums["down"] = ColumnSum(act_low, cot_rel, "x")
    d_act = dot_back(cot_rel, down_full)
    d_gu_low = pull_act(d_act)[0].astype(BF16)
    sums["up"] = HalfSum(by_half(two_low), d_gu_low)
    d_gu_low = after(d_gu_low, sums["down"].second())
    d_two = jnp.einsum("tf,df->td", d_gu_low, up_full, preferred_element_type=F32)
    d_resid, d_attended, feed_grad = pull_resid((cotangent.astype(F32), d_two))
    d_att_low = d_attended.astype(BF16)
    d_att_rel = reorder(d_att_low, "sp")
    sums["out"] = ColumnSum(gated_low, d_att_rel, "sp")
    d_gated = jnp.einsum("td,ed->te", d_att_low, out_full, preferred_element_type=F32)
    d_mixed, d_gate, heads_grad = pull_gate(d_gated)
    d_gate_low = d_gate.astype(BF16)
    d_gate_rel = reorder(d_gate_low, "x")
    sums["gate"] = ColumnSum(normed_low, d_gate_rel, "x")
    d_mixed_low = after(
        d_mixed.astype(BF16), *(sums[key].second() for key in ("up", "out", "gate"))
    )
    d_more, from_next, conv_grad, d_rates, decay_grad = pull_mix(d_mixed_low)
    edge = jnp.pad(from_next.astype(F32), ((length - HALO, 0), (0, 0)))
    d_qkv = (d_more[HALO:].astype(F32) + edge).astype(BF16)
    d_rate_low = d_rates.astype(BF16)
    d_qk_rel = reorder(d_qkv[:, :qk_cols], "x")
    d_v_rel = reorder(d_qkv[:, qk_cols:], "sp")
    sums["qk"] = ColumnSum(normed_low, d_qk_rel, "x")
    sums["v"] = ColumnSum(normed_low, d_v_rel, "sp")
    sums["up"].third()
    sums["up"].from_y = after(sums["up"].from_y, sums["qk"].second(), sums["v"].second())
    for key in ("qk", "v"):
        sums[key].third()
    places = spread_places()
    blocks = [sum_blocks(own) for own in owns]
    down_rows, out_rows = blocks[0].shape[0], blocks[1].shape[0]
    early_sums = spread_aside([narrow(block) for block in blocks])
    down_shard, output_shard = unpack(
        places,
        [(0, 0, 0, 0, down_rows, 1, 3), (0, down_rows, 1, 0, out_rows, 1, 4)],
        early_sums,
        [down_weight.shape, output_weight.shape],
    )
    up_block = sum_blocks(sums["up"].own())
    (up_shard,) = unpack(
        places,
        [(0, 0, 0, 0, up_block.shape[0], up_block.shape[1] // 128, 5)],
        spread_aside([narrow(up_block)]),
        [up_weight.shape],
    )
    late_block = sum_blocks(jnp.concatenate([sums["qk"].own(), sums["v"].own()], axis=1))
    rows, wide = late_block.shape[0], late_block.shape[1] // 256
    gate_wide = blocks[2].shape[1] // 128
    (input_shard,) = unpack(
        places,
        [
            (0, 0, 0, 0, rows, wide, 0),
            (0, wide * rows, 0, qk_cols, rows, wide, 1),
            (1, down_rows + out_rows, 0, qkv_cols, rows, gate_wide, 3),
        ],
        spread([narrow(late_block)]) + early_sums,
        [input_weight.shape],
    )
    rate_grad = jnp.einsum("td,tf->df", normed_low, d_rate_low, preferred_element_type=F32)
    d_normed = dot_back(d_qk_rel, qk_full) + dot_back(d_v_rel, v_full)
    d_normed = d_normed + dot_back(d_gate_rel, gate_full)
    d_normed = d_normed + jnp.einsum(
        "tf,df->td", d_rate_low, rate_full, preferred_element_type=F32
    )
    d_front, mixer_grad = pull_norm(d_normed)
    tokens_grad = (d_resid + d_front).astype(BF16)
    rate_sum, conv_sum, decay_sum, mixer_sum, heads_sum, feed_sum = sum_small(
        (rate_grad, conv_grad, decay_grad, mixer_grad, heads_grad, feed_grad),
        sums["qk"].outgoing,
        sums["v"].outgoing,
    )
    return (
        block_out,
        tokens_grad,
        input_shard,
        own_part(jnp.swapaxes(rate_sum.reshape(-1, 2, H), 1, 2).reshape(-1, 2 * H), 0),
        own_part(conv_sum, 1),
        own_part(decay_sum, 1),
        own_part(mixer_sum, 0),
        own_part(heads_sum, 0),
        output_shard,
        own_part(feed_sum, 0),
        up_shard,
        down_shard,
    )


def solution(mesh):
    dp, fsdp, sp = (mesh.shape[axis] for axis in ("dp", "fsdp", "sp"))
    dp_axes = ("hi", "x", "core")
    cut = jax.sharding.Mesh(
        mesh.devices.reshape(dp // 4, 2, 2, fsdp, sp), dp_axes + ("fsdp", "sp")
    )
    rows = P(dp_axes + ("fsdp", "sp"), None)
    split = P("fsdp", None)
    return jax.shard_map(
        body,
        mesh=cut,
        in_specs=(
            rows,
            rows,
            P(dp_axes + ("fsdp",), None),
            split,
            split,
            P(None, "fsdp"),
            P(None, "fsdp"),
            P("fsdp"),
            P("fsdp"),
            split,
            P("fsdp"),
            split,
            split,
        ),
        out_specs=(
            rows,
            rows,
            split,
            split,
            P(None, "fsdp"),
            P(None, "fsdp"),
            P("fsdp"),
            P("fsdp"),
            split,
            P("fsdp"),
            split,
            split,
        ),
        check_vma=False,
    )
```

```python
import functools
import jax
import jax.numpy as jnp
from jax import lax
from jax.experimental import pallas as pl
from jax.experimental.pallas import tpu as pltpu
from jax.sharding import PartitionSpec as P

H = 8
DK = 128
DV = 256
CONV = 4
BLOCK = 64
EPSILON = 1e-06
HALO = 16
STACK = 4
ROWS = STACK * BLOCK
SCALE = DK ** (-0.5)
VMEM_BYTES = 56 * 1024 * 1024
F32 = jnp.float32
BF16 = jnp.bfloat16


def mm(a, b, dims=((1,), (0,))):
    return lax.dot_general(
        a.astype(BF16), b.astype(BF16), (dims, ((), ())), preferred_element_type=F32
    )


def halves(a):
    high = a.astype(BF16)
    return high, (a - high.astype(F32)).astype(BF16)


def mm_fine(a, b):
    (ah, al), (bh, bl) = a, b
    return mm(ah, bh) + (mm(ah, bl) + mm(al, bh))


def stack_heads(ref, block, group, base, width):
    rows = pl.ds(pl.multiple_of(block * BLOCK, BLOCK), BLOCK)
    return jnp.concatenate(
        [
            ref[rows, base + (group * STACK + h) * width : base + (group * STACK + h + 1) * width]
            for h in range(STACK)
        ],
        axis=0,
    )


def store_heads(ref, block, group, base, width, value):
    rows = pl.ds(pl.multiple_of(block * BLOCK, BLOCK), BLOCK)
    for h in range(STACK):
        start = base + (group * STACK + h) * width
        ref[rows, start : start + width] = value[h * BLOCK : (h + 1) * BLOCK].astype(ref.dtype)


def head(value, h):
    return value[h * BLOCK : (h + 1) * BLOCK]


def columns(feat_ref, block, group):
    packed = feat_ref[pl.ds(pl.multiple_of(block * BLOCK, BLOCK), BLOCK), :]
    return [
        jnp.concatenate(
            [
                packed[:, f * H + group * STACK + h : f * H + group * STACK + h + 1]
                for h in range(STACK)
            ],
            axis=0,
        )
        for f in range(6)
    ]


def decay_matrix(cum, doc):
    i = lax.broadcasted_iota(jnp.int32, (ROWS, ROWS), 0)
    j = lax.broadcasted_iota(jnp.int32, (ROWS, ROWS), 1)
    cum_row, doc_row = (
        jnp.sum(jnp.where(i == j, c, 0.0), axis=0, keepdims=True) for c in (cum, doc)
    )
    inside = ((i // BLOCK) == (j // BLOCK)) & (i >= j) & (doc == doc_row)
    decay = jnp.exp(jnp.where(inside, cum - cum_row, -1e30))
    return decay, jnp.where(i > j, decay, 0.0)


def unit_inverses(lowers):
    i = lax.broadcasted_iota(jnp.int32, (ROWS, ROWS), 0)
    j = lax.broadcasted_iota(jnp.int32, (ROWS, ROWS), 1)
    apart = jnp.bitwise_xor(i, j)
    inverses = [
        jnp.where(i == j, 1.0, 0.0) - jnp.where(apart == 1, lower, 0.0) for lower in lowers
    ]
    size = 2
    while size < BLOCK:
        cross = (apart >= size) & (apart < 2 * size)
        parts = [halves(inverse) for inverse in inverses]
        right = [
            halves(mm_fine(halves(jnp.where(cross, lower, 0.0)), part))
            for lower, part in zip(lowers, parts)
        ]
        inverses = [
            inverse - mm_fine(part, r) for inverse, part, r in zip(inverses, parts, right)
        ]
        size *= 2
    return inverses


def conv_taps(x, masks, weights):
    taps = [x[HALO:]]
    for s in range(1, CONV):
        taps.append(pltpu.roll(x, s, 0)[HALO:] * masks[s - 1])
    z = taps[0] * weights[0:1]
    for s in range(1, CONV):
        z = z + taps[s] * weights[s : s + 1]
    return taps, z


def conv_masks(mask_ref, length):
    return [
        jnp.broadcast_to(mask_ref[:, s : s + 1], (length, 128)) for s in range(CONV - 1)
    ]


def conv_kernel(x_ref, cw_ref, mask_ref, n_ref):
    length = n_ref.shape[0]
    qk_cols = 2 * H * DK

    def chunk(c, normalise):
        lanes = pl.ds(pl.multiple_of(c * 128, 128), 128)
        masks = conv_masks(mask_ref, length)
        _, z = conv_taps(x_ref[:, lanes].astype(F32), masks, cw_ref[:, lanes])
        y = z * jax.nn.sigmoid(z)
        if normalise:
            y = y * lax.rsqrt(jnp.sum(y * y, axis=1, keepdims=True) + EPSILON)
        n_ref[:, lanes] = y.astype(BF16)

    @pl.loop(0, qk_cols // 128)
    def _(c):
        chunk(c, True)

    @pl.loop(qk_cols // 128, x_ref.shape[1] // 128)
    def _(c):
        chunk(c, False)


def inverse_kernel(n_ref, col_ref, inv_ref):
    @pl.loop(0, n_ref.shape[0] // BLOCK)
    def _(block):
        lowers = []
        for group in range(H // STACK):
            cum, beta, _, _, _, doc = columns(col_ref, block, group)
            keys = stack_heads(n_ref, block, group, H * DK, DK)
            _, strict = decay_matrix(cum, doc)
            lowers.append(beta * mm(keys, keys, ((1,), (1,))) * strict)
        for group, inverse in enumerate(unit_inverses(lowers)):
            inv_ref[block, group] = inverse


def state_steps(n_ref, inv_ref, col_ref, state_ref):
    @pl.loop(0, n_ref.shape[0] // BLOCK)
    def _(block):
        for group in range(H // STACK):
            _, beta, a, d, kappa, _ = columns(col_ref, block, group)
            keys = stack_heads(n_ref, block, group, H * DK, DK)
            values = stack_heads(n_ref, block, group, 2 * H * DK, DV).astype(F32)
            seen = jnp.concatenate(
                [mm(head(keys, h), state_ref[group * STACK + h]) for h in range(STACK)], axis=0
            )
            corrected = mm(inv_ref[block, group], beta * (values - a * seen))
            update = d * corrected
            for h in range(STACK):
                n = group * STACK + h
                state_ref[n] = kappa[h * BLOCK : h * BLOCK + 1] * state_ref[n] + mm(
                    head(keys, h), head(update, h), ((0,), (0,))
                )


def state_kernel(n_ref, inv_ref, col_ref, start_ref, state_ref):
    state_ref[...] = start_ref[...].astype(F32)
    state_steps(n_ref, inv_ref, col_ref, state_ref)


def scan_kernel(n_ref, inv_ref, col_ref, start_ref, out_ref, cor_ref, states_ref, state):
    state[...] = start_ref[...].astype(F32)

    @pl.loop(0, n_ref.shape[0] // BLOCK)
    def _(block):
        for group in range(H // STACK):
            cum, beta, a, d, kappa, doc = columns(col_ref, block, group)
            queries = stack_heads(n_ref, block, group, 0, DK)
            keys = stack_heads(n_ref, block, group, H * DK, DK)
            values = stack_heads(n_ref, block, group, 2 * H * DK, DV).astype(F32)
            within, _ = decay_matrix(cum, doc)
            scores = SCALE * mm(queries, keys, ((1,), (1,))) * within
            both = []
            for h in range(STACK):
                low = state[group * STACK + h].astype(BF16)
                states_ref[block, group * STACK + h] = low
                both.append(mm(jnp.concatenate([head(keys, h), head(queries, h)], axis=0), low))
            seen = jnp.concatenate([b[:BLOCK] for b in both], axis=0)
            asked = jnp.concatenate([b[BLOCK:] for b in both], axis=0)
            corrected = mm(inv_ref[block, group], beta * (values - a * seen))
            cor_ref[block, group] = corrected.astype(BF16)
            out = (SCALE * a) * asked + mm(scores, corrected)
            store_heads(out_ref, block, group, 0, DV, out)
            update = d * corrected
            for h in range(STACK):
                n = group * STACK + h
                state[n] = kappa[h * BLOCK : h * BLOCK + 1] * state[n] + mm(
                    head(keys, h), head(update, h), ((0,), (0,))
                )


def back_state_kernel(n_ref, inv_ref, col_ref, dout_ref, start_ref, dstate_ref):
    blocks = n_ref.shape[0] // BLOCK
    dstate_ref[...] = start_ref[...].astype(F32)

    @pl.loop(0, blocks)
    def _(step):
        block = blocks - 1 - step
        for group in range(H // STACK):
            cum, beta, a, d, kappa, doc = columns(col_ref, block, group)
            queries = stack_heads(n_ref, block, group, 0, DK)
            keys = stack_heads(n_ref, block, group, H * DK, DK)
            within, _ = decay_matrix(cum, doc)
            scores = SCALE * mm(queries, keys, ((1,), (1,))) * within
            dout = stack_heads(dout_ref, block, group, 0, DV)
            wide = (SCALE * a) * dout.astype(F32)
            pulled = jnp.concatenate(
                [mm(head(keys, h), dstate_ref[group * STACK + h]) for h in range(STACK)], axis=0
            )
            d_cor = mm(scores, dout, ((0,), (0,))) + d * pulled
            d_right = mm(inv_ref[block, group], d_cor, ((0,), (0,)))
            d_seen = (-a * beta) * d_right
            for h in range(STACK):
                n = group * STACK + h
                left = jnp.concatenate([head(keys, h), head(queries, h)], axis=0)
                right = jnp.concatenate([head(d_seen, h), head(wide, h)], axis=0)
                dstate_ref[n] = kappa[h * BLOCK : h * BLOCK + 1] * dstate_ref[n] + mm(
                    left, right, ((0,), (0,))
                )


def back_kernel(
    n_ref,
    inv_ref,
    col_ref,

    dout_ref,
    cor_ref,
    states_ref,
    start_ref,
    dn_ref,
    gfeat_ref,
    dstate,
):
    length = n_ref.shape[0]
    blocks = length // BLOCK
    dstate[...] = start_ref[...].astype(F32)

    @pl.loop(0, blocks)
    def _(step):
        block = blocks - 1 - step
        packed = jnp.zeros((BLOCK, 128), F32)
        for group in range(H // STACK):
            cum, beta, a, d, kappa, doc = columns(col_ref, block, group)
            queries = stack_heads(n_ref, block, group, 0, DK)
            keys = stack_heads(n_ref, block, group, H * DK, DK)
            values = stack_heads(n_ref, block, group, 2 * H * DK, DV).astype(F32)
            within, strict = decay_matrix(cum, doc)
            scores = SCALE * mm(queries, keys, ((1,), (1,))) * within
            weighted = mm(keys, keys, ((1,), (1,))) * strict
            dout = stack_heads(dout_ref, block, group, 0, DV)
            dout_wide = dout.astype(F32)
            corrected = cor_ref[block, group]
            cor_wide = corrected.astype(F32)
            wide = (SCALE * a) * dout_wide
            pulled, seen, asked, dk_state, d_kappa = [], [], [], [], []
            update = (d * cor_wide).astype(BF16)
            for h in range(STACK):
                n = group * STACK + h
                state = states_ref[block, n]
                after = dstate[n]
                after_low = after.astype(BF16)
                both = mm(jnp.concatenate([head(keys, h), head(queries, h)], axis=0), state)
                seen.append(both[:BLOCK])
                asked.append(both[BLOCK:])
                pulled.append(mm(head(keys, h), after_low))
                dk_state.append(mm(head(update, h), after_low, ((1,), (1,))))
                total = jnp.sum(
                    jnp.sum(state.astype(F32) * after, axis=0, keepdims=True),
                    axis=1,
                    keepdims=True,
                )
                d_kappa.append(jnp.broadcast_to(total * (1.0 / BLOCK), (BLOCK, 1)))
            pulled, seen, asked, d_kappa = (
                jnp.concatenate(p, axis=0) for p in (pulled, seen, asked, d_kappa)
            )
            d_cor = mm(scores, dout, ((0,), (0,))) + d * pulled
            d_right = mm(inv_ref[block, group], d_cor, ((0,), (0,)))
            scaled = beta * d_right
            d_seen = -a * scaled
            dk_left, dq_left = [], []
            for h in range(STACK):
                n = group * STACK + h
                left = jnp.concatenate([head(keys, h), head(queries, h)], axis=0)
                right = jnp.concatenate([head(d_seen, h), head(wide, h)], axis=0).astype(BF16)
                both = mm(right, states_ref[block, n], ((1,), (1,)))
                dk_left.append(both[:BLOCK])
                dq_left.append(both[BLOCK:])
                dstate[n] = kappa[h * BLOCK : h * BLOCK + 1] * dstate[n] + mm(
                    left, right, ((0,), (0,))
                )
            d_scores = mm(dout, corrected, ((1,), (1,)))
            d_system = -mm(d_right, corrected, ((1,), (1,)))
            to_rows = (SCALE * d_scores * within).astype(BF16)
            by_gram = d_system * weighted
            to_keys = (beta * d_system * strict).astype(BF16)
            dq = jnp.concatenate(dq_left, axis=0) + mm(to_rows, keys)
            dk = (
                jnp.concatenate(dk_left, axis=0)
                + jnp.concatenate(dk_state, axis=0)
                + mm(to_rows, queries, ((0,), (0,)))
                + mm(to_keys, keys)
                + mm(to_keys, keys, ((0,), (0,)))
            )
            store_heads(dn_ref, block, group, 0, DK, dq)
            store_heads(dn_ref, block, group, H * DK, DK, dk)
            store_heads(dn_ref, block, group, 2 * H * DK, DV, scaled)
            spread = d_scores * scores + beta * by_gram
            d_cum = jnp.sum(spread, axis=1, keepdims=True)
            d_beta = jnp.sum(by_gram, axis=1, keepdims=True) + jnp.sum(
                d_right * (values - a * seen), axis=1, keepdims=True
            )
            d_a = jnp.sum(SCALE * dout_wide * asked - scaled * seen, axis=1, keepdims=True)
            d_d = jnp.sum(cor_wide * pulled, axis=1, keepdims=True)
            i = lax.broadcasted_iota(jnp.int32, (ROWS, ROWS), 0)
            j = lax.broadcasted_iota(jnp.int32, (ROWS, ROWS), 1)
            by_column = jnp.sum(spread, axis=0, keepdims=True)
            d_cum = d_cum - jnp.sum(jnp.where(i == j, by_column, 0.0), axis=1, keepdims=True)
            lane = lax.broadcasted_iota(jnp.int32, (BLOCK, 128), 1)
            for f, part in enumerate((d_cum, d_beta, d_a, d_d, d_kappa)):
                for h in range(STACK):
                    packed = jnp.where(lane == f * H + group * STACK + h, head(part, h), packed)
        gfeat_ref[pl.ds(pl.multiple_of(block * BLOCK, BLOCK), BLOCK), :] = packed


def conv_back_kernel(x_ref, cw_ref, mask_ref, dn_ref, dx_ref, dcw_ref):
    length = dn_ref.shape[0]

    def chunk(c, normalise):
        lanes = pl.ds(pl.multiple_of(c * 128, 128), 128)
        masks = conv_masks(mask_ref, length)
        weights = cw_ref[:, lanes]
        taps, z = conv_taps(x_ref[:, lanes].astype(F32), masks, weights)
        gate = jax.nn.sigmoid(z)
        dn = dn_ref[:, lanes]
        if normalise:
            y = z * gate
            r = lax.rsqrt(jnp.sum(y * y, axis=1, keepdims=True) + EPSILON)
            dn = r * dn - y * (r * r * r * jnp.sum(y * dn, axis=1, keepdims=True))
        dz = dn * gate * (1.0 + z * (1.0 - gate))
        edge = jnp.zeros((HALO, 128), F32)
        dx = jnp.concatenate([edge, dz * weights[0:1]], axis=0)
        sums = [jnp.sum(dz * taps[0], axis=0, keepdims=True)]
        for s in range(1, CONV):
            sums.append(jnp.sum(dz * taps[s], axis=0, keepdims=True))
            moved = jnp.concatenate([edge, dz * masks[s - 1] * weights[s : s + 1]], axis=0)
            dx = dx + pltpu.roll(moved, length + HALO - s, 0)
        dx_ref[:, lanes] = dx.astype(BF16)
        dcw_ref[:, lanes] = jnp.concatenate(sums, axis=0)

    qk_cols = 2 * H * DK

    @pl.loop(0, qk_cols // 128)
    def _(c):
        chunk(c, True)

    @pl.loop(qk_cols // 128, x_ref.shape[1] // 128)
    def _(c):
        chunk(c, False)


def call(kernel, outs, scratch, *args):
    return pl.pallas_call(
        kernel,
        out_shape=[jax.ShapeDtypeStruct(s, t) for s, t in outs],
        in_specs=[pl.BlockSpec(memory_space=pltpu.VMEM)] * len(args),
        out_specs=[pl.BlockSpec(memory_space=pltpu.VMEM)] * len(outs),
        scratch_shapes=scratch,
        compiler_params=pltpu.CompilerParams(vmem_limit_bytes=VMEM_BYTES),
        cost_estimate=pl.CostEstimate(flops=1, bytes_accessed=1, transcendentals=0),
    )(*args)


def mixer(x, weights, rates, decay, doc_all, member, sp_size, points):
    length = x.shape[0] - HALO
    blocks = length // BLOCK
    groups = H // STACK
    channels = x.shape[1]
    padded = jnp.concatenate([jnp.full((HALO,), -1, jnp.int32), doc_all])
    near = lax.dynamic_slice_in_dim(padded, member * length, length + HALO, 0)
    docs = near[HALO:]
    masks = jnp.stack(
        [(near[HALO - s : HALO - s + length] == docs).astype(F32) for s in range(1, CONV)]
        + [jnp.zeros((length,), F32)] * (8 - CONV + 1),
        axis=1,
    )
    doc_blocks = docs.reshape(blocks, BLOCK, 1)
    before = near[HALO - 1 : -1].reshape(blocks, BLOCK, 1)[:, :1]
    last = doc_blocks[:, -1:]
    from_before = (doc_blocks == before).astype(F32)
    to_last = (doc_blocks == last).astype(F32)
    kept = (last == before).astype(F32)

    def small(rates, decay):
        beta = jax.nn.sigmoid(rates[:, H:]).reshape(blocks, BLOCK, H)
        log_decay = -jnp.exp(decay[:1]) * jax.nn.softplus(rates[:, :H] + decay[1:])
        i = lax.broadcasted_iota(jnp.int32, (BLOCK, BLOCK), 0)
        j = lax.broadcasted_iota(jnp.int32, (BLOCK, BLOCK), 1)
        cum = jnp.einsum(
            "bih,ij->bjh",
            log_decay.reshape(blocks, BLOCK, H),
            (i <= j).astype(F32),
            precision=lax.Precision.HIGHEST,
        )
        final = cum[:, -1:]
        a = jnp.exp(cum) * from_before
        d = jnp.exp(final - cum) * to_last
        kappa = jnp.broadcast_to(jnp.exp(final) * kept, cum.shape)
        return jnp.concatenate([cum, beta, a, d, kappa], axis=2).reshape(length, 5 * H)

    five, pull_small = jax.vjp(small, rates, decay)
    doc_lanes = jnp.broadcast_to(docs.astype(F32)[:, None], (length, H))
    col = jnp.concatenate([five, doc_lanes, jnp.zeros((length, 128 - 6 * H), F32)], axis=1)

    n_shape = ((length, channels), BF16)
    inv_shape = ((blocks, groups, ROWS, ROWS), F32)
    state_shape = ((H, DK, DV), F32)
    cor_shape = ((blocks, groups, ROWS, ROWS), BF16)
    x = points("conv", x)
    (n,) = call(conv_kernel, [n_shape], [], x, weights, masks)
    n = points("inverse", n)
    (inv,) = call(inverse_kernel, [inv_shape], [], n, col)
    inv = points("state", inv)
    start = jnp.zeros((H, DK, DV), BF16)
    ahead = [(i, i + 1) for i in range(sp_size - 1)]
    behind = [(i + 1, i) for i in range(sp_size - 1)]
    for _ in range(sp_size - 1):
        (state,) = call(state_kernel, [state_shape], [], n, inv, col, start)
        state = points("state_done", state)
        start = lax.ppermute(state.astype(BF16), "sp", ahead)
    mixed, cor, states = call(
        scan_kernel,
        [((length, H * DV), BF16), cor_shape, ((blocks, H, DK, DV), BF16)],
        [pltpu.VMEM((H, DK, DV), F32)],
        n,
        inv,
        col,
        start,
    )

    def pull(dout):
        dstart = jnp.zeros((H, DK, DV), BF16)
        for _ in range(sp_size - 1):
            (dstate,) = call(
                back_state_kernel, [state_shape], [], n, inv, col, dout, dstart
            )
            dstart = lax.ppermute(points("sent", dstate.astype(BF16)), "sp", behind)
        dstart = points("back", dstart)
        dn, gfeat = call(
            back_kernel,
            [
                ((length, channels), F32),
                ((length, 128), F32),
            ],
            [pltpu.VMEM((H, DK, DV), F32)],
            n,
            inv,
            col,
                dout,
            cor,
            states,
            dstart,
        )
        dn = points("conv_back", dn)
        dx, dcw = call(
            conv_back_kernel,
            [((length + HALO, channels), BF16), ((CONV, channels), F32)],
            [],
            x,
            weights,
            masks,
            dn,
        )
        d_rates, d_decay = pull_small(gfeat[:, : 5 * H])
        from_next = lax.ppermute(dx[:HALO], "sp", behind)
        return dx, from_next, dcw, d_rates, d_decay

    return mixed, pull


def rms_norm(values, scales):
    return values * lax.rsqrt(jnp.mean(values * values, axis=-1, keepdims=True) + EPSILON) * scales


def output_gate(mixed, gate_raw, scales):
    length = mixed.shape[0]
    normed = rms_norm(mixed.reshape(length, H, DV), scales)
    return (normed * jax.nn.silu(gate_raw).reshape(length, H, DV)).reshape(length, H * DV)


def residual_norm(values, attended, scales):
    hidden = values + attended
    return (hidden, rms_norm(hidden, scales))


def after(value, *earlier):
    return lax.optimization_barrier((value,) + earlier)[0] if earlier else value


def swap(value, axis):
    return lax.ppermute(value, axis, [(0, 1), (1, 0)])


def other(first):
    return "sp" if first == "x" else "x"


def pair(axis, mine, theirs, dim):
    first = lax.axis_index(axis) == 0
    return jnp.where(
        first,
        jnp.concatenate([mine, theirs], axis=dim),
        jnp.concatenate([theirs, mine], axis=dim),
    )


def relative_axes(first):
    return ("core", first, other(first))


def place(first, k):
    total = 0
    for shift, axis in zip((2, 1, 0), relative_axes(first)):
        bit = lax.axis_index(axis)
        total = total + (1 << shift) * (1 - bit if (k >> shift) & 1 else bit)
    return total


def reorder(value, first):
    width = value.shape[1] // 8
    return jnp.concatenate(
        [lax.dynamic_slice_in_dim(value, place(first, i) * width, width, 1) for i in range(8)],
        axis=1,
    )


def shifted(value, step):
    count = lax.axis_size("fsdp")
    return lax.ppermute(value, "fsdp", [(i, (i + step) % count) for i in range(count)])


def gather_blocks(piece, *late):
    count, rows = lax.axis_size("fsdp"), piece.shape[0]
    parts = [piece] + [after(shifted(piece, s), *late) for s in range(1, count)]
    line = jnp.concatenate([parts[(count - 1 - i) % count] for i in range(2 * count - 1)], axis=0)
    start = (count - 1 - lax.axis_index("fsdp")) * rows
    return lax.dynamic_slice_in_dim(line, start, count * rows, 0)


def sum_blocks(value):
    total = lax.psum_scatter(value.astype(BF16), "fsdp", scatter_dimension=0, tiled=True)
    if lax.axis_size("hi") > 1:
        total = lax.psum(total, "hi")
    return total


WEIGHT_AXES = ("fsdp", "hi", "x", "core", "sp")


def gather_rows(shard):
    count, own = 1, 0
    for axis in WEIGHT_AXES[1:]:
        count = count * lax.axis_size(axis)
        own = own * lax.axis_size(axis) + lax.axis_index(axis)
    rows = shard.shape[0] // count
    piece = lax.dynamic_slice_in_dim(shard, own * rows, rows, 0)
    return lax.all_gather(piece, WEIGHT_AXES, axis=0, tiled=True)


class ColumnGather:
    def __init__(self, shard, first):
        width = shard.shape[1] // 8
        self.first = first
        self.piece = lax.dynamic_slice_in_dim(shard, place(first, 0) * width, width, 1)

    def blocks(self, earlier, late):
        self.held = gather_blocks(after(self.piece, *earlier), late)
        return self.held

    def second(self, *earlier):
        held = after(self.held, *earlier) if earlier else self.held
        self.held = jnp.concatenate([held, swap(held, other(self.first))], axis=1)
        return self.held

    def third(self, *earlier):
        held = after(self.held, *earlier) if earlier else self.held
        self.held = jnp.concatenate([held, swap(held, self.first)], axis=1)
        return self.held

    def full(self):
        return self.held, swap(self.held, "core")


def dot_columns(values, halves_of):
    parts = [jnp.dot(values, w, preferred_element_type=F32) for w in halves_of]
    return jnp.concatenate(parts, axis=1)


def dot_back(grads, halves_of):
    half = grads.shape[1] // 2
    return jnp.einsum(
        "tf,df->td", grads[:, :half], halves_of[0], preferred_element_type=F32
    ) + jnp.einsum("tf,df->td", grads[:, half:], halves_of[1], preferred_element_type=F32)


def grad_dot(left, right):
    return jnp.einsum("td,tf->df", left, right, preferred_element_type=F32)


class ColumnSum:
    def __init__(self, left, right, first):
        self.left, self.right, self.first = left, right, first
        self.width = right.shape[1] // 8
        self.from_core = swap(grad_dot(left, right[:, 4 * self.width :]).astype(BF16), "core")

    def second(self):
        width = self.width
        outgoing = grad_dot(self.left, self.right[:, 2 * width : 4 * width])
        self.outgoing = (outgoing + self.from_core[:, 2 * width :].astype(F32)).astype(BF16)
        self.from_first = swap(self.outgoing, self.first)
        return self.outgoing

    def third(self, *late):
        width = self.width
        self.from_first = after(self.from_first, *late)
        self.outgoing = (
            grad_dot(self.left, self.right[:, width : 2 * width])
            + self.from_core[:, width : 2 * width].astype(F32)
            + self.from_first[:, width:].astype(F32)
        ).astype(BF16)
        self.from_second = swap(self.outgoing, other(self.first))
        return self.outgoing

    def own(self):
        width = self.width
        return (
            grad_dot(self.left, self.right[:, :width])
            + self.from_core[:, :width].astype(F32)
            + self.from_first[:, :width].astype(F32)
            + self.from_second.astype(F32)
        )


def spread(blocks):
    held = jnp.concatenate(blocks, axis=0)[None]
    for axis in ("sp", "x"):
        held = jnp.concatenate([held, swap(held, axis)], axis=0)
    return held, swap(held, "core")


def spread_aside(blocks):
    every = lax.all_gather(jnp.concatenate(blocks, axis=0), ("x", "core", "sp"), axis=0)
    return every[:4], every[4:]


def unpack_kernel(segments, count, places_ref, *refs):
    sources, outs = refs[:count], refs[count:]
    for source, row, out, column, rows, blocks, way in segments:
        for k in range(8):
            piece = sources[2 * source + k // 4]
            at = pl.multiple_of(column + places_ref[2 * way, k] * (128 * blocks), 128)
            down = pl.multiple_of(places_ref[2 * way + 1, k] * rows, 16)
            for j in range(blocks):
                outs[out][pl.ds(down, rows), pl.ds(at + 128 * j, 128)] = piece[
                    k % 4, row + j * rows : row + (j + 1) * rows
                ].astype(F32)


def unpack(places, segments, sources, shapes):
    count = len(sources)
    return pl.pallas_call(
        functools.partial(unpack_kernel, segments, count),
        out_shape=[jax.ShapeDtypeStruct(s, F32) for s in shapes],
        in_specs=[pl.BlockSpec(memory_space=pltpu.SMEM)]
        + [pl.BlockSpec(memory_space=pltpu.VMEM)] * count,
        out_specs=[pl.BlockSpec(memory_space=pltpu.VMEM)] * len(shapes),
        compiler_params=pltpu.CompilerParams(vmem_limit_bytes=VMEM_BYTES),
    )(places, *sources)


def spread_places():
    core, x, y = lax.axis_index("core"), lax.axis_index("x"), lax.axis_index("sp")
    table = [[] for _ in range(12)]
    for k in range(8):
        c, d, e = (
            1 - bit if (k >> shift) & 1 else bit for shift, bit in ((2, core), (1, x), (0, y))
        )
        for line, value in enumerate((4 * c + 2 * d + e, 0, 4 * c + 2 * e + d, 0, 2 * c + d, e)):
            table[line].append(jnp.asarray(value, jnp.int32))
        d, c, e = (k >> 2) & 1, (k >> 1) & 1, k & 1
        for line, value in enumerate((4 * c + 2 * d + e, 0, 4 * c + 2 * e + d, 0, 2 * c + d, e)):
            table[6 + line].append(jnp.asarray(value, jnp.int32))
    return jnp.stack([jnp.stack(line) for line in table])


def by_half(values):
    blocks = values.reshape(values.shape[0], lax.axis_size("fsdp"), 2, -1)
    low = blocks[:, :, 0].reshape(values.shape[0], -1)
    high = blocks[:, :, 1].reshape(values.shape[0], -1)
    first = lax.axis_index("sp") == 0
    return jnp.concatenate(
        [jnp.where(first, low, high), jnp.where(first, high, low)], axis=1
    )


class HalfSum:
    def __init__(self, left, right):
        self.left, self.first = left, "x"
        self.width = width = right.shape[1] // 4
        core, x = lax.axis_index("core"), lax.axis_index("x")

        def half(c):
            return jnp.concatenate(
                [
                    lax.dynamic_slice_in_dim(right, (2 * c + d) * width, width, 1)
                    for d in (x, 1 - x)
                ],
                axis=1,
            )

        self.near, far_core = half(core), half(1 - core)
        self.rows = left.shape[1] // 2
        self.from_core = swap(grad_dot(left, far_core).astype(BF16), "core")

    def second(self):
        width = self.width
        outgoing = grad_dot(self.left, self.near[:, width:])
        self.outgoing = (outgoing + self.from_core[:, width:].astype(F32)).astype(BF16)
        self.from_x = swap(self.outgoing, "x")
        return self.outgoing

    def third(self):
        rows, width = self.rows, self.width
        self.outgoing = (
            grad_dot(self.left[:, rows:], self.near[:, :width])
            + self.from_core[rows:, :width].astype(F32)
            + self.from_x[rows:].astype(F32)
        ).astype(BF16)
        self.from_y = swap(self.outgoing, "sp")
        return self.outgoing

    def own(self):
        rows, width = self.rows, self.width
        return (
            grad_dot(self.left[:, :rows], self.near[:, :width])
            + self.from_core[:rows, :width].astype(F32)
            + self.from_x[:rows].astype(F32)
            + self.from_y.astype(F32)
        )


def narrow(value):
    return jnp.concatenate(
        [value[:, i : i + 128] for i in range(0, value.shape[1], 128)], axis=0
    )


def by_member(value):
    blocks = value.reshape(lax.axis_size("fsdp"), -1, value.shape[1])
    return jnp.concatenate(
        [blocks[:, :, i : i + 128] for i in range(0, value.shape[1], 128)], axis=1
    )


def pack_small(parts, width):
    flat = jnp.concatenate([p.reshape(-1) for p in parts])
    return jnp.pad(flat, (0, -flat.shape[0] % (16 * width))).reshape(-1, width)


def unpack_small(every, parts):
    out, start = [], 0
    for p in parts:
        out.append(every[:, start : start + p.size].reshape((-1,) + p.shape))
        start += p.size
    return out


def sum_small(parts, *earlier):
    flat = jnp.concatenate([p.reshape(-1) for p in parts])
    size = flat.shape[0]
    flat = after(jnp.pad(flat, (0, -size % 1024)).reshape(-1, 128), *earlier)
    for axis in ("core", "x", "sp"):
        flat = flat + swap(flat, axis)
    members = lax.axis_size("fsdp")
    for bit in range(members.bit_length() - 1):
        flat = flat + lax.ppermute(flat, "fsdp", [(i, i ^ (1 << bit)) for i in range(members)])
    if lax.axis_size("hi") > 1:
        flat = lax.psum(flat, "hi")
    total = flat.reshape(-1)
    out, start = [], 0
    for p in parts:
        out.append(total[start : start + p.size].reshape(p.shape))
        start += p.size
    return out


def own_part(value, axis):
    size = value.shape[axis] // lax.axis_size("fsdp")
    return lax.dynamic_slice_in_dim(value, lax.axis_index("fsdp") * size, size, axis)


def body(
    tokens,
    cotangent,
    doc_lengths,
    input_weight,
    rate_weight,
    conv_weight,
    head_decay,
    mixer_gain,
    heads_gain,
    output_weight,
    feed_gain,
    up_weight,
    down_weight,
):
    length = tokens.shape[0]
    sp_size = lax.axis_size("sp")
    member = lax.axis_index("sp")
    qkv_cols = H * (2 * DK + DV)
    qk_cols = 2 * H * DK
    members = lax.axis_size("fsdp")
    qk_way = ColumnGather(input_weight[:, :qk_cols], "x")
    v_way = ColumnGather(input_weight[:, qk_cols:qkv_cols], "sp")
    gate_way = ColumnGather(input_weight[:, qkv_cols:], "sp")
    down_way = ColumnGather(down_weight, "x")
    pair_rows, pair_cols = qk_way.piece.shape[0], 2 * qk_way.piece.shape[1]
    smalls = (rate_weight, conv_weight, head_decay, mixer_gain, heads_gain, feed_gain)
    first_load = jnp.concatenate(
        [
            jnp.concatenate([qk_way.piece, v_way.piece], axis=1),
            pack_small(smalls, pair_cols),
        ],
        axis=0,
    )
    first_all = gather_blocks(first_load).reshape(members, -1, pair_cols)
    both = first_all[:, :pair_rows].reshape(-1, pair_cols)
    qk_way.held, v_way.held = both[:, : pair_cols // 2], both[:, pair_cols // 2 :]
    rate_all, conv_all, decay_all, mixer_all, heads_all, feed_all = unpack_small(
        first_all[:, pair_rows:].reshape(members, -1), smalls
    )
    qkv_second = (qk_way.second(), v_way.second())
    qkv_third = (qk_way.third(), v_way.third())
    qk_full, v_full = qk_way.full(), v_way.full()
    out_full = gather_rows(output_weight)
    up_full = gather_rows(up_weight)
    rate_full = jnp.swapaxes(rate_all.reshape(-1, H, 2), 1, 2).reshape(-1, 2 * H)
    conv_full = jnp.swapaxes(conv_all, 0, 1).reshape(CONV, -1).astype(F32)
    decay_full = jnp.swapaxes(decay_all, 0, 1).reshape(2, H).astype(F32)
    mixer_scale = mixer_all.reshape(-1).astype(F32)
    heads_scale = heads_all.reshape(-1).astype(F32)
    feed_scale = feed_all.reshape(-1).astype(F32)

    def points(name, value):
        if name == "conv":
            gate_way.blocks(qkv_third, value)
            gate_way.second()
            return value
        if name == "inverse":
            value = after(value, gate_way.held)
            gate_way.third(value)
            ready.append(value)
            return value
        if name == "state":
            down_way.blocks(ready, value)
            down_way.second()
            return after(value, gate_way.held)
        if name == "state_done":
            down_way.third(value)
            return value
        if name == "sent":
            for key in ("down", "out", "gate"):
                sums[key].third(value)
            return value
        if name == "back":
            return after(value, sums["down"].outgoing)
        if name == "conv_back":
            for key in ("out", "gate"):
                sums[key].from_second = after(sums[key].from_second, value)
            packed = jnp.concatenate(
                [by_member(sums[key].own().astype(BF16)) for key in ("down", "out", "gate")],
                axis=1,
            )
            owns.append(packed.reshape(-1, 128))
            return after(value, owns[0], sums["up"].third())
        return value

    sums, ready, owns = {}, [], []

    ends = jnp.cumsum(doc_lengths[0])
    positions = lax.broadcasted_iota(jnp.int32, (length * sp_size, 1), 0)
    doc_ids = jnp.sum((positions >= ends[None, :]).astype(jnp.int32), axis=1)

    ahead = [(i, i + 1) for i in range(sp_size - 1)]
    halo = lax.ppermute(tokens[-HALO:], "sp", ahead)
    x_float = tokens.astype(F32)
    normed, pull_norm = jax.vjp(rms_norm, x_float, mixer_scale)
    normed_low = normed.astype(BF16)
    halo_low = rms_norm(halo.astype(F32), mixer_scale).astype(BF16)
    normed_more = jnp.concatenate([halo_low, normed_low], axis=0)
    qkv = jnp.concatenate(
        [
            reorder(dot_columns(normed_more, qk_full).astype(BF16), "x"),
            reorder(dot_columns(normed_more, v_full).astype(BF16), "sp"),
        ],
        axis=1,
    )
    rate_raw = jnp.dot(normed_low, rate_full, preferred_element_type=F32)
    rates = rate_raw.astype(BF16).astype(F32)
    mixed, pull_mix = mixer(qkv, conv_full, rates, decay_full, doc_ids, member, sp_size, points)
    gate_full, down_full = gate_way.full(), down_way.full()
    gate_raw = reorder(dot_columns(normed_low, gate_full), "sp")
    gated, pull_gate = jax.vjp(output_gate, mixed.astype(F32), gate_raw, heads_scale)
    gated_low = gated.astype(BF16)
    attended = jnp.dot(gated_low, out_full, preferred_element_type=F32)
    (hidden, normed_two), pull_resid = jax.vjp(residual_norm, x_float, attended, feed_scale)
    two_low = normed_two.astype(BF16)
    gate_up = jnp.dot(two_low, up_full, preferred_element_type=F32)

    def feed_act(gate_up):
        half = gate_up.shape[1] // 2
        return jax.nn.silu(gate_up[:, :half]) * gate_up[:, half:]

    activated, pull_act = jax.vjp(feed_act, gate_up)
    act_low = activated.astype(BF16)
    block_out = (hidden + reorder(dot_columns(act_low, down_full), "x")).astype(BF16)
    cot_rel = reorder(cotangent, "x")
    sums["down"] = ColumnSum(act_low, cot_rel, "x")
    d_act = dot_back(cot_rel, down_full)
    d_gu_low = pull_act(d_act)[0].astype(BF16)
    sums["up"] = HalfSum(by_half(two_low), d_gu_low)
    d_gu_low = after(d_gu_low, sums["down"].second())
    d_two = jnp.einsum("tf,df->td", d_gu_low, up_full, preferred_element_type=F32)
    d_resid, d_attended, feed_grad = pull_resid((cotangent.astype(F32), d_two))
    d_att_low = d_attended.astype(BF16)
    d_att_rel = reorder(d_att_low, "sp")
    sums["out"] = ColumnSum(gated_low, d_att_rel, "sp")
    d_gated = jnp.einsum("td,ed->te", d_att_low, out_full, preferred_element_type=F32)
    d_mixed, d_gate, heads_grad = pull_gate(d_gated)
    d_gate_low = d_gate.astype(BF16)
    d_gate_rel = reorder(d_gate_low, "sp")
    sums["gate"] = ColumnSum(normed_low, d_gate_rel, "sp")
    d_mixed_low = after(
        d_mixed.astype(BF16), *(sums[key].second() for key in ("up", "out", "gate"))
    )
    d_more, from_next, conv_grad, d_rates, decay_grad = pull_mix(d_mixed_low)
    edge = jnp.pad(from_next.astype(F32), ((length - HALO, 0), (0, 0)))
    d_qkv = (d_more[HALO:].astype(F32) + edge).astype(BF16)
    d_rate_low = d_rates.astype(BF16)
    d_qk_rel = reorder(d_qkv[:, :qk_cols], "x")
    d_v_rel = reorder(d_qkv[:, qk_cols:], "sp")
    sums["qk"] = ColumnSum(normed_low, d_qk_rel, "x")
    sums["v"] = ColumnSum(normed_low, d_v_rel, "sp")
    sums["up"].from_y = after(sums["up"].from_y, sums["qk"].second(), sums["v"].second())
    d_normed = dot_back(d_qk_rel, qk_full) + dot_back(d_v_rel, v_full)
    d_normed = d_normed + dot_back(d_gate_rel, gate_full)
    d_normed = d_normed + jnp.einsum(
        "tf,df->td", d_rate_low, rate_full, preferred_element_type=F32
    )
    for key in ("qk", "v"):
        sums[key].third()
        sums[key].from_second = after(sums[key].from_second, d_normed)
    places = spread_places()
    early_block = sum_blocks(owns[0])
    down_rows, out_rows = down_weight.shape[0], output_weight.shape[0]
    early_sums = spread_aside([early_block])
    down_shard, output_shard = unpack(
        places,
        [(0, 0, 0, 0, down_rows, 1, 3), (0, down_rows, 1, 0, out_rows, 1, 4)],
        early_sums,
        [down_weight.shape, output_weight.shape],
    )
    up_block = sum_blocks(sums["up"].own())
    (up_shard,) = unpack(
        places,
        [(0, 0, 0, 0, up_block.shape[0], up_block.shape[1] // 128, 5)],
        spread_aside([narrow(up_block)]),
        [up_weight.shape],
    )
    late_block = sum_blocks(jnp.concatenate([sums["qk"].own(), sums["v"].own()], axis=1))
    rows, wide = late_block.shape[0], late_block.shape[1] // 256
    gate_wide = H * DV // 8 // 128
    (input_shard,) = unpack(
        places,
        [
            (0, 0, 0, 0, rows, wide, 0),
            (0, wide * rows, 0, qk_cols, rows, wide, 1),
            (1, down_rows + out_rows, 0, qkv_cols, rows, gate_wide, 4),
        ],
        spread([narrow(late_block)]) + early_sums,
        [input_weight.shape],
    )
    rate_grad = jnp.einsum("td,tf->df", normed_low, d_rate_low, preferred_element_type=F32)
    d_front, mixer_grad = pull_norm(d_normed)
    tokens_grad = (d_resid + d_front).astype(BF16)
    rate_sum, conv_sum, decay_sum, mixer_sum, heads_sum, feed_sum = sum_small(
        (rate_grad, conv_grad, decay_grad, mixer_grad, heads_grad, feed_grad),
        sums["qk"].outgoing,
        sums["v"].outgoing,
    )
    return (
        block_out,
        tokens_grad,
        input_shard,
        own_part(jnp.swapaxes(rate_sum.reshape(-1, 2, H), 1, 2).reshape(-1, 2 * H), 0),
        own_part(conv_sum, 1),
        own_part(decay_sum, 1),
        own_part(mixer_sum, 0),
        own_part(heads_sum, 0),
        output_shard,
        own_part(feed_sum, 0),
        up_shard,
        down_shard,
    )


def solution(mesh):
    dp, fsdp, sp = (mesh.shape[axis] for axis in ("dp", "fsdp", "sp"))
    dp_axes = ("hi", "x", "core")
    cut = jax.sharding.Mesh(
        mesh.devices.reshape(dp // 4, 2, 2, fsdp, sp), dp_axes + ("fsdp", "sp")
    )
    rows = P(dp_axes + ("fsdp", "sp"), None)
    split = P("fsdp", None)
    return jax.shard_map(
        body,
        mesh=cut,
        in_specs=(
            rows,
            rows,
            P(dp_axes + ("fsdp",), None),
            split,
            split,
            P(None, "fsdp"),
            P(None, "fsdp"),
            P("fsdp"),
            P("fsdp"),
            split,
            P("fsdp"),
            split,
            split,
        ),
        out_specs=(
            rows,
            rows,
            split,
            split,
            P(None, "fsdp"),
            P(None, "fsdp"),
            P("fsdp"),
            P("fsdp"),
            split,
            P("fsdp"),
            split,
            split,
        ),
        check_vma=False,
    )
```

```python
import functools
import jax
import jax.numpy as jnp
from jax import lax
from jax.experimental import pallas as pl
from jax.experimental.pallas import tpu as pltpu
from jax.sharding import PartitionSpec as P

H = 8
DK = 128
DV = 256
CONV = 4
BLOCK = 64
EPSILON = 1e-06
HALO = 16
STACK = 4
ROWS = STACK * BLOCK
SCALE = DK ** (-0.5)
VMEM_BYTES = 56 * 1024 * 1024
F32 = jnp.float32
BF16 = jnp.bfloat16


def mm(a, b, dims=((1,), (0,))):
    return lax.dot_general(
        a.astype(BF16), b.astype(BF16), (dims, ((), ())), preferred_element_type=F32
    )


def halves(a):
    high = a.astype(BF16)
    return high, (a - high.astype(F32)).astype(BF16)


def mm_fine(a, b):
    (ah, al), (bh, bl) = a, b
    return mm(ah, bh) + (mm(ah, bl) + mm(al, bh))


def stack_heads(ref, block, group, base, width):
    rows = pl.ds(pl.multiple_of(block * BLOCK, BLOCK), BLOCK)
    return jnp.concatenate(
        [
            ref[rows, base + (group * STACK + h) * width : base + (group * STACK + h + 1) * width]
            for h in range(STACK)
        ],
        axis=0,
    )


def store_heads(ref, block, group, base, width, value):
    rows = pl.ds(pl.multiple_of(block * BLOCK, BLOCK), BLOCK)
    for h in range(STACK):
        start = base + (group * STACK + h) * width
        ref[rows, start : start + width] = value[h * BLOCK : (h + 1) * BLOCK].astype(ref.dtype)


def head(value, h):
    return value[h * BLOCK : (h + 1) * BLOCK]


def columns(feat_ref, block, group):
    packed = feat_ref[pl.ds(pl.multiple_of(block * BLOCK, BLOCK), BLOCK), :]
    return [
        jnp.concatenate(
            [
                packed[:, f * H + group * STACK + h : f * H + group * STACK + h + 1]
                for h in range(STACK)
            ],
            axis=0,
        )
        for f in range(6)
    ]


def decay_matrix(cum, doc):
    i = lax.broadcasted_iota(jnp.int32, (ROWS, ROWS), 0)
    j = lax.broadcasted_iota(jnp.int32, (ROWS, ROWS), 1)
    cum_row, doc_row = (
        jnp.sum(jnp.where(i == j, c, 0.0), axis=0, keepdims=True) for c in (cum, doc)
    )
    inside = ((i // BLOCK) == (j // BLOCK)) & (i >= j) & (doc == doc_row)
    decay = jnp.exp(jnp.where(inside, cum - cum_row, -1e30))
    return decay, jnp.where(i > j, decay, 0.0)


def unit_inverses(lowers):
    i = lax.broadcasted_iota(jnp.int32, (ROWS, ROWS), 0)
    j = lax.broadcasted_iota(jnp.int32, (ROWS, ROWS), 1)
    apart = jnp.bitwise_xor(i, j)
    inverses = [
        jnp.where(i == j, 1.0, 0.0) - jnp.where(apart == 1, lower, 0.0) for lower in lowers
    ]
    size = 2
    while size < BLOCK:
        cross = (apart >= size) & (apart < 2 * size)
        parts = [halves(inverse) for inverse in inverses]
        right = [
            halves(mm_fine(halves(jnp.where(cross, lower, 0.0)), part))
            for lower, part in zip(lowers, parts)
        ]
        inverses = [
            inverse - mm_fine(part, r) for inverse, part, r in zip(inverses, parts, right)
        ]
        size *= 2
    return inverses


def conv_taps(x, masks, weights):
    taps = [x[HALO:]]
    for s in range(1, CONV):
        taps.append(pltpu.roll(x, s, 0)[HALO:] * masks[s - 1])
    z = taps[0] * weights[0:1]
    for s in range(1, CONV):
        z = z + taps[s] * weights[s : s + 1]
    return taps, z


def conv_masks(mask_ref, length):
    return [
        jnp.broadcast_to(mask_ref[:, s : s + 1], (length, 128)) for s in range(CONV - 1)
    ]


def conv_kernel(x_ref, cw_ref, mask_ref, n_ref):
    length = n_ref.shape[0]
    qk_cols = 2 * H * DK

    def chunk(c, normalise):
        lanes = pl.ds(pl.multiple_of(c * 128, 128), 128)
        masks = conv_masks(mask_ref, length)
        _, z = conv_taps(x_ref[:, lanes].astype(F32), masks, cw_ref[:, lanes])
        y = z * jax.nn.sigmoid(z)
        if normalise:
            y = y * lax.rsqrt(jnp.sum(y * y, axis=1, keepdims=True) + EPSILON)
        n_ref[:, lanes] = y.astype(BF16)

    @pl.loop(0, qk_cols // 128)
    def _(c):
        chunk(c, True)

    @pl.loop(qk_cols // 128, x_ref.shape[1] // 128)
    def _(c):
        chunk(c, False)


def inverse_kernel(n_ref, col_ref, inv_ref):
    @pl.loop(0, n_ref.shape[0] // BLOCK)
    def _(block):
        lowers = []
        for group in range(H // STACK):
            cum, beta, _, _, _, doc = columns(col_ref, block, group)
            keys = stack_heads(n_ref, block, group, H * DK, DK)
            _, strict = decay_matrix(cum, doc)
            lowers.append(beta * mm(keys, keys, ((1,), (1,))) * strict)
        for group, inverse in enumerate(unit_inverses(lowers)):
            inv_ref[block, group] = inverse


def state_steps(n_ref, inv_ref, col_ref, state_ref):
    @pl.loop(0, n_ref.shape[0] // BLOCK)
    def _(block):
        for group in range(H // STACK):
            _, beta, a, d, kappa, _ = columns(col_ref, block, group)
            keys = stack_heads(n_ref, block, group, H * DK, DK)
            values = stack_heads(n_ref, block, group, 2 * H * DK, DV).astype(F32)
            seen = jnp.concatenate(
                [mm(head(keys, h), state_ref[group * STACK + h]) for h in range(STACK)], axis=0
            )
            corrected = mm(inv_ref[block, group], beta * (values - a * seen))
            update = d * corrected
            for h in range(STACK):
                n = group * STACK + h
                state_ref[n] = kappa[h * BLOCK : h * BLOCK + 1] * state_ref[n] + mm(
                    head(keys, h), head(update, h), ((0,), (0,))
                )


def state_kernel(n_ref, inv_ref, col_ref, start_ref, state_ref):
    state_ref[...] = start_ref[...].astype(F32)
    state_steps(n_ref, inv_ref, col_ref, state_ref)


def scan_kernel(n_ref, inv_ref, col_ref, start_ref, out_ref, cor_ref, states_ref, state):
    state[...] = start_ref[...].astype(F32)

    @pl.loop(0, n_ref.shape[0] // BLOCK)
    def _(block):
        for group in range(H // STACK):
            cum, beta, a, d, kappa, doc = columns(col_ref, block, group)
            queries = stack_heads(n_ref, block, group, 0, DK)
            keys = stack_heads(n_ref, block, group, H * DK, DK)
            values = stack_heads(n_ref, block, group, 2 * H * DK, DV).astype(F32)
            within, _ = decay_matrix(cum, doc)
            scores = SCALE * mm(queries, keys, ((1,), (1,))) * within
            both = []
            for h in range(STACK):
                low = state[group * STACK + h].astype(BF16)
                states_ref[block, group * STACK + h] = low
                both.append(mm(jnp.concatenate([head(keys, h), head(queries, h)], axis=0), low))
            seen = jnp.concatenate([b[:BLOCK] for b in both], axis=0)
            asked = jnp.concatenate([b[BLOCK:] for b in both], axis=0)
            corrected = mm(inv_ref[block, group], beta * (values - a * seen))
            cor_ref[block, group] = corrected.astype(BF16)
            out = (SCALE * a) * asked + mm(scores, corrected)
            store_heads(out_ref, block, group, 0, DV, out)
            update = d * corrected
            for h in range(STACK):
                n = group * STACK + h
                state[n] = kappa[h * BLOCK : h * BLOCK + 1] * state[n] + mm(
                    head(keys, h), head(update, h), ((0,), (0,))
                )


def back_state_kernel(n_ref, inv_ref, col_ref, dout_ref, start_ref, dstate_ref):
    blocks = n_ref.shape[0] // BLOCK
    dstate_ref[...] = start_ref[...].astype(F32)

    @pl.loop(0, blocks)
    def _(step):
        block = blocks - 1 - step
        for group in range(H // STACK):
            cum, beta, a, d, kappa, doc = columns(col_ref, block, group)
            queries = stack_heads(n_ref, block, group, 0, DK)
            keys = stack_heads(n_ref, block, group, H * DK, DK)
            within, _ = decay_matrix(cum, doc)
            scores = SCALE * mm(queries, keys, ((1,), (1,))) * within
            dout = stack_heads(dout_ref, block, group, 0, DV)
            wide = (SCALE * a) * dout.astype(F32)
            pulled = jnp.concatenate(
                [mm(head(keys, h), dstate_ref[group * STACK + h]) for h in range(STACK)], axis=0
            )
            d_cor = mm(scores, dout, ((0,), (0,))) + d * pulled
            d_right = mm(inv_ref[block, group], d_cor, ((0,), (0,)))
            d_seen = (-a * beta) * d_right
            for h in range(STACK):
                n = group * STACK + h
                left = jnp.concatenate([head(keys, h), head(queries, h)], axis=0)
                right = jnp.concatenate([head(d_seen, h), head(wide, h)], axis=0)
                dstate_ref[n] = kappa[h * BLOCK : h * BLOCK + 1] * dstate_ref[n] + mm(
                    left, right, ((0,), (0,))
                )


def back_kernel(
    n_ref,
    inv_ref,
    col_ref,

    dout_ref,
    cor_ref,
    states_ref,
    start_ref,
    dn_ref,
    gfeat_ref,
    dstate,
):
    length = n_ref.shape[0]
    blocks = length // BLOCK
    dstate[...] = start_ref[...].astype(F32)

    @pl.loop(0, blocks)
    def _(step):
        block = blocks - 1 - step
        packed = jnp.zeros((BLOCK, 128), F32)
        for group in range(H // STACK):
            cum, beta, a, d, kappa, doc = columns(col_ref, block, group)
            queries = stack_heads(n_ref, block, group, 0, DK)
            keys = stack_heads(n_ref, block, group, H * DK, DK)
            values = stack_heads(n_ref, block, group, 2 * H * DK, DV).astype(F32)
            within, strict = decay_matrix(cum, doc)
            scores = SCALE * mm(queries, keys, ((1,), (1,))) * within
            weighted = mm(keys, keys, ((1,), (1,))) * strict
            dout = stack_heads(dout_ref, block, group, 0, DV)
            dout_wide = dout.astype(F32)
            corrected = cor_ref[block, group]
            cor_wide = corrected.astype(F32)
            wide = (SCALE * a) * dout_wide
            pulled, seen, asked, dk_state, d_kappa = [], [], [], [], []
            update = (d * cor_wide).astype(BF16)
            for h in range(STACK):
                n = group * STACK + h
                state = states_ref[block, n]
                after = dstate[n]
                after_low = after.astype(BF16)
                both = mm(jnp.concatenate([head(keys, h), head(queries, h)], axis=0), state)
                seen.append(both[:BLOCK])
                asked.append(both[BLOCK:])
                pulled.append(mm(head(keys, h), after_low))
                dk_state.append(mm(head(update, h), after_low, ((1,), (1,))))
                total = jnp.sum(
                    jnp.sum(state.astype(F32) * after, axis=0, keepdims=True),
                    axis=1,
                    keepdims=True,
                )
                d_kappa.append(jnp.broadcast_to(total * (1.0 / BLOCK), (BLOCK, 1)))
            pulled, seen, asked, d_kappa = (
                jnp.concatenate(p, axis=0) for p in (pulled, seen, asked, d_kappa)
            )
            d_cor = mm(scores, dout, ((0,), (0,))) + d * pulled
            d_right = mm(inv_ref[block, group], d_cor, ((0,), (0,)))
            scaled = beta * d_right
            d_seen = -a * scaled
            dk_left, dq_left = [], []
            for h in range(STACK):
                n = group * STACK + h
                left = jnp.concatenate([head(keys, h), head(queries, h)], axis=0)
                right = jnp.concatenate([head(d_seen, h), head(wide, h)], axis=0).astype(BF16)
                both = mm(right, states_ref[block, n], ((1,), (1,)))
                dk_left.append(both[:BLOCK])
                dq_left.append(both[BLOCK:])
                dstate[n] = kappa[h * BLOCK : h * BLOCK + 1] * dstate[n] + mm(
                    left, right, ((0,), (0,))
                )
            d_scores = mm(dout, corrected, ((1,), (1,)))
            d_system = -mm(d_right, corrected, ((1,), (1,)))
            to_rows = (SCALE * d_scores * within).astype(BF16)
            by_gram = d_system * weighted
            to_keys = (beta * d_system * strict).astype(BF16)
            dq = jnp.concatenate(dq_left, axis=0) + mm(to_rows, keys)
            dk = (
                jnp.concatenate(dk_left, axis=0)
                + jnp.concatenate(dk_state, axis=0)
                + mm(to_rows, queries, ((0,), (0,)))
                + mm(to_keys, keys)
                + mm(to_keys, keys, ((0,), (0,)))
            )
            store_heads(dn_ref, block, group, 0, DK, dq)
            store_heads(dn_ref, block, group, H * DK, DK, dk)
            store_heads(dn_ref, block, group, 2 * H * DK, DV, scaled)
            spread = d_scores * scores + beta * by_gram
            d_cum = jnp.sum(spread, axis=1, keepdims=True)
            d_beta = jnp.sum(by_gram, axis=1, keepdims=True) + jnp.sum(
                d_right * (values - a * seen), axis=1, keepdims=True
            )
            d_a = jnp.sum(SCALE * dout_wide * asked - scaled * seen, axis=1, keepdims=True)
            d_d = jnp.sum(cor_wide * pulled, axis=1, keepdims=True)
            i = lax.broadcasted_iota(jnp.int32, (ROWS, ROWS), 0)
            j = lax.broadcasted_iota(jnp.int32, (ROWS, ROWS), 1)
            by_column = jnp.sum(spread, axis=0, keepdims=True)
            d_cum = d_cum - jnp.sum(jnp.where(i == j, by_column, 0.0), axis=1, keepdims=True)
            lane = lax.broadcasted_iota(jnp.int32, (BLOCK, 128), 1)
            for f, part in enumerate((d_cum, d_beta, d_a, d_d, d_kappa)):
                for h in range(STACK):
                    packed = jnp.where(lane == f * H + group * STACK + h, head(part, h), packed)
        gfeat_ref[pl.ds(pl.multiple_of(block * BLOCK, BLOCK), BLOCK), :] = packed


def conv_back_kernel(x_ref, cw_ref, mask_ref, dn_ref, dx_ref, dcw_ref):
    length = dn_ref.shape[0]

    def chunk(c, normalise):
        lanes = pl.ds(pl.multiple_of(c * 128, 128), 128)
        masks = conv_masks(mask_ref, length)
        weights = cw_ref[:, lanes]
        taps, z = conv_taps(x_ref[:, lanes].astype(F32), masks, weights)
        gate = jax.nn.sigmoid(z)
        dn = dn_ref[:, lanes]
        if normalise:
            y = z * gate
            r = lax.rsqrt(jnp.sum(y * y, axis=1, keepdims=True) + EPSILON)
            dn = r * dn - y * (r * r * r * jnp.sum(y * dn, axis=1, keepdims=True))
        dz = dn * gate * (1.0 + z * (1.0 - gate))
        edge = jnp.zeros((HALO, 128), F32)
        dx = jnp.concatenate([edge, dz * weights[0:1]], axis=0)
        sums = [jnp.sum(dz * taps[0], axis=0, keepdims=True)]
        for s in range(1, CONV):
            sums.append(jnp.sum(dz * taps[s], axis=0, keepdims=True))
            moved = jnp.concatenate([edge, dz * masks[s - 1] * weights[s : s + 1]], axis=0)
            dx = dx + pltpu.roll(moved, length + HALO - s, 0)
        dx_ref[:, lanes] = dx.astype(BF16)
        dcw_ref[:, lanes] = jnp.concatenate(sums, axis=0)

    qk_cols = 2 * H * DK

    @pl.loop(0, qk_cols // 128)
    def _(c):
        chunk(c, True)

    @pl.loop(qk_cols // 128, x_ref.shape[1] // 128)
    def _(c):
        chunk(c, False)


def call(kernel, outs, scratch, *args):
    return pl.pallas_call(
        kernel,
        out_shape=[jax.ShapeDtypeStruct(s, t) for s, t in outs],
        in_specs=[pl.BlockSpec(memory_space=pltpu.VMEM)] * len(args),
        out_specs=[pl.BlockSpec(memory_space=pltpu.VMEM)] * len(outs),
        scratch_shapes=scratch,
        compiler_params=pltpu.CompilerParams(vmem_limit_bytes=VMEM_BYTES),
        cost_estimate=pl.CostEstimate(flops=1, bytes_accessed=1, transcendentals=0),
    )(*args)


def mixer(x, weights, rates, decay, doc_all, member, sp_size, points):
    length = x.shape[0] - HALO
    blocks = length // BLOCK
    groups = H // STACK
    channels = x.shape[1]
    padded = jnp.concatenate([jnp.full((HALO,), -1, jnp.int32), doc_all])
    near = lax.dynamic_slice_in_dim(padded, member * length, length + HALO, 0)
    docs = near[HALO:]
    masks = jnp.stack(
        [(near[HALO - s : HALO - s + length] == docs).astype(F32) for s in range(1, CONV)]
        + [jnp.zeros((length,), F32)] * (8 - CONV + 1),
        axis=1,
    )
    doc_blocks = docs.reshape(blocks, BLOCK, 1)
    before = near[HALO - 1 : -1].reshape(blocks, BLOCK, 1)[:, :1]
    last = doc_blocks[:, -1:]
    from_before = (doc_blocks == before).astype(F32)
    to_last = (doc_blocks == last).astype(F32)
    kept = (last == before).astype(F32)

    def small(rates, decay):
        beta = jax.nn.sigmoid(rates[:, H:]).reshape(blocks, BLOCK, H)
        log_decay = -jnp.exp(decay[:1]) * jax.nn.softplus(rates[:, :H] + decay[1:])
        i = lax.broadcasted_iota(jnp.int32, (BLOCK, BLOCK), 0)
        j = lax.broadcasted_iota(jnp.int32, (BLOCK, BLOCK), 1)
        cum = jnp.einsum(
            "bih,ij->bjh",
            log_decay.reshape(blocks, BLOCK, H),
            (i <= j).astype(F32),
            precision=lax.Precision.HIGHEST,
        )
        final = cum[:, -1:]
        a = jnp.exp(cum) * from_before
        d = jnp.exp(final - cum) * to_last
        kappa = jnp.broadcast_to(jnp.exp(final) * kept, cum.shape)
        return jnp.concatenate([cum, beta, a, d, kappa], axis=2).reshape(length, 5 * H)

    five, pull_small = jax.vjp(small, rates, decay)
    doc_lanes = jnp.broadcast_to(docs.astype(F32)[:, None], (length, H))
    col = jnp.concatenate([five, doc_lanes, jnp.zeros((length, 128 - 6 * H), F32)], axis=1)

    n_shape = ((length, channels), BF16)
    inv_shape = ((blocks, groups, ROWS, ROWS), F32)
    state_shape = ((H, DK, DV), F32)
    cor_shape = ((blocks, groups, ROWS, ROWS), BF16)
    x = points("conv", x)
    (n,) = call(conv_kernel, [n_shape], [], x, weights, masks)
    n = points("inverse", n)
    (inv,) = call(inverse_kernel, [inv_shape], [], n, col)
    inv = points("state", inv)
    start = jnp.zeros((H, DK, DV), BF16)
    ahead = [(i, i + 1) for i in range(sp_size - 1)]
    behind = [(i + 1, i) for i in range(sp_size - 1)]
    for _ in range(sp_size - 1):
        (state,) = call(state_kernel, [state_shape], [], n, inv, col, start)
        start = lax.ppermute(state.astype(BF16), "sp", ahead)
    mixed, cor, states = call(
        scan_kernel,
        [((length, H * DV), BF16), cor_shape, ((blocks, H, DK, DV), BF16)],
        [pltpu.VMEM((H, DK, DV), F32)],
        n,
        inv,
        col,
        start,
    )

    def pull(dout):
        dstart = jnp.zeros((H, DK, DV), BF16)
        for _ in range(sp_size - 1):
            (dstate,) = call(
                back_state_kernel, [state_shape], [], n, inv, col, dout, dstart
            )
            dstart = lax.ppermute(points("sent", dstate.astype(BF16)), "sp", behind)
        dstart = points("back", dstart)
        dn, gfeat = call(
            back_kernel,
            [
                ((length, channels), F32),
                ((length, 128), F32),
            ],
            [pltpu.VMEM((H, DK, DV), F32)],
            n,
            inv,
            col,
                dout,
            cor,
            states,
            dstart,
        )
        dn = points("conv_back", dn)
        dx, dcw = call(
            conv_back_kernel,
            [((length + HALO, channels), BF16), ((CONV, channels), F32)],
            [],
            x,
            weights,
            masks,
            dn,
        )
        d_rates, d_decay = pull_small(gfeat[:, : 5 * H])
        from_next = lax.ppermute(dx[:HALO], "sp", behind)
        dx = points("conv_back_done", dx)
        return dx, from_next, dcw, d_rates, d_decay

    return mixed, pull


def rms_norm(values, scales):
    return values * lax.rsqrt(jnp.mean(values * values, axis=-1, keepdims=True) + EPSILON) * scales


def output_gate(mixed, gate_raw, scales):
    length = mixed.shape[0]
    normed = rms_norm(mixed.reshape(length, H, DV), scales)
    return (normed * jax.nn.silu(gate_raw).reshape(length, H, DV)).reshape(length, H * DV)


def residual_norm(values, attended, scales):
    hidden = values + attended
    return (hidden, rms_norm(hidden, scales))


def after(value, *earlier):
    return lax.optimization_barrier((value,) + earlier)[0] if earlier else value


def swap(value, axis):
    return lax.ppermute(value, axis, [(0, 1), (1, 0)])


def other(first):
    return "sp" if first == "x" else "x"


def pair(axis, mine, theirs, dim):
    first = lax.axis_index(axis) == 0
    return jnp.where(
        first,
        jnp.concatenate([mine, theirs], axis=dim),
        jnp.concatenate([theirs, mine], axis=dim),
    )


def relative_axes(first):
    return ("core", first, other(first))


def place(first, k):
    total = 0
    for shift, axis in zip((2, 1, 0), relative_axes(first)):
        bit = lax.axis_index(axis)
        total = total + (1 << shift) * (1 - bit if (k >> shift) & 1 else bit)
    return total


def reorder(value, first):
    width = value.shape[1] // 8
    return jnp.concatenate(
        [lax.dynamic_slice_in_dim(value, place(first, i) * width, width, 1) for i in range(8)],
        axis=1,
    )


def shifted(value, step):
    count = lax.axis_size("fsdp")
    return lax.ppermute(value, "fsdp", [(i, (i + step) % count) for i in range(count)])


def gather_blocks(piece, *late):
    count, rows = lax.axis_size("fsdp"), piece.shape[0]
    parts = [piece] + [after(shifted(piece, s), *late) for s in range(1, count)]
    line = jnp.concatenate([parts[(count - 1 - i) % count] for i in range(2 * count - 1)], axis=0)
    start = (count - 1 - lax.axis_index("fsdp")) * rows
    return lax.dynamic_slice_in_dim(line, start, count * rows, 0)


def sum_blocks(value):
    total = lax.psum_scatter(value.astype(BF16), "fsdp", scatter_dimension=0, tiled=True)
    if lax.axis_size("hi") > 1:
        total = lax.psum(total, "hi")
    return total


WEIGHT_AXES = ("fsdp", "hi", "x", "core", "sp")


def gather_rows(shard):
    count, own = 1, 0
    for axis in WEIGHT_AXES[1:]:
        count = count * lax.axis_size(axis)
        own = own * lax.axis_size(axis) + lax.axis_index(axis)
    rows = shard.shape[0] // count
    piece = lax.dynamic_slice_in_dim(shard, own * rows, rows, 0)
    return lax.all_gather(piece, WEIGHT_AXES, axis=0, tiled=True)


class ColumnGather:
    def __init__(self, shard, first):
        width = shard.shape[1] // 8
        self.first = first
        self.piece = lax.dynamic_slice_in_dim(shard, place(first, 0) * width, width, 1)

    def blocks(self, earlier, late):
        self.held = gather_blocks(after(self.piece, *earlier), late)
        return self.held

    def second(self, *earlier):
        held = after(self.held, *earlier) if earlier else self.held
        self.held = jnp.concatenate([held, swap(held, other(self.first))], axis=1)
        return self.held

    def third(self, *earlier):
        held = after(self.held, *earlier) if earlier else self.held
        self.held = jnp.concatenate([held, swap(held, self.first)], axis=1)
        return self.held

    def full(self):
        return self.held, swap(self.held, "core")


def dot_columns(values, halves_of):
    parts = [jnp.dot(values, w, preferred_element_type=F32) for w in halves_of]
    return jnp.concatenate(parts, axis=1)


def dot_back(grads, halves_of):
    half = grads.shape[1] // 2
    return jnp.einsum(
        "tf,df->td", grads[:, :half], halves_of[0], preferred_element_type=F32
    ) + jnp.einsum("tf,df->td", grads[:, half:], halves_of[1], preferred_element_type=F32)


def grad_dot(left, right):
    return jnp.einsum("td,tf->df", left, right, preferred_element_type=F32)


class ColumnSum:
    def __init__(self, left, right, first):
        self.left, self.right, self.first = left, right, first
        self.width = right.shape[1] // 8
        self.from_core = swap(grad_dot(left, right[:, 4 * self.width :]).astype(BF16), "core")

    def second(self):
        width = self.width
        outgoing = grad_dot(self.left, self.right[:, 2 * width : 4 * width])
        self.outgoing = (outgoing + self.from_core[:, 2 * width :].astype(F32)).astype(BF16)
        self.from_first = swap(self.outgoing, self.first)
        return self.outgoing

    def third(self, *late):
        width = self.width
        self.from_first = after(self.from_first, *late)
        self.outgoing = (
            grad_dot(self.left, self.right[:, width : 2 * width])
            + self.from_core[:, width : 2 * width].astype(F32)
            + self.from_first[:, width:].astype(F32)
        ).astype(BF16)
        self.from_second = swap(self.outgoing, other(self.first))
        return self.outgoing

    def own(self):
        width = self.width
        return (
            grad_dot(self.left, self.right[:, :width])
            + self.from_core[:, :width].astype(F32)
            + self.from_first[:, :width].astype(F32)
            + self.from_second.astype(F32)
        )


def spread(blocks):
    held = jnp.concatenate(blocks, axis=0)[None]
    for axis in ("sp", "x"):
        held = jnp.concatenate([held, swap(held, axis)], axis=0)
    return held, swap(held, "core")


def spread_aside(blocks):
    every = lax.all_gather(jnp.concatenate(blocks, axis=0), ("x", "core", "sp"), axis=0)
    return every[:4], every[4:]


def unpack_kernel(segments, count, places_ref, *refs):
    sources, outs = refs[:count], refs[count:]
    for source, row, out, column, rows, blocks, way in segments:
        for k in range(8):
            piece = sources[2 * source + k // 4]
            at = pl.multiple_of(column + places_ref[2 * way, k] * (128 * blocks), 128)
            down = pl.multiple_of(places_ref[2 * way + 1, k] * rows, 16)
            for j in range(blocks):
                outs[out][pl.ds(down, rows), pl.ds(at + 128 * j, 128)] = piece[
                    k % 4, row + j * rows : row + (j + 1) * rows
                ].astype(F32)


def unpack(places, segments, sources, shapes):
    count = len(sources)
    return pl.pallas_call(
        functools.partial(unpack_kernel, segments, count),
        out_shape=[jax.ShapeDtypeStruct(s, F32) for s in shapes],
        in_specs=[pl.BlockSpec(memory_space=pltpu.SMEM)]
        + [pl.BlockSpec(memory_space=pltpu.VMEM)] * count,
        out_specs=[pl.BlockSpec(memory_space=pltpu.VMEM)] * len(shapes),
        compiler_params=pltpu.CompilerParams(vmem_limit_bytes=VMEM_BYTES),
    )(places, *sources)


def spread_places():
    core, x, y = lax.axis_index("core"), lax.axis_index("x"), lax.axis_index("sp")
    table = [[] for _ in range(12)]
    for k in range(8):
        c, d, e = (
            1 - bit if (k >> shift) & 1 else bit for shift, bit in ((2, core), (1, x), (0, y))
        )
        for line, value in enumerate((4 * c + 2 * d + e, 0, 4 * c + 2 * e + d, 0, 2 * c + d, e)):
            table[line].append(jnp.asarray(value, jnp.int32))
        d, c, e = (k >> 2) & 1, (k >> 1) & 1, k & 1
        for line, value in enumerate((4 * c + 2 * d + e, 0, 4 * c + 2 * e + d, 0, 2 * c + d, e)):
            table[6 + line].append(jnp.asarray(value, jnp.int32))
    return jnp.stack([jnp.stack(line) for line in table])


def by_half(values):
    blocks = values.reshape(values.shape[0], lax.axis_size("fsdp"), 2, -1)
    low = blocks[:, :, 0].reshape(values.shape[0], -1)
    high = blocks[:, :, 1].reshape(values.shape[0], -1)
    first = lax.axis_index("sp") == 0
    return jnp.concatenate(
        [jnp.where(first, low, high), jnp.where(first, high, low)], axis=1
    )


class HalfSum:
    def __init__(self, left, right):
        self.left, self.first = left, "x"
        self.width = width = right.shape[1] // 4
        core, x = lax.axis_index("core"), lax.axis_index("x")

        def half(c):
            return jnp.concatenate(
                [
                    lax.dynamic_slice_in_dim(right, (2 * c + d) * width, width, 1)
                    for d in (x, 1 - x)
                ],
                axis=1,
            )

        self.near, far_core = half(core), half(1 - core)
        self.rows = left.shape[1] // 2
        self.from_core = swap(grad_dot(left, far_core).astype(BF16), "core")

    def second(self):
        width = self.width
        outgoing = grad_dot(self.left, self.near[:, width:])
        self.outgoing = (outgoing + self.from_core[:, width:].astype(F32)).astype(BF16)
        self.from_x = swap(self.outgoing, "x")
        return self.outgoing

    def third(self):
        rows, width = self.rows, self.width
        self.outgoing = (
            grad_dot(self.left[:, rows:], self.near[:, :width])
            + self.from_core[rows:, :width].astype(F32)
            + self.from_x[rows:].astype(F32)
        ).astype(BF16)
        self.from_y = swap(self.outgoing, "sp")
        return self.outgoing

    def own(self):
        rows, width = self.rows, self.width
        return (
            grad_dot(self.left[:, :rows], self.near[:, :width])
            + self.from_core[:rows, :width].astype(F32)
            + self.from_x[:rows].astype(F32)
            + self.from_y.astype(F32)
        )


def narrow(value):
    return jnp.concatenate(
        [value[:, i : i + 128] for i in range(0, value.shape[1], 128)], axis=0
    )


def by_member(value):
    blocks = value.reshape(lax.axis_size("fsdp"), -1, value.shape[1])
    return jnp.concatenate(
        [blocks[:, :, i : i + 128] for i in range(0, value.shape[1], 128)], axis=1
    )


def pack_small(parts, width):
    flat = jnp.concatenate([p.reshape(-1) for p in parts])
    return jnp.pad(flat, (0, -flat.shape[0] % (16 * width))).reshape(-1, width)


def unpack_small(every, parts):
    out, start = [], 0
    for p in parts:
        out.append(every[:, start : start + p.size].reshape((-1,) + p.shape))
        start += p.size
    return out


def sum_small(parts, *earlier):
    flat = jnp.concatenate([p.reshape(-1) for p in parts])
    size = flat.shape[0]
    flat = after(jnp.pad(flat, (0, -size % 1024)).reshape(-1, 128), *earlier)
    for axis in ("core", "x", "sp"):
        flat = flat + swap(flat, axis)
    members = lax.axis_size("fsdp")
    for bit in range(members.bit_length() - 1):
        flat = flat + lax.ppermute(flat, "fsdp", [(i, i ^ (1 << bit)) for i in range(members)])
    if lax.axis_size("hi") > 1:
        flat = lax.psum(flat, "hi")
    total = flat.reshape(-1)
    out, start = [], 0
    for p in parts:
        out.append(total[start : start + p.size].reshape(p.shape))
        start += p.size
    return out


def own_part(value, axis):
    size = value.shape[axis] // lax.axis_size("fsdp")
    return lax.dynamic_slice_in_dim(value, lax.axis_index("fsdp") * size, size, axis)


def body(
    tokens,
    cotangent,
    doc_lengths,
    input_weight,
    rate_weight,
    conv_weight,
    head_decay,
    mixer_gain,
    heads_gain,
    output_weight,
    feed_gain,
    up_weight,
    down_weight,
):
    length = tokens.shape[0]
    sp_size = lax.axis_size("sp")
    member = lax.axis_index("sp")
    qkv_cols = H * (2 * DK + DV)
    qk_cols = 2 * H * DK
    members = lax.axis_size("fsdp")
    qk_way = ColumnGather(input_weight[:, :qk_cols], "x")
    v_way = ColumnGather(input_weight[:, qk_cols:qkv_cols], "sp")
    gate_way = ColumnGather(input_weight[:, qkv_cols:], "x")
    down_way = ColumnGather(down_weight, "x")
    pair_rows, pair_cols = qk_way.piece.shape[0], 2 * qk_way.piece.shape[1]
    smalls = (rate_weight, conv_weight, head_decay, mixer_gain, heads_gain, feed_gain)
    first_load = jnp.concatenate(
        [
            jnp.concatenate([qk_way.piece, v_way.piece], axis=1),
            pack_small(smalls, pair_cols),
        ],
        axis=0,
    )
    first_all = gather_blocks(first_load).reshape(members, -1, pair_cols)
    both = first_all[:, :pair_rows].reshape(-1, pair_cols)
    qk_way.held, v_way.held = both[:, : pair_cols // 2], both[:, pair_cols // 2 :]
    rate_all, conv_all, decay_all, mixer_all, heads_all, feed_all = unpack_small(
        first_all[:, pair_rows:].reshape(members, -1), smalls
    )
    qkv_second = (qk_way.second(), v_way.second())
    qkv_third = (qk_way.third(*qkv_second), v_way.third(*qkv_second))
    qk_full, v_full = qk_way.full(), v_way.full()
    out_full = gather_rows(output_weight)
    up_full = gather_rows(up_weight)
    rate_full = jnp.swapaxes(rate_all.reshape(-1, H, 2), 1, 2).reshape(-1, 2 * H)
    conv_full = jnp.swapaxes(conv_all, 0, 1).reshape(CONV, -1).astype(F32)
    decay_full = jnp.swapaxes(decay_all, 0, 1).reshape(2, H).astype(F32)
    mixer_scale = mixer_all.reshape(-1).astype(F32)
    heads_scale = heads_all.reshape(-1).astype(F32)
    feed_scale = feed_all.reshape(-1).astype(F32)

    def points(name, value):
        if name == "conv":
            gate_way.blocks(qkv_third, value)
            gate_way.second()
            ready.append(value)
            return value
        if name == "inverse":
            down_way.blocks(ready, value)
            value = after(value, gate_way.held, down_way.held)
            gate_way.third(value)
            down_way.second(value)
            return value
        if name == "state":
            value = after(value, gate_way.held, down_way.held)
            down_way.third(value)
            return value
        if name == "sent":
            for key in ("down", "out", "gate"):
                sums[key].third(value)
            return value
        if name == "back":
            return after(value, sums["down"].outgoing)
        if name == "conv_back":
            for key in ("out", "gate"):
                sums[key].from_second = after(sums[key].from_second, value)
            packed = jnp.concatenate(
                [by_member(sums[key].own().astype(BF16)) for key in ("down", "out", "gate")],
                axis=1,
            )
            owns.append(packed.reshape(-1, 128))
            return after(value, owns[0])
        if name == "conv_back_done":
            return after(value, sums["up"].third())
        return value

    sums, ready, owns = {}, [], []

    ends = jnp.cumsum(doc_lengths[0])
    positions = lax.broadcasted_iota(jnp.int32, (length * sp_size, 1), 0)
    doc_ids = jnp.sum((positions >= ends[None, :]).astype(jnp.int32), axis=1)

    ahead = [(i, i + 1) for i in range(sp_size - 1)]
    halo = lax.ppermute(tokens[-HALO:], "sp", ahead)
    x_float = tokens.astype(F32)
    normed, pull_norm = jax.vjp(rms_norm, x_float, mixer_scale)
    normed_low = normed.astype(BF16)
    halo_low = rms_norm(halo.astype(F32), mixer_scale).astype(BF16)
    normed_more = jnp.concatenate([halo_low, normed_low], axis=0)
    qkv = jnp.concatenate(
        [
            reorder(dot_columns(normed_more, qk_full).astype(BF16), "x"),
            reorder(dot_columns(normed_more, v_full).astype(BF16), "sp"),
        ],
        axis=1,
    )
    rate_raw = jnp.dot(normed_low, rate_full, preferred_element_type=F32)
    rates = rate_raw.astype(BF16).astype(F32)
    mixed, pull_mix = mixer(qkv, conv_full, rates, decay_full, doc_ids, member, sp_size, points)
    gate_full, down_full = gate_way.full(), down_way.full()
    gate_raw = reorder(dot_columns(normed_low, gate_full), "x")
    gated, pull_gate = jax.vjp(output_gate, mixed.astype(F32), gate_raw, heads_scale)
    gated_low = gated.astype(BF16)
    attended = jnp.dot(gated_low, out_full, preferred_element_type=F32)
    (hidden, normed_two), pull_resid = jax.vjp(residual_norm, x_float, attended, feed_scale)
    two_low = normed_two.astype(BF16)
    gate_up = jnp.dot(two_low, up_full, preferred_element_type=F32)

    def feed_act(gate_up):
        half = gate_up.shape[1] // 2
        return jax.nn.silu(gate_up[:, :half]) * gate_up[:, half:]

    activated, pull_act = jax.vjp(feed_act, gate_up)
    act_low = activated.astype(BF16)
    block_out = (hidden + reorder(dot_columns(act_low, down_full), "x")).astype(BF16)
    cot_rel = reorder(cotangent, "x")
    sums["down"] = ColumnSum(act_low, cot_rel, "x")
    d_act = dot_back(cot_rel, down_full)
    d_gu_low = pull_act(d_act)[0].astype(BF16)
    sums["up"] = HalfSum(by_half(two_low), d_gu_low)
    d_gu_low = after(d_gu_low, sums["down"].second())
    d_two = jnp.einsum("tf,df->td", d_gu_low, up_full, preferred_element_type=F32)
    d_resid, d_attended, feed_grad = pull_resid((cotangent.astype(F32), d_two))
    d_att_low = d_attended.astype(BF16)
    d_att_rel = reorder(d_att_low, "sp")
    sums["out"] = ColumnSum(gated_low, d_att_rel, "sp")
    d_gated = jnp.einsum("td,ed->te", d_att_low, out_full, preferred_element_type=F32)
    d_mixed, d_gate, heads_grad = pull_gate(d_gated)
    d_gate_low = d_gate.astype(BF16)
    d_gate_rel = reorder(d_gate_low, "x")
    sums["gate"] = ColumnSum(normed_low, d_gate_rel, "x")
    d_mixed_low = after(
        d_mixed.astype(BF16), *(sums[key].second() for key in ("up", "out", "gate"))
    )
    d_more, from_next, conv_grad, d_rates, decay_grad = pull_mix(d_mixed_low)
    edge = jnp.pad(from_next.astype(F32), ((length - HALO, 0), (0, 0)))
    d_qkv = (d_more[HALO:].astype(F32) + edge).astype(BF16)
    d_rate_low = d_rates.astype(BF16)
    d_qk_rel = reorder(d_qkv[:, :qk_cols], "x")
    d_v_rel = reorder(d_qkv[:, qk_cols:], "sp")
    sums["qk"] = ColumnSum(normed_low, d_qk_rel, "x")
    sums["v"] = ColumnSum(normed_low, d_v_rel, "sp")
    places = spread_places()
    early_block = sum_blocks(owns[0])
    early_sums = spread_aside([early_block])
    for key in ("qk", "v"):
        sums[key].from_core = after(sums[key].from_core, early_block)
        sums[key].second()
    up_own = sums["up"].own().astype(BF16)
    d_normed = dot_back(d_qk_rel, qk_full) + dot_back(d_v_rel, v_full)
    d_normed = d_normed + dot_back(d_gate_rel, gate_full)
    d_normed = d_normed + jnp.einsum(
        "tf,df->td", d_rate_low, rate_full, preferred_element_type=F32
    )
    for key in ("qk", "v"):
        sums[key].third()
        sums[key].from_second = after(
            sums[key].from_second, d_normed, up_own, early_sums[0]
        )
    down_rows, out_rows = down_weight.shape[0], output_weight.shape[0]
    down_shard, output_shard = unpack(
        places,
        [(0, 0, 0, 0, down_rows, 1, 3), (0, down_rows, 1, 0, out_rows, 1, 4)],
        early_sums,
        [down_weight.shape, output_weight.shape],
    )
    up_block = sum_blocks(up_own)
    (up_shard,) = unpack(
        places,
        [(0, 0, 0, 0, up_block.shape[0], up_block.shape[1] // 128, 5)],
        spread_aside([narrow(up_block)]),
        [up_weight.shape],
    )
    late_block = sum_blocks(jnp.concatenate([sums["qk"].own(), sums["v"].own()], axis=1))
    rows, wide = late_block.shape[0], late_block.shape[1] // 256
    gate_wide = H * DV // 8 // 128
    (input_shard,) = unpack(
        places,
        [
            (0, 0, 0, 0, rows, wide, 0),
            (0, wide * rows, 0, qk_cols, rows, wide, 1),
            (1, down_rows + out_rows, 0, qkv_cols, rows, gate_wide, 3),
        ],
        spread([narrow(late_block)]) + early_sums,
        [input_weight.shape],
    )
    rate_grad = jnp.einsum("td,tf->df", normed_low, d_rate_low, preferred_element_type=F32)
    d_front, mixer_grad = pull_norm(d_normed)
    tokens_grad = (d_resid + d_front).astype(BF16)
    rate_sum, conv_sum, decay_sum, mixer_sum, heads_sum, feed_sum = sum_small(
        (rate_grad, conv_grad, decay_grad, mixer_grad, heads_grad, feed_grad),
        sums["qk"].outgoing,
        sums["v"].outgoing,
    )
    return (
        block_out,
        tokens_grad,
        input_shard,
        own_part(jnp.swapaxes(rate_sum.reshape(-1, 2, H), 1, 2).reshape(-1, 2 * H), 0),
        own_part(conv_sum, 1),
        own_part(decay_sum, 1),
        own_part(mixer_sum, 0),
        own_part(heads_sum, 0),
        output_shard,
        own_part(feed_sum, 0),
        up_shard,
        down_shard,
    )


def solution(mesh):
    dp, fsdp, sp = (mesh.shape[axis] for axis in ("dp", "fsdp", "sp"))
    dp_axes = ("hi", "x", "core")
    cut = jax.sharding.Mesh(
        mesh.devices.reshape(dp // 4, 2, 2, fsdp, sp), dp_axes + ("fsdp", "sp")
    )
    rows = P(dp_axes + ("fsdp", "sp"), None)
    split = P("fsdp", None)
    return jax.shard_map(
        body,
        mesh=cut,
        in_specs=(
            rows,
            rows,
            P(dp_axes + ("fsdp",), None),
            split,
            split,
            P(None, "fsdp"),
            P(None, "fsdp"),
            P("fsdp"),
            P("fsdp"),
            split,
            P("fsdp"),
            split,
            split,
        ),
        out_specs=(
            rows,
            rows,
            split,
            split,
            P(None, "fsdp"),
            P(None, "fsdp"),
            P("fsdp"),
            P("fsdp"),
            split,
            P("fsdp"),
            split,
            split,
        ),
        check_vma=False,
    )
```
